32 devices in a mesh: img: 4 (over z), ctx: 2 (over core), tp: 4 (over y, x).
Axes of the slice: x: 2, y: 2, z: 4, core: 2. Of those that a mesh axis runs over, the one named last changes fastest.
Arguments:
- tokens: bfloat16 [8, 24, 24, 768], P('img', 'ctx'), may hold values from -6 to 6
- cotangent: bfloat16 [8, 24, 24, 768], P('img', 'ctx'), may hold values from -6 to 6
- adapter_id: int32 [8], P('img'), may hold values from 0 to 7
- valid_flag: int32 [8], P('img'), may hold values 0 or 1
- regions: int32 [24, 24], P('ctx'), may hold values from 0 to 2
- w_qkv: bfloat16 [768, 3, 768], P('img', None, 'tp'), may hold values from -0.21875 to 0.21875
- b_qkv: bfloat16 [3, 768], P(None, 'tp'), may hold values from -2 to 2
- rel_table: bfloat16 [529, 24], P(None, 'tp'), may hold values from -4 to 4
- w_proj: bfloat16 [768, 768], P('tp', 'img'), may hold values from -0.625 to 0.625
- b_proj: bfloat16 [768], replicated, may hold values from -2 to 2
- w_fc1: bfloat16 [768, 3072], P('img', 'tp'), may hold values from -0.21875 to 0.21875
- b_fc1: bfloat16 [3072], P('tp'), may hold values from -2 to 2
- w_fc2: bfloat16 [3072, 768], P('tp', 'img'), may hold values from -0.109375 to 0.109375
- b_fc2: bfloat16 [768], replicated, may hold values from -2 to 2
- norm_gains: bfloat16 [2, 768], replicated, may hold values from 0.5 to 1.5
- norm_shifts: bfloat16 [2, 768], replicated, may hold values from -2 to 2
- down_main: bfloat16 [8, 3, 12288], P(None, None, ('img', 'ctx')), may hold values from -0.21875 to 0.21875
- down_fc2: bfloat16 [8, 49152], P(None, ('img', 'ctx')), may hold values from -0.109375 to 0.109375
- up_qkv: bfloat16 [8, 36864], P(None, ('img', 'ctx')), may hold values from -1.5 to 1.5
- up_fc1: bfloat16 [8, 49152], P(None, ('img', 'ctx')), may hold values from -1.5 to 1.5
- up_out: bfloat16 [8, 2, 12288], P(None, None, ('img', 'ctx')), may hold values from -1.5 to 1.5
Outputs:
- output: bfloat16 [8, 24, 24, 768], P('img', 'ctx')
- grad_tokens: float32 [8, 24, 24, 768], P('img', 'ctx')
- grad_down_main: float32 [8, 3, 12288], P(None, None, ('img', 'ctx', 'tp'))
- grad_down_fc2: float32 [8, 49152], P(None, ('img', 'ctx', 'tp'))
- grad_up_qkv: float32 [8, 36864], P(None, ('img', 'ctx', 'tp'))
- grad_up_fc1: float32 [8, 49152], P(None, ('img', 'ctx', 'tp'))
- grad_up_out: float32 [8, 2, 12288], P(None, None, ('img', 'ctx', 'tp'))
The draws below stay inside these ranges and needn't reach their ends.
All inputs are finite; a program needn't handle non-finite values. No bound on the sum of `valid_flag` on one device may be relied on, other than what follows from the above.
Results may differ from the reference program's by a relative error of at most 0.014.
The reference program's roundings to bfloat16 on the way count: a program that leaves them out, or rounds other values in their place, can miss the bound.
Values may be sent and summed in bfloat16 or wider, within the bound.
No kernel may reach another device: no remote copies, remote signals or barrier semaphores. Data moves between devices by JAX's collectives and lax.ppermute only.
A program may use at most 256 MiB of HBM per device.

```python
import jax
import jax.numpy as jnp
from jax import lax

C = 768
HEADS = 24
HD = 32
FF = 3072
WIN = 12
SHIFT = 6
SIDE = 24
RANK = 16
ADAPT = 8
IMGS = 8
RELS = 529


def set_ends(values, own_key, smallest, largest):
    longest = values.shape.index(max(values.shape))
    spots = []
    for shift in (0, 1):
        where = [jax.random.randint(jax.random.fold_in(own_key, axis), (), 0, length) for axis, length in enumerate(values.shape)]
        where[longest] = (where[longest] + shift) % values.shape[longest]
        spots.append(tuple(where))
    return values.at[spots[0]].set(smallest).at[spots[1]].set(largest)


def shard_levels(key, extent, shards, smallest, largest):
    def one(axis_at, blocks):
        steps = jax.random.uniform(jax.random.fold_in(jax.random.fold_in(key, 6), axis_at), (blocks,), jnp.float32, smallest / len(shards), largest / len(shards))
        return jnp.repeat(jnp.exp(steps), extent[axis_at] // blocks).reshape((-1,) + (1,) * (len(extent) - axis_at - 1))

    factor_of = one(*shards[0])
    for cut in shards[1:]:
        factor_of = factor_of * one(*cut)
    return factor_of


def gaussian(rng, dims, spread, most, pieces=(), dtype=jnp.bfloat16):
    loudness = shard_levels(rng, dims, pieces, -0.22, 0.18) if pieces else 1.0
    values = jax.random.normal(rng, dims, jnp.float32) * spread * loudness
    return jnp.minimum(jnp.maximum(values, -most), most).astype(dtype)


def setup_inputs(seed: int = 0) -> dict:
    keys = jax.random.split(jax.random.key(seed), 22)
    tokens = gaussian(keys[0], (IMGS, SIDE, SIDE, C), 1.0, 6.0, ((0, 4), (1, 2)))
    cotangent = gaussian(keys[1], (IMGS, SIDE, SIDE, C), 1.0, 6.0, ((0, 4), (1, 2)))
    adapter_id = set_ends(jax.random.randint(keys[2], (IMGS,), 0, ADAPT), jax.random.fold_in(keys[2], 1), 0, ADAPT - 1).astype(jnp.int32)
    valid_flag = set_ends((jax.random.randint(keys[3], (IMGS,), 0, 8) < 7).astype(jnp.int32), jax.random.fold_in(keys[3], 1), 0, 1)
    regions = set_ends(jax.random.randint(keys[4], (SIDE, SIDE), 0, 3), jax.random.fold_in(keys[4], 1), 0, 2).astype(jnp.int32)
    w_qkv = gaussian(keys[5], (C, 3, C), C ** -0.5, 0.21875, ((0, 4), (2, 4)))
    b_qkv = gaussian(keys[6], (3, C), 0.3, 2.0, ((1, 4),))
    rel_table = gaussian(keys[7], (RELS, HEADS), 1.0, 4.0, ((1, 4),))
    w_proj = gaussian(keys[8], (C, C), (C // 8) ** -0.5, 0.625, ((0, 4), (1, 4)))
    b_proj = gaussian(keys[9], (C,), 0.3, 2.0)
    w_fc1 = gaussian(keys[10], (C, FF), C ** -0.5, 0.21875, ((0, 4), (1, 4)))
    b_fc1 = gaussian(keys[11], (FF,), 0.3, 2.0, ((0, 4),))
    w_fc2 = gaussian(keys[12], (FF, C), FF ** -0.5, 0.109375, ((0, 4), (1, 4)))
    b_fc2 = gaussian(keys[13], (C,), 0.3, 2.0)
    norm_gains = jnp.clip(1.0 + 0.1 * jax.random.normal(keys[14], (2, C), jnp.float32), 0.5, 1.5).astype(jnp.bfloat16)
    norm_shifts = gaussian(keys[15], (2, C), 0.3, 2.0)
    down_main = gaussian(keys[16], (ADAPT, 3, C * RANK), C ** -0.5, 0.21875, ((2, 8),))
    down_fc2 = gaussian(keys[17], (ADAPT, FF * RANK), FF ** -0.5, 0.109375, ((1, 8),))
    up_qkv = gaussian(keys[18], (ADAPT, RANK * 3 * C), RANK ** -0.5, 1.5, ((1, 8),))
    up_fc1 = gaussian(keys[19], (ADAPT, RANK * FF), RANK ** -0.5, 1.5, ((1, 8),))
    up_out = gaussian(keys[20], (ADAPT, 2, RANK * C), RANK ** -0.5, 1.5, ((2, 8),))
    return dict(tokens=tokens, cotangent=cotangent, adapter_id=adapter_id, valid_flag=valid_flag, regions=regions, w_qkv=w_qkv, b_qkv=b_qkv, rel_table=rel_table, w_proj=w_proj, b_proj=b_proj, w_fc1=w_fc1, b_fc1=b_fc1, w_fc2=w_fc2, b_fc2=b_fc2, norm_gains=norm_gains, norm_shifts=norm_shifts, down_main=down_main, down_fc2=down_fc2, up_qkv=up_qkv, up_fc1=up_fc1, up_out=up_out)


@jax.custom_vjp
def low(v):
    return lax.optimization_barrier(v.astype(jnp.bfloat16)).astype(jnp.float32)

@jax.custom_vjp
def low_back(v):
    return v

def low_keep(v):
    return (low(v), None)

def low_pass(kept, grad):
    return (grad,)

def back_keep(v):
    return (v, None)

def back_low(kept, grad):
    return (low(grad),)
low.defvjp(low_keep, low_pass)
low_back.defvjp(back_keep, back_low)
epsilon = 1e-05
highest = lax.Precision.HIGHEST

def rounded(field):
    return low_back(low(field))

def contract(pattern, left, right):
    return jnp.einsum(pattern, left, right, precision=highest)

def layer_norm(field, gain, offset):
    average = lax.optimization_barrier(jnp.mean(field, -1, keepdims=True))
    centred = field - average
    variance = lax.optimization_barrier(jnp.mean(centred * centred, -1, keepdims=True))
    return centred * lax.rsqrt(variance + epsilon) * gain + offset

def activate(field):
    return jax.nn.gelu(field, approximate=False)

def relative_index():
    offsets_win = jnp.arange(WIN)
    row_diff = offsets_win[:, None, None, None] - offsets_win[None, None, :, None]
    col_diff = offsets_win[None, :, None, None] - offsets_win[None, None, None, :]
    return ((row_diff + WIN - 1) * (2 * WIN - 1) + col_diff + WIN - 1).reshape(WIN * WIN, WIN * WIN)

def windows(field):
    grid = SIDE // WIN
    depth = field.shape[-1]
    field = field.reshape(grid, WIN, grid, WIN, depth)
    return jnp.transpose(field, (0, 2, 1, 3, 4)).reshape(grid * grid, WIN * WIN, depth)

def unwindows(field):
    grid = SIDE // WIN
    depth = field.shape[-1]
    field = field.reshape(grid, grid, WIN, WIN, depth)
    return jnp.transpose(field, (0, 2, 1, 3, 4)).reshape(SIDE, SIDE, depth)

def reference(tokens, cotangent, adapter_id, valid_flag, regions, w_qkv, b_qkv, rel_table, w_proj, b_proj, w_fc1, b_fc1, w_fc2, b_fc2, norm_gains, norm_shifts, down_main, down_fc2, up_qkv, up_fc1, up_out):
    gains = norm_gains.astype(jnp.float32)
    offsets = norm_shifts.astype(jnp.float32)
    weight_qkv = w_qkv.astype(jnp.float32)
    bias_qkv = b_qkv.astype(jnp.float32)
    weight_proj = w_proj.astype(jnp.float32)
    bias_proj = b_proj.astype(jnp.float32)
    weight_fc1 = w_fc1.astype(jnp.float32)
    bias_fc1 = b_fc1.astype(jnp.float32)
    weight_fc2 = w_fc2.astype(jnp.float32)
    bias_fc2 = b_fc2.astype(jnp.float32)
    rel_bias = jnp.transpose(rel_table.astype(jnp.float32)[relative_index()], (2, 0, 1))
    region_win = windows(regions[:, :, None])[:, :, 0]
    region_mask = jnp.where(region_win[:, :, None] == region_win[:, None, :], 0.0, -100.0).astype(jnp.float32)
    additive = rel_bias[None] + region_mask[:, None]
    score_scale = HD ** (-0.5)
    adapters = tuple((table.astype(jnp.float32) for table in (down_main, down_fc2, up_qkv, up_fc1, up_out)))

    def block_forward(inputs, chosen, validity):
        main_down = chosen[0].reshape(3, C, RANK)
        fc2_down = chosen[1].reshape(FF, RANK)
        qkv_up = chosen[2].reshape(RANK, 3, C)
        fc1_up = chosen[3].reshape(RANK, FF)
        out_up = chosen[4].reshape(2, RANK, C)
        normed = low(layer_norm(inputs, gains[0], offsets[0]))
        shifted = jnp.roll(normed, (-SHIFT, -SHIFT), (0, 1))
        low_qkv = rounded(contract('ijc,cn->ijn', shifted, main_down[0]))
        mixed = contract('ijc,ctd->ijtd', shifted, weight_qkv) + bias_qkv + contract('ijn,ntd->ijtd', low_qkv, qkv_up)
        queries = windows(rounded(mixed[:, :, 0])).reshape(-1, WIN * WIN, HEADS, HD)
        keys_win = windows(rounded(mixed[:, :, 1])).reshape(-1, WIN * WIN, HEADS, HD)
        values_win = windows(rounded(mixed[:, :, 2])).reshape(-1, WIN * WIN, HEADS, HD)
        scores = low_back(score_scale * contract('wqhd,wkhd->whqk', queries, keys_win) + additive)
        probs_win = jax.nn.softmax(scores, axis=-1)
        attended = rounded(contract('whqk,wkhd->wqhd', low(probs_win), values_win))
        heads_out = jnp.roll(unwindows(attended.reshape(-1, WIN * WIN, C)), (SHIFT, SHIFT), (0, 1))
        low_proj = rounded(contract('ijc,cn->ijn', heads_out, main_down[1]))
        attention = low_back(contract('ijc,cd->ijd', heads_out, weight_proj) + bias_proj + contract('ijn,nd->ijd', low_proj, out_up[0]))
        residual = inputs + validity * attention
        normed2 = low(layer_norm(residual, gains[1], offsets[1]))
        low_fc1 = rounded(contract('ijc,cn->ijn', normed2, main_down[2]))
        preact = low_back(contract('ijc,cf->ijf', normed2, weight_fc1) + bias_fc1 + contract('ijn,nf->ijf', low_fc1, fc1_up))
        hidden = low(activate(preact))
        low_fc2 = rounded(contract('ijf,fn->ijn', hidden, fc2_down))
        branch = contract('ijf,fd->ijd', hidden, weight_fc2) + bias_fc2 + contract('ijn,nd->ijd', low_fc2, out_up[1])
        return residual + validity * branch

    def per_image(totals, inputs_one):
        image, grad_image_out, adapter_one, flag_one = inputs_one
        validity = flag_one.astype(jnp.float32)

        def forward(field, tables):
            chosen = tuple((table[adapter_one] for table in tables))
            return block_forward(field, chosen, validity)
        result, pullback = jax.vjp(forward, image.astype(jnp.float32), adapters)
        grad_image, grad_tables = pullback(grad_image_out.astype(jnp.float32))
        totals = tuple((total + piece for total, piece in zip(totals, grad_tables)))
        return (totals, (result.astype(jnp.bfloat16), grad_image))
    zero_grads = tuple((jnp.zeros(table.shape, jnp.float32) for table in adapters))
    grads_all, (output, grad_tokens) = lax.scan(per_image, zero_grads, (tokens, cotangent, adapter_id, valid_flag))
    return (output, grad_tokens, grads_all[0], grads_all[1], grads_all[2], grads_all[3], grads_all[4])
```

```python
import jax
import jax.numpy as jnp
from jax import lax
from jax.sharding import PartitionSpec as P

C = 768
HD = 32
FF = 3072
WIN = 12
SHIFT = 6
RANK = 16
ADAPT = 8
RELS = 529
TOK = WIN * WIN
SCALE = HD ** (-0.5)
EPS = 1e-05

bf16 = jnp.bfloat16
f32 = jnp.float32


def dot(left, right):
    return jnp.dot(left, right, preferred_element_type=f32)


def dot_t(left, right):
    return lax.dot_general(left, right, (((1,), (1,)), ((), ())), preferred_element_type=f32)


def tdot(left, right):
    return lax.dot_general(left, right, (((0,), (0,)), ((), ())), preferred_element_type=f32)


def swap_ctx(v):
    return lax.ppermute(v, "ctx", [(0, 1), (1, 0)])


def swap_x(v):
    return lax.ppermute(v, "tp", [(0, 1), (1, 0), (2, 3), (3, 2)])


def swap_y(v):
    return lax.ppermute(v, "tp", [(0, 2), (2, 0), (1, 3), (3, 1)])


def ring(v):
    count = lax.axis_size("img")
    if count > 8:
        whole = lax.all_gather(v, "img", axis=0)
        here = lax.axis_index("img")
        return [lax.dynamic_index_in_dim(whole, (here - k) % count, 0, False) for k in range(count)]
    held = [v]
    for _ in range(count - 1):
        held.append(lax.ppermute(held[-1], "img", [(i, (i + 1) % count) for i in range(count)]))
    return held


def spread_first(v):
    held = ring(v)
    half = len(held) // 2
    by_x = [swap_x(a) for a in held]
    by_y = [swap_y(a) for a in held]
    by_xy = [swap_y(a) for a in by_x[:half]] + [swap_x(a) for a in by_y[half:]]
    out = {}
    for k in range(len(held)):
        out[k, 0], out[k, 1], out[k, 2], out[k, 3] = held[k], by_x[k], by_y[k], by_xy[k]
    return out


def spread_last(v, first, second, one, two):
    held = ring(jnp.stack([v, first(v)]))
    out = {}
    for k, pair in enumerate(held):
        other = second(pair)
        out[k, 0], out[k, one] = pair[0], pair[1]
        out[k, two], out[k, one + two] = other[0], other[1]
    return out


def assemble(pieces, z, c, t):
    count = lax.axis_size("img")
    rows, cols = pieces[0, 0].shape
    whole = jnp.zeros((count * 2 * rows, 4 * cols), bf16)
    for (k, j), piece in pieces.items():
        other = swap_ctx(piece)
        top = ((z - k) % count) * 2 * rows
        left = (t ^ j) * cols
        whole = lax.dynamic_update_slice(whole, piece, (top + c * rows, left))
        whole = lax.dynamic_update_slice(whole, other, (top + (1 - c) * rows, left))
    return whole


def norm_parts(field):
    average = jnp.mean(field, -1, keepdims=True)
    centred = field - average
    variance = jnp.mean(centred * centred, -1, keepdims=True)
    scale = lax.rsqrt(variance + EPS)
    return centred * scale, scale


def norm_back(grad, gain, unit, scale):
    scaled = grad * gain
    return scale * (
        scaled
        - jnp.mean(scaled, -1, keepdims=True)
        - unit * jnp.mean(scaled * unit, -1, keepdims=True)
    )


def bias_of(table):
    heads = table.shape[0]
    span = 2 * WIN - 1
    q_col = jnp.arange(WIN)[:, None, None]
    step = jnp.arange(span)[None, :, None]
    k_col = jnp.arange(WIN)[None, None, :]
    index = ((span - 1 - step) * span + q_col - k_col + WIN - 1).reshape(-1)
    chosen = (jnp.arange(RELS)[:, None] == index[None, :]).astype(bf16)
    strips = dot(table, chosen).reshape(heads, WIN, span * WIN)
    rows = [strips[:, :, (WIN - 1 - r) * WIN :][:, :, :TOK] for r in range(WIN)]
    return jnp.stack(rows, 1).reshape(heads, TOK, TOK)


def per_device(
    tokens,
    cotangent,
    adapter_id,
    valid_flag,
    regions,
    w_qkv,
    b_qkv,
    rel_table,
    w_proj,
    b_proj,
    w_fc1,
    b_fc1,
    w_fc2,
    b_fc2,
    norm_gains,
    norm_shifts,
    down_main,
    down_fc2,
    up_qkv,
    up_fc1,
    up_out,
):
    z, c, t = (lax.axis_index(name) for name in ("img", "ctx", "tp"))
    z_count, t_count = lax.axis_size("img"), lax.axis_size("tp")
    images, height, breadth = tokens.shape[:3]
    across = breadth // WIN
    image, column = t // across, t % across
    heads_here = rel_table.shape[1]
    heads = heads_here * t_count
    wide = heads_here * HD
    ff_here = w_fc1.shape[1]

    both = jnp.stack([lax.dynamic_index_in_dim(a, image, 0, False) for a in (tokens, cotangent)])
    both = lax.dynamic_slice_in_dim(jnp.roll(both, -SHIFT, 2), column * WIN, WIN, 2)
    upper = swap_ctx(both[:, :SHIFT])
    inputs, grad_output = jnp.concatenate([both[:, SHIFT:], upper], 1).reshape(2, TOK, C).astype(f32)

    def half(v):
        rows = v.shape[0] // 2
        return lax.dynamic_slice_in_dim(v, c * rows, rows, 0)

    group_a = jnp.concatenate([half(w_qkv).reshape(-1, 3 * wide), half(w_proj.T)], 1)
    group_b = half(w_fc1)
    group_c = half(w_fc2.T)
    full_a = assemble(spread_first(group_a), z, c, t).reshape(C, t_count, 4 * wide)
    full_fc1 = assemble(spread_last(group_b, swap_x, swap_y, 1, 2), z, c, t)
    full_fc2 = assemble(spread_last(group_c, swap_y, swap_x, 2, 1), z, c, t)
    full_qkv = full_a[:, :, : 3 * wide].reshape(C, 3 * C)
    full_proj = full_a[:, :, 3 * wide :].reshape(C, C)

    ids = lax.all_gather(adapter_id, "img")
    tables = jnp.concatenate(
        [v.reshape(ADAPT, -1) for v in (down_main, down_fc2, up_qkv, up_fc1, up_out)], 1
    )
    wanted = lax.dynamic_index_in_dim(ids, image, 1, False)
    pick = (wanted[:, None] == jnp.arange(ADAPT)[None, :]).astype(bf16)
    sent = dot(pick, tables).astype(bf16)
    mine = lax.all_to_all(sent, "img", 0, 0, tiled=True)
    theirs = swap_ctx(mine)
    mine, theirs = jnp.where(c == 0, mine, theirs), jnp.where(c == 0, theirs, mine)
    owned = jnp.stack([mine, theirs], 1).reshape(2 * z_count, -1)
    sizes = [v.size // ADAPT for v in (down_main, down_fc2, up_qkv, up_fc1, up_out)]
    cuts = [sum(sizes[:i]) for i in range(6)]
    main, fc2, qkv, fc1, out = (owned[:, cuts[i] : cuts[i + 1]] for i in range(5))
    main = main.reshape(2 * z_count, 3, -1).transpose(1, 0, 2).reshape(3, C, RANK)
    out = out.reshape(2 * z_count, 2, -1).transpose(1, 0, 2).reshape(2, RANK, C)
    qkv_down, proj_down, fc1_down = main
    fc2_down = fc2.reshape(FF, RANK)
    qkv_up = qkv.reshape(RANK, 3, t_count, wide).transpose(0, 2, 1, 3).reshape(RANK, 3 * C)
    fc1_up = fc1.reshape(RANK, FF)
    proj_up, fc2_up = out

    small = jnp.concatenate([b_qkv.reshape(-1), b_fc1, rel_table.T.reshape(-1)])
    small = lax.all_gather(small, "tp")
    bias_qkv = small[:, : 3 * wide].reshape(-1).astype(f32)
    bias_fc1 = small[:, 3 * wide : 3 * wide + ff_here].reshape(-1).astype(f32)
    table = small[:, 3 * wide + ff_here :].reshape(heads, RELS)

    region = lax.dynamic_slice_in_dim(regions, column * WIN, WIN, 1).reshape(TOK)
    mask = jnp.where(region[:, None] == region[None, :], 0.0, -100.0).astype(f32)
    additive = bias_of(table) + mask[None]
    valid = lax.dynamic_index_in_dim(valid_flag, image, 0, False).astype(f32)
    gains = norm_gains.astype(f32)
    shifts = norm_shifts.astype(f32)

    unit1, scale1 = norm_parts(inputs)
    shifted = (unit1 * gains[0] + shifts[0]).astype(bf16)
    low_qkv = dot(shifted, qkv_down).astype(bf16)
    mixed = (dot(shifted, full_qkv) + bias_qkv + dot(low_qkv, qkv_up)).astype(bf16)
    mixed = mixed.reshape(TOK, t_count, 3, heads_here, HD)
    queries, keys, values = (
        mixed[:, :, i].reshape(TOK, heads, HD).transpose(1, 0, 2) for i in range(3)
    )
    scores = SCALE * jnp.einsum("hqd,hkd->hqk", queries, keys, preferred_element_type=f32) + additive
    probs = jax.nn.softmax(scores, axis=-1)
    probs_low = probs.astype(bf16)
    attended = jnp.einsum("hqk,hkd->hqd", probs_low, values, preferred_element_type=f32)
    attended = attended.astype(bf16).transpose(1, 0, 2).reshape(TOK, C)
    low_proj = dot(attended, proj_down).astype(bf16)
    residual = inputs + valid * (
        dot_t(attended, full_proj) + b_proj.astype(f32) + dot(low_proj, proj_up)
    )
    unit2, scale2 = norm_parts(residual)
    normed2 = (unit2 * gains[1] + shifts[1]).astype(bf16)
    low_fc1 = dot(normed2, fc1_down).astype(bf16)
    preact = dot(normed2, full_fc1) + bias_fc1 + dot(low_fc1, fc1_up)
    cdf = 0.5 * (1.0 + lax.erf(preact * (0.5**0.5)))
    hidden = (preact * cdf).astype(bf16)
    slope = cdf + preact * jnp.exp(-0.5 * preact * preact) * (0.5 / jnp.pi) ** 0.5
    low_fc2 = dot(hidden, fc2_down).astype(bf16)
    output = residual + valid * (
        dot_t(hidden, full_fc2) + b_fc2.astype(f32) + dot(low_fc2, fc2_up)
    )

    grad_branch = (valid * grad_output).astype(bf16)
    grad_fc2_up = tdot(low_fc2, grad_branch)
    grad_low_fc2 = dot_t(grad_branch, fc2_up).astype(bf16)
    grad_fc2_down = tdot(hidden, grad_low_fc2)
    grad_hidden = dot(grad_branch, full_fc2) + dot_t(grad_low_fc2, fc2_down)
    grad_preact = (grad_hidden * slope).astype(bf16)
    grad_fc1_up = tdot(low_fc1, grad_preact)
    grad_low_fc1 = dot_t(grad_preact, fc1_up).astype(bf16)
    grad_normed2 = dot_t(grad_preact, full_fc1) + dot_t(grad_low_fc1, fc1_down)
    grad_fc1_down = tdot(normed2, grad_low_fc1)
    grad_residual = grad_output + norm_back(grad_normed2, gains[1], unit2, scale2)
    grad_attn = (valid * grad_residual).astype(bf16)
    grad_proj_up = tdot(low_proj, grad_attn)
    grad_low_proj = dot_t(grad_attn, proj_up).astype(bf16)
    grad_proj_down = tdot(attended, grad_low_proj)
    grad_attended = dot(grad_attn, full_proj) + dot_t(grad_low_proj, proj_down)
    grad_attended = grad_attended.astype(bf16).reshape(TOK, heads, HD).transpose(1, 0, 2)
    grad_probs = jnp.einsum("hqd,hkd->hqk", grad_attended, values, preferred_element_type=f32)
    centre = jnp.sum(grad_probs * probs, -1, keepdims=True)
    grad_scores = (probs * (grad_probs - centre)).astype(bf16)
    grad_queries = SCALE * jnp.einsum("hqk,hkd->hqd", grad_scores, keys, preferred_element_type=f32)
    grad_keys = SCALE * jnp.einsum("hqk,hqd->hkd", grad_scores, queries, preferred_element_type=f32)
    grad_values = jnp.einsum("hqk,hqd->hkd", probs_low, grad_attended, preferred_element_type=f32)
    grad_mixed = jnp.stack([grad_queries, grad_keys, grad_values]).astype(bf16)
    grad_mixed = grad_mixed.reshape(3, t_count, heads_here, TOK, HD).transpose(3, 1, 0, 2, 4)
    grad_mixed = grad_mixed.reshape(TOK, 3 * C)
    grad_qkv_up = tdot(low_qkv, grad_mixed)
    grad_low_qkv = dot_t(grad_mixed, qkv_up).astype(bf16)
    grad_shifted = dot_t(grad_mixed, full_qkv) + dot_t(grad_low_qkv, qkv_down)
    grad_qkv_down = tdot(shifted, grad_low_qkv)
    grad_tokens = grad_residual + norm_back(grad_shifted, gains[0], unit1, scale1)

    def placed(field):
        field = field.astype(bf16).reshape(2, SHIFT, WIN, C)
        lower = swap_ctx(field[1])
        here = lax.all_gather(jnp.concatenate([lower, field[0]], 0), "tp")
        here = here.reshape(images, across, height, WIN, C).transpose(0, 2, 1, 3, 4)
        return jnp.roll(here.reshape(images, height, breadth, C), SHIFT, 2)

    output = placed(output)
    grad_tokens = placed(grad_tokens).astype(f32)

    count = 2 * z_count * t_count
    grad_main = jnp.stack([grad_qkv_down, grad_proj_down, grad_fc1_down])
    grad_main = grad_main.reshape(3, count, -1).transpose(1, 0, 2).reshape(count, -1)
    grad_out = jnp.stack([grad_proj_up, grad_fc2_up])
    grad_out = grad_out.reshape(2, count, -1).transpose(1, 0, 2).reshape(count, -1)
    grad_qkv_up = grad_qkv_up.reshape(RANK, t_count, 3, wide).transpose(0, 2, 1, 3)
    terms = [
        grad_main,
        grad_fc2_down.reshape(count, -1),
        grad_qkv_up.reshape(count, -1),
        grad_fc1_up.reshape(count, -1),
        grad_out,
    ]
    sizes = [v.shape[1] for v in terms]
    cuts = [sum(sizes[:i]) for i in range(6)]
    terms = jnp.concatenate(terms, 1).astype(bf16)
    terms = lax.all_to_all(terms, ("img", "ctx", "tp"), 0, 0, tiled=True)
    source = jnp.broadcast_to(ids[:, None, :, None], (z_count, 2, images, across)).reshape(-1)
    pick = (jnp.arange(ADAPT)[:, None] == source[None, :]).astype(bf16)
    sums = dot(pick, terms)
    grad_main, grad_fc2, grad_qkv, grad_fc1, grad_out = (
        sums[:, cuts[i] : cuts[i + 1]] for i in range(5)
    )
    return (
        output,
        grad_tokens,
        grad_main.reshape(ADAPT, 3, -1),
        grad_fc2,
        grad_qkv,
        grad_fc1,
        grad_out.reshape(ADAPT, 2, -1),
    )


def solution(mesh):
    in_specs = (
        P("img", "ctx", None, None),
        P("img", "ctx", None, None),
        P("img"),
        P("img"),
        P("ctx", None),
        P("img", None, "tp"),
        P(None, "tp"),
        P(None, "tp"),
        P("tp", "img"),
        P(),
        P("img", "tp"),
        P("tp"),
        P("tp", "img"),
        P(),
        P(),
        P(),
        P(None, None, ("img", "ctx")),
        P(None, ("img", "ctx")),
        P(None, ("img", "ctx")),
        P(None, ("img", "ctx")),
        P(None, None, ("img", "ctx")),
    )
    out_specs = (
        P("img", "ctx", None, None),
        P("img", "ctx", None, None),
        P(None, None, ("img", "ctx", "tp")),
        P(None, ("img", "ctx", "tp")),
        P(None, ("img", "ctx", "tp")),
        P(None, ("img", "ctx", "tp")),
        P(None, None, ("img", "ctx", "tp")),
    )
    return jax.shard_map(
        per_device, mesh=mesh, in_specs=in_specs, out_specs=out_specs, check_vma=False
    )
```

```python
import jax
import jax.numpy as jnp
from jax import lax
from jax.experimental import pallas as pl
from jax.experimental.pallas import tpu as pltpu
from jax.sharding import PartitionSpec as P

C = 768
HD = 32
FF = 3072
WIN = 12
SHIFT = 6
RANK = 16
ADAPT = 8
RELS = 529
TOK = WIN * WIN
SCALE = HD ** (-0.5)
EPS = 1e-05
LANES = 128
SHARDS = 8
OWNERS = 32

bf16 = jnp.bfloat16
f32 = jnp.float32

VM = pl.BlockSpec(memory_space=pltpu.VMEM)
SM = pl.BlockSpec(memory_space=pltpu.SMEM)
ANY = pl.BlockSpec(memory_space=pl.ANY)


def dot(left, right):
    return jnp.dot(left, right, preferred_element_type=f32)


def dot_t(left, right):
    return lax.dot_general(left, right, (((1,), (1,)), ((), ())), preferred_element_type=f32)


def tdot(left, right):
    return lax.dot_general(left, right, (((0,), (0,)), ((), ())), preferred_element_type=f32)


def swap_ctx(v):
    return lax.ppermute(v, "ctx", [(0, 1), (1, 0)])


def swap_x(v):
    return lax.ppermute(v, "tp", [(0, 1), (1, 0), (2, 3), (3, 2)])


def swap_y(v):
    return lax.ppermute(v, "tp", [(0, 2), (2, 0), (1, 3), (3, 1)])


def ring(v):
    count = lax.axis_size("img")
    if count > 8:
        whole = lax.all_gather(v, "img", axis=0)
        here = lax.axis_index("img")
        return [lax.dynamic_index_in_dim(whole, (here - k) % count, 0, False) for k in range(count)]
    held = [v]
    for _ in range(count - 1):
        held.append(lax.ppermute(held[-1], "img", [(i, (i + 1) % count) for i in range(count)]))
    return held


class Group:
    def __init__(self, own):
        self.arrays, self.plan, self.places = [own], [(0, None)], [(0, 0, None)]

    def add(self, array, subs, keys):
        for core, held in ((0, array), (1, swap_ctx(array))):
            for sub, (k, j) in zip(subs, keys):
                self.plan.append((len(self.arrays), sub))
                self.places.append((k, j, core))
            self.arrays.append(held)

    def table(self):
        z, c, t = (lax.axis_index(name) for name in ("img", "ctx", "tp"))
        count = lax.axis_size("img")
        rows = C // count
        out = []
        for k, j, core in self.places:
            first = ((z - k) % count) * rows
            if core is not None:
                first = first + (c ^ core) * (rows // 2)
            out += [first, t ^ j]
        return jnp.stack([jnp.asarray(v, jnp.int32) for v in out])


def spread_first(own, half):
    group = Group(own)
    held = ring(half)
    by_x = [swap_x(a) for a in held]
    by_y = [swap_y(a) for a in held]
    cut = len(held) // 2
    by_xy = [swap_y(a) for a in by_x[:cut]] + [swap_x(a) for a in by_y[cut:]]
    for k in range(len(held)):
        for j, array in enumerate((held[k], by_x[k], by_y[k], by_xy[k])):
            if k or j:
                group.add(array, [None], [(k, j)])
    return group


def spread_last(own, half, first, second, one, two):
    group = Group(own)
    near = first(half)
    group.add(near, [None], [(0, one)])
    held = ring(jnp.stack([half, near]))
    for k, pair in enumerate(held):
        if k:
            group.add(pair, [0, 1], [(k, 0), (k, one)])
        group.add(second(pair), [0, 1], [(k, two), (k, one + two)])
    return group


def spread_far(own):
    whole = lax.all_gather(own, "img", axis=0, tiled=True)
    group = Group(whole)
    by_x = swap_x(whole)
    group.arrays += [by_x, swap_y(whole), swap_y(by_x)]
    group.plan += [(1, None), (2, None), (3, None)]
    group.places += [(0, 1, None), (0, 2, None), (0, 3, None)]

    def table():
        t = lax.axis_index("tp")
        return jnp.stack([v for j in range(4) for v in (jnp.int32(0), t ^ j)])

    group.table = table
    return group


def norm_parts(field):
    average = jnp.mean(field, -1, keepdims=True)
    centred = field - average
    variance = jnp.mean(centred * centred, -1, keepdims=True)
    scale = lax.rsqrt(variance + EPS)
    return centred * scale, scale


def norm_back(grad, gain, unit, scale):
    scaled = grad * gain
    return scale * (
        scaled
        - jnp.mean(scaled, -1, keepdims=True)
        - unit * jnp.mean(scaled * unit, -1, keepdims=True)
    )


def bias_of(table):
    heads = table.shape[0]
    span = 2 * WIN - 1
    q_col = jnp.arange(WIN)[:, None, None]
    step = jnp.arange(span)[None, :, None]
    k_col = jnp.arange(WIN)[None, None, :]
    index = ((span - 1 - step) * span + q_col - k_col + WIN - 1).reshape(-1)
    chosen = (jnp.arange(RELS)[:, None] == index[None, :]).astype(bf16)
    strips = dot(table, chosen).reshape(heads, WIN, span * WIN)
    rows = [strips[:, :, (WIN - 1 - r) * WIN :][:, :, :TOK] for r in range(WIN)]
    return jnp.stack(rows, 1).reshape(heads, TOK, TOK)


def start(group_refs, plan, places, whole, sems):
    for n, (index, sub) in enumerate(plan):
        source = group_refs[index]
        if sub is not None:
            source = source.at[sub]
        rows = source.shape[0]
        first = pl.multiple_of(places[2 * n], 16)
        block = places[2 * n + 1]
        pltpu.make_async_copy(
            source, whole.at[block, pl.ds(first, rows), :], sems.at[block]
        ).start()


def finish(whole, sems, block):
    pltpu.make_async_copy(whole.at[block], whole.at[block], sems.at[block]).wait()


def lane_group(rows):
    lane = lax.broadcasted_iota(jnp.int32, (rows, LANES), 1) // RANK
    row = lax.broadcasted_iota(jnp.int32, (rows, LANES), 0) % 8
    return (lane == row).astype(f32)


def low_of(spread_sum):
    for step in (64, 32, 16):
        spread_sum = spread_sum + pltpu.roll(spread_sum, step, 1)
    return spread_sum[:, :RANK].astype(bf16)


def over_lanes(low):
    lane = lax.broadcasted_iota(jnp.int32, (RANK, LANES), 1) % RANK
    rank = lax.broadcasted_iota(jnp.int32, (RANK, LANES), 0)
    return dot(low, (lane == rank).astype(bf16)).astype(bf16)


def fold(product):
    rows = product.shape[0]
    kept = (product * lane_group(rows)).reshape(rows // 8, 8, LANES)
    return jnp.sum(kept, 1)


def put_ranks(stage, tile, h, grad):
    for k in range(grad.shape[1] // LANES):
        stage[tile + k, pl.ds(h, RANK, stride=2), :] = grad[:, k * LANES : (k + 1) * LANES]


def pack_ranks(stage, tile, grad):
    width = grad.shape[1] // 2
    for h in range(2):
        put_ranks(stage, tile, h, grad[:, h * width : (h + 1) * width])
    return tile + width // LANES


def pack_flat(stage, tile, flat, rows):
    each = rows // OWNERS
    for k in range(each):
        stage[tile + k] = flat[pl.ds(k, OWNERS, stride=each), :]
    return tile + each


def pack_out(pay_out, stage):
    for k in range(stage.shape[0]):
        pay_out[:, k * LANES : (k + 1) * LANES] = stage[k].astype(bf16)


def adapters_kernel(owned, qkv_down, proj_down, fc1_down, fc2_down, qkv_up, fc1_up, proj_up, fc2_up, flat, ranks):
    col = 0
    for out in (qkv_down, proj_down, fc1_down, fc2_down):
        rows = out.shape[0] // 8
        each = rows // SHARDS
        for k in range(each):
            flat[pl.ds(k, SHARDS, stride=each), :] = owned[:, col : col + LANES].astype(f32)
            col += LANES
        spread = jnp.broadcast_to(flat[:rows, :][:, None, :], (rows, 8, LANES))
        out[...] = (spread.reshape(rows * 8, LANES) * lane_group(rows * 8)).astype(bf16)
    for out, width in ((qkv_up, 3 * C), (fc1_up, FF), (proj_up, C), (fc2_up, C)):
        tiles = width // LANES
        for e in range(2):
            for k in range(tiles):
                ranks[k, pl.ds(e, SHARDS, stride=2), :] = owned[:, col : col + LANES].astype(f32)
                col += LANES
        if out is qkv_up:
            wide = C // 4
            table = jnp.concatenate([ranks[k] for k in range(tiles)], 1)
            for b in range(4):
                parts = [table[:, i * C + b * wide : i * C + (b + 1) * wide] for i in range(3)]
                out[b] = jnp.concatenate(parts, 1).astype(bf16)
        else:
            for k in range(tiles):
                out[:, k * LANES : (k + 1) * LANES] = ranks[k].astype(bf16)


def prepare_adapters(owned):
    shapes = [(C, LANES)] * 3 + [(FF, LANES), (4, RANK, 3 * C // 4), (RANK, FF), (RANK, C), (RANK, C)]
    return pl.pallas_call(
        adapters_kernel,
        out_shape=[jax.ShapeDtypeStruct(s, bf16) for s in shapes],
        in_specs=[VM],
        out_specs=[VM] * 8,
        scratch_shapes=[pltpu.VMEM((FF // 8, LANES), f32), pltpu.VMEM((FF // LANES, RANK, LANES), f32)],
        compiler_params=pltpu.CompilerParams(vmem_limit_bytes=32 << 20),
        name="adapters",
    )(owned)


def head_mask(head):
    lane = lax.broadcasted_iota(jnp.int32, (TOK, C // 4), 1) // HD
    return lane == head


def only(head, field):
    return jnp.where(head_mask(head), field, jnp.zeros_like(field))


def attend_kernel(plan, places, valid, shifted, inputs, additive, bias_qkv, bias_proj, gain, offset, qkv_down, qkv_up, proj_down, proj_up, fc1_down, *rest):
    count = len(rest) - 11 - 2
    pieces, outs, (whole, sems) = rest[:count], rest[count:-2], rest[-2:]
    mixed_out, probs_out, attended_out, low_qkv_out, low_proj_out, low_fc1_out, residual_out, unit_out, scale_out, normed_out, _ = outs
    start(pieces, plan, places, whole, sems)
    wide = C // 4
    heads = wide // HD
    field = shifted[...]
    low_qkv = low_of(dot(field, qkv_down[...]))
    low_qkv_out[...] = low_qkv
    total = jnp.zeros((TOK, C), f32)
    low_total = jnp.zeros((TOK, LANES), f32)
    for b in range(4):
        finish(whole, sems, b)
        mixed = dot(field, whole[b, :, : 3 * wide]) + bias_qkv[b : b + 1] + dot(low_qkv, qkv_up[b])
        mixed = mixed.astype(bf16)
        mixed_out[b] = mixed
        queries, keys, values = (mixed[:, i * wide : (i + 1) * wide] for i in range(3))
        attended = jnp.zeros((TOK, wide), f32)
        for h in range(heads):
            scores = SCALE * dot_t(only(h, queries), keys) + additive[b * heads + h]
            weight = jnp.exp(scores - jnp.max(scores, -1, keepdims=True))
            probs = weight / jnp.sum(weight, -1, keepdims=True)
            probs_out[b * heads + h] = probs
            attended = attended + dot(probs.astype(bf16), only(h, values))
        attended = attended.astype(bf16)
        attended_out[b] = attended
        total = total + dot_t(attended, whole[b, :, 3 * wide :])
        low_total = low_total + dot(attended, proj_down[b * wide : (b + 1) * wide, :])
    low_proj = low_of(low_total)
    low_proj_out[...] = low_proj
    residual = inputs[...] + valid[0] * (total + bias_proj[...] + dot(low_proj, proj_up[...]))
    residual_out[...] = residual
    unit, scale = norm_parts(residual)
    unit_out[...] = unit
    scale_out[...] = scale
    normed = (unit * gain[...] + offset[...]).astype(bf16)
    normed_out[...] = normed
    low_fc1_out[...] = low_of(dot(normed, fc1_down[...]))


def attend(group, places, valid, *args):
    heads = C // HD
    shapes = [
        ((4, TOK, 3 * C // 4), bf16),
        ((heads, TOK, TOK), f32),
        ((4, TOK, C // 4), bf16),
        ((TOK, RANK), bf16),
        ((TOK, RANK), bf16),
        ((TOK, RANK), bf16),
        ((TOK, C), f32),
        ((TOK, C), f32),
        ((TOK, 1), f32),
        ((TOK, C), bf16),
        ((8, LANES), f32),
    ]
    return pl.pallas_call(
        lambda *refs: attend_kernel(group.plan, *refs),
        out_shape=[jax.ShapeDtypeStruct(*s) for s in shapes],
        in_specs=[SM, SM] + [VM] * len(args) + [ANY] * len(group.arrays),
        out_specs=[VM] * len(shapes),
        scratch_shapes=[pltpu.VMEM((4, C, C), bf16), pltpu.SemaphoreType.DMA((4,))],
        compiler_params=pltpu.CompilerParams(vmem_limit_bytes=48 << 20),
        name="attend",
    )(places, valid, *args, *group.arrays)


def expand_kernel(plan, places, normed, low_fc1, fc1_up, bias_fc1, fc2_down, *rest):
    count = len(rest) - 3 - 2
    pieces, (hidden_out, slope_out, low_out), (whole, sems) = rest[:count], rest[count:-2], rest[-2:]
    start(pieces, plan, places, whole, sems)
    field, low_fc1 = normed[...], low_fc1[...]
    low_total = jnp.zeros((TOK, LANES), f32)
    for b in range(4):
        cols = slice(b * C, (b + 1) * C)
        finish(whole, sems, b)
        preact = dot(field, whole[b]) + bias_fc1[:, cols] + dot(low_fc1, fc1_up[:, cols])
        cdf = 0.5 * (1.0 + lax.erf(preact * (0.5**0.5)))
        hidden = (preact * cdf).astype(bf16)
        hidden_out[b] = hidden
        slope_out[b] = cdf + preact * jnp.exp(-0.5 * preact * preact) * (0.5 / jnp.pi) ** 0.5
        low_total = low_total + dot(hidden, fc2_down[cols, :])
    low_out[...] = low_of(low_total)


def expand(group, places, *args):
    shapes = [((4, TOK, C), bf16), ((4, TOK, C), f32), ((TOK, RANK), bf16)]
    return pl.pallas_call(
        lambda *refs: expand_kernel(group.plan, *refs),
        out_shape=[jax.ShapeDtypeStruct(*s) for s in shapes],
        in_specs=[SM] + [VM] * len(args) + [ANY] * len(group.arrays),
        out_specs=[VM] * len(shapes),
        scratch_shapes=[pltpu.VMEM((4, C, C), bf16), pltpu.SemaphoreType.DMA((4,))],
        compiler_params=pltpu.CompilerParams(vmem_limit_bytes=48 << 20),
        name="expand",
    )(places, *args, *group.arrays)


def contract_kernel(plan_b, plan_c, count_b, places_b, places_c, valid, grad_output, residual, unit, scale, hidden, slope, low_fc2, normed, low_fc1, fc2_down, fc2_up, fc1_down, fc1_up, bias_fc2, gain, *rest):
    pieces, (output_out, grad_out, pay_out), (whole_b, whole_c, sems_b, sems_c, stage, flat) = rest[:-9], rest[-9:-6], rest[-6:]
    start(pieces[count_b:], plan_c, places_c, whole_c, sems_c)
    start(pieces[:count_b], plan_b, places_b, whole_b, sems_b)
    dz = grad_output[...]
    branch = (valid[0] * dz).astype(bf16)
    low_fc2, low_fc1, normed = low_fc2[...], low_fc1[...], normed[...]
    grad_low_fc2 = dot_t(branch, fc2_up[...]).astype(bf16)
    spread_fc2 = over_lanes(grad_low_fc2)
    grad_low_fc1 = jnp.zeros((TOK, RANK), f32)
    grad_normed = jnp.zeros((TOK, C), f32)
    total = jnp.zeros((TOK, C), f32)
    for b in range(4):
        cols = slice(b * C, (b + 1) * C)
        finish(whole_c, sems_c, b)
        total = total + dot_t(hidden[b], whole_c[b])
        grad_hidden = dot(branch, whole_c[b]) + dot_t(spread_fc2, fc2_down[cols, :])
        grad_preact = (grad_hidden * slope[b]).astype(bf16)
        flat[b * C // 8 : (b + 1) * C // 8, :] = fold(tdot(hidden[b], spread_fc2))
        grad_up = tdot(low_fc1, grad_preact)
        width = FF // 2
        at = b * C % width
        put_ranks(stage, (FF // 2 + at) // LANES, b * C // width, grad_up)
        grad_low_fc1 = grad_low_fc1 + dot_t(grad_preact, fc1_up[:, cols])
        finish(whole_b, sems_b, b)
        grad_normed = grad_normed + dot_t(grad_preact, whole_b[b])
    pack_flat(stage, 0, flat, FF // 8)
    tile = FF // LANES
    residual = residual[...]
    output_out[...] = (
        residual + valid[0] * (total + bias_fc2[...] + dot(low_fc2, fc2_up[...]))
    ).astype(bf16)
    tile = pack_ranks(stage, tile, tdot(low_fc2, branch))
    grad_low_fc1 = grad_low_fc1.astype(bf16)
    spread_fc1 = over_lanes(grad_low_fc1)
    grad_normed = grad_normed + dot_t(spread_fc1, fc1_down[...])
    grad_out[...] = dz + norm_back(grad_normed, gain[...], unit[...], scale[...])
    flat[: C // 8, :] = fold(tdot(normed, spread_fc1))
    pack_flat(stage, tile, flat, C // 8)
    pack_out(pay_out, stage)


def contract(group_b, group_c, places_b, places_c, valid, *args):
    width = FF + C
    shapes = [((TOK, C), bf16), ((TOK, C), f32), ((OWNERS, width), bf16)]
    return pl.pallas_call(
        lambda *refs: contract_kernel(group_b.plan, group_c.plan, len(group_b.arrays), *refs),
        out_shape=[jax.ShapeDtypeStruct(*s) for s in shapes],
        in_specs=[SM] * 3 + [VM] * len(args) + [ANY] * (len(group_b.arrays) + len(group_c.arrays)),
        out_specs=[VM] * len(shapes),
        scratch_shapes=[
            pltpu.VMEM((4, C, C), bf16),
            pltpu.VMEM((4, C, C), bf16),
            pltpu.SemaphoreType.DMA((4,)),
            pltpu.SemaphoreType.DMA((4,)),
            pltpu.VMEM((width // LANES, OWNERS, LANES), f32),
            pltpu.VMEM((FF // 8, LANES), f32),
        ],
        compiler_params=pltpu.CompilerParams(vmem_limit_bytes=56 << 20),
        name="contract",
    )(places_b, places_c, valid, *args, *group_b.arrays, *group_c.arrays)


def back_kernel(plan, places, valid, grad_residual, unit, scale, gain, shifted, mixed, probs, attended, low_qkv, low_proj, qkv_down, qkv_up, proj_down, proj_up, *rest):
    pieces, (grad_out, pay_out), (whole, sems, stage, flat, ranks) = rest[:-7], rest[-7:-5], rest[-5:]
    start(pieces, plan, places, whole, sems)
    wide = C // 4
    heads = wide // HD
    grad_residual = grad_residual[...]
    grad_attn = (valid[0] * grad_residual).astype(bf16)
    low_qkv = low_qkv[...]
    grad_low_proj = dot_t(grad_attn, proj_up[...]).astype(bf16)
    spread_proj = over_lanes(grad_low_proj)
    grad_shifted = jnp.zeros((TOK, C), f32)
    grad_low_qkv = jnp.zeros((TOK, RANK), f32)
    for b in range(4):
        rows = slice(b * wide, (b + 1) * wide)
        finish(whole, sems, b)
        flat[b * wide // 8 : (b + 1) * wide // 8, :] = fold(tdot(attended[b], spread_proj))
        grad_heads = dot(grad_attn, whole[b, :, 3 * wide :]) + dot_t(spread_proj, proj_down[rows, :])
        grad_heads = grad_heads.astype(bf16)
        queries, keys, values = (mixed[b, :, i * wide : (i + 1) * wide] for i in range(3))
        grad_queries, grad_keys, grad_values = (jnp.zeros((TOK, wide), f32) for _ in range(3))
        for h in range(heads):
            here = probs[b * heads + h]
            mine = only(h, grad_heads)
            grad_probs = dot_t(mine, values)
            centre = jnp.sum(grad_probs * here, -1, keepdims=True)
            grad_scores = (here * (grad_probs - centre)).astype(bf16)
            grad_queries = grad_queries + dot(grad_scores, only(h, keys))
            grad_keys = grad_keys + tdot(grad_scores, only(h, queries))
            grad_values = grad_values + tdot(here.astype(bf16), mine)
        grad_mixed = jnp.concatenate([SCALE * grad_queries, SCALE * grad_keys, grad_values], 1).astype(bf16)
        grad_up = tdot(low_qkv, grad_mixed)
        for i in range(3):
            ranks[:, i * C + b * wide : i * C + (b + 1) * wide] = grad_up[:, i * wide : (i + 1) * wide]
        grad_low_qkv = grad_low_qkv + dot_t(grad_mixed, qkv_up[b])
        grad_shifted = grad_shifted + dot_t(grad_mixed, whole[b, :, : 3 * wide])
    tile = pack_ranks(stage, 0, ranks[...])
    tile = pack_flat(stage, tile, flat, C // 8)
    tile = pack_ranks(stage, tile, tdot(low_proj[...], grad_attn))
    spread_qkv = over_lanes(grad_low_qkv.astype(bf16))
    grad_shifted = grad_shifted + dot_t(spread_qkv, qkv_down[...])
    grad_out[...] = (
        grad_residual + norm_back(grad_shifted, gain[...], unit[...], scale[...])
    ).astype(bf16)
    flat[...] = fold(tdot(shifted[...], spread_qkv))
    pack_flat(stage, tile, flat, C // 8)
    pack_out(pay_out, stage)


def back(group, places, valid, *args):
    width = (3 * C * RANK + 3 * C * RANK) // OWNERS
    shapes = [((TOK, C), bf16), ((OWNERS, width), bf16)]
    return pl.pallas_call(
        lambda *refs: back_kernel(group.plan, *refs),
        out_shape=[jax.ShapeDtypeStruct(*s) for s in shapes],
        in_specs=[SM] * 2 + [VM] * len(args) + [ANY] * len(group.arrays),
        out_specs=[VM] * len(shapes),
        scratch_shapes=[
            pltpu.VMEM((4, C, C), bf16),
            pltpu.SemaphoreType.DMA((4,)),
            pltpu.VMEM((width // LANES, OWNERS, LANES), f32),
            pltpu.VMEM((C // 8, LANES), f32),
            pltpu.VMEM((RANK, 3 * C), f32),
        ],
        compiler_params=pltpu.CompilerParams(vmem_limit_bytes=48 << 20),
        name="back",
    )(places, valid, *args, *group.arrays)


def per_device(
    tokens,
    cotangent,
    adapter_id,
    valid_flag,
    regions,
    w_qkv,
    b_qkv,
    rel_table,
    w_proj,
    b_proj,
    w_fc1,
    b_fc1,
    w_fc2,
    b_fc2,
    norm_gains,
    norm_shifts,
    down_main,
    down_fc2,
    up_qkv,
    up_fc1,
    up_out,
):
    z, c, t = (lax.axis_index(name) for name in ("img", "ctx", "tp"))
    z_count, t_count = lax.axis_size("img"), lax.axis_size("tp")
    images, height, breadth = tokens.shape[:3]
    across = breadth // WIN
    image, column = t // across, t % across
    heads_here = rel_table.shape[1]
    heads = heads_here * t_count
    wide = heads_here * HD
    ff_here = w_fc1.shape[1]

    both = jnp.stack([lax.dynamic_index_in_dim(a, image, 0, False) for a in (tokens, cotangent)])
    both = lax.dynamic_slice_in_dim(jnp.roll(both, -SHIFT, 2), column * WIN, WIN, 2)
    upper = swap_ctx(both[:, :SHIFT])
    inputs, grad_output = jnp.concatenate([both[:, SHIFT:], upper], 1).reshape(2, TOK, C).astype(f32)

    def half(v):
        rows = v.shape[0] // 2
        return lax.dynamic_slice_in_dim(v, c * rows, rows, 0)

    own_a = jnp.concatenate([w_qkv.reshape(-1, 3 * wide), w_proj.T], 1)
    own_b = w_fc1
    own_c = w_fc2.T
    if z_count <= 8:
        group_a = spread_first(own_a, half(own_a))
        group_b = spread_last(own_b, half(own_b), swap_x, swap_y, 1, 2)
        group_c = spread_last(own_c, half(own_c), swap_y, swap_x, 2, 1)
    else:
        group_a, group_b, group_c = (spread_far(v) for v in (own_a, own_b, own_c))
    places_a, places_b, places_c = (group.table() for group in (group_a, group_b, group_c))

    ids = lax.all_gather(adapter_id, "img")
    parts = [down_main[:, i] for i in range(3)] + [down_fc2, up_qkv, up_fc1] + [up_out[:, i] for i in range(2)]
    sizes = [v.shape[1] for v in parts]
    tables = jnp.concatenate(parts, 1)
    wanted = lax.dynamic_index_in_dim(ids, image, 1, False)
    pick = (wanted[:, None] == jnp.arange(ADAPT)[None, :]).astype(bf16)
    sent = dot(pick, tables).astype(bf16)
    mine = lax.all_to_all(sent, "img", 0, 0, tiled=True)
    theirs = swap_ctx(mine)
    mine, theirs = jnp.where(c == 0, mine, theirs), jnp.where(c == 0, theirs, mine)
    owned = jnp.stack([mine, theirs], 1).reshape(2 * z_count, -1)
    if 2 * z_count != SHARDS:
        cuts = [sum(sizes[:i]) for i in range(9)]
        owned = jnp.concatenate([owned[:, cuts[i] : cuts[i + 1]].reshape(SHARDS, -1) for i in range(8)], 1)
    qkv_down, proj_down, fc1_down, fc2_down, qkv_up, fc1_up, proj_up, fc2_up = prepare_adapters(owned)

    small = jnp.concatenate([b_qkv.reshape(-1), b_fc1, rel_table.T.reshape(-1)])
    small = lax.all_gather(small, "tp")
    bias_qkv = small[:, : 3 * wide].astype(f32)
    bias_fc1 = small[:, 3 * wide : 3 * wide + ff_here].reshape(1, -1).astype(f32)
    table = small[:, 3 * wide + ff_here :].reshape(heads, RELS)

    region = lax.dynamic_slice_in_dim(regions, column * WIN, WIN, 1).reshape(TOK)
    mask = jnp.where(region[:, None] == region[None, :], 0.0, -100.0).astype(f32)
    additive = bias_of(table) + mask[None]
    valid = lax.dynamic_index_in_dim(valid_flag, image, 0, False).astype(f32).reshape(1)
    gains = norm_gains.astype(f32)
    shifts = norm_shifts.astype(f32)

    unit1, scale1 = norm_parts(inputs)
    shifted = (unit1 * gains[0] + shifts[0]).astype(bf16)
    mixed, probs, attended, low_qkv, low_proj, low_fc1, residual, unit2, scale2, normed2, _ = attend(
        group_a, places_a, valid, shifted, inputs, additive, bias_qkv, b_proj.astype(f32)[None],
        gains[1:], shifts[1:], qkv_down, qkv_up, proj_down, proj_up, fc1_down,
    )
    hidden, slope, low_fc2 = expand(group_b, places_b, normed2, low_fc1, fc1_up, bias_fc1, fc2_down)
    output, grad_residual, pay_one = contract(
        group_b, group_c, places_b, places_c, valid, grad_output, residual, unit2, scale2, hidden, slope,
        low_fc2, normed2, low_fc1, fc2_down, fc2_up, fc1_down, fc1_up, b_fc2.astype(f32)[None], gains[1:],
    )
    grad_tokens, pay_two = back(
        group_a, places_a, valid, grad_residual, unit1, scale1, gains[:1], shifted, mixed, probs, attended,
        low_qkv, low_proj, qkv_down, qkv_up, proj_down, proj_up,
    )

    def placed(field):
        field = field.reshape(2, SHIFT, WIN, C)
        lower = swap_ctx(field[1])
        here = lax.all_gather(jnp.concatenate([lower, field[0]], 0), "tp")
        here = here.reshape(images, across, height, WIN, C).transpose(0, 2, 1, 3, 4)
        return jnp.roll(here.reshape(images, height, breadth, C), SHIFT, 2)

    output = placed(output)
    grad_tokens = placed(grad_tokens).astype(f32)

    count = 2 * z_count * t_count
    source = jnp.broadcast_to(ids[:, None, :, None], (z_count, 2, images, across)).reshape(-1)
    pick = (jnp.arange(ADAPT)[:, None] == source[None, :]).astype(bf16)

    def summed(pay, widths):
        cuts = [sum(widths[:i]) for i in range(len(widths) + 1)]
        if count != OWNERS:
            pay = jnp.concatenate(
                [pay[:, a:b].reshape(count, -1) for a, b in zip(cuts, cuts[1:])], 1
            )
            cuts = [v * OWNERS // count for v in cuts]
        sums = dot(pick, lax.all_to_all(pay, ("img", "ctx", "tp"), 0, 0, tiled=True))
        return [sums[:, a:b] for a, b in zip(cuts, cuts[1:])]

    one = C * RANK // OWNERS
    grad_fc2, grad_fc1, grad_fc2_up, grad_fc1_down = summed(pay_one, [4 * one, 4 * one, one, one])
    grad_qkv, grad_proj_down, grad_proj_up, grad_qkv_down = summed(pay_two, [3 * one, one, one, one])
    return (
        output,
        grad_tokens,
        jnp.stack([grad_qkv_down, grad_proj_down, grad_fc1_down], 1),
        grad_fc2,
        grad_qkv,
        grad_fc1,
        jnp.stack([grad_proj_up, grad_fc2_up], 1),
    )


def solution(mesh):
    in_specs = (
        P("img", "ctx", None, None),
        P("img", "ctx", None, None),
        P("img"),
        P("img"),
        P("ctx", None),
        P("img", None, "tp"),
        P(None, "tp"),
        P(None, "tp"),
        P("tp", "img"),
        P(),
        P("img", "tp"),
        P("tp"),
        P("tp", "img"),
        P(),
        P(),
        P(),
        P(None, None, ("img", "ctx")),
        P(None, ("img", "ctx")),
        P(None, ("img", "ctx")),
        P(None, ("img", "ctx")),
        P(None, None, ("img", "ctx")),
    )
    out_specs = (
        P("img", "ctx", None, None),
        P("img", "ctx", None, None),
        P(None, None, ("img", "ctx", "tp")),
        P(None, ("img", "ctx", "tp")),
        P(None, ("img", "ctx", "tp")),
        P(None, ("img", "ctx", "tp")),
        P(None, None, ("img", "ctx", "tp")),
    )
    return jax.shard_map(
        per_device, mesh=mesh, in_specs=in_specs, out_specs=out_specs, check_vma=False
    )
```

```python
import jax
import jax.numpy as jnp
from jax import lax
from jax.experimental import pallas as pl
from jax.experimental.pallas import tpu as pltpu
from jax.sharding import PartitionSpec as P

C = 768
HD = 32
FF = 3072
WIN = 12
SHIFT = 6
RANK = 16
ADAPT = 8
RELS = 529
TOK = WIN * WIN
SCALE = HD ** (-0.5)
EPS = 1e-05
LANES = 128
SHARDS = 8
OWNERS = 32

bf16 = jnp.bfloat16
f32 = jnp.float32

VM = pl.BlockSpec(memory_space=pltpu.VMEM)
SM = pl.BlockSpec(memory_space=pltpu.SMEM)
HBM = pl.BlockSpec(memory_space=pltpu.HBM)


def params(mib):
    return pltpu.CompilerParams(vmem_limit_bytes=mib << 20)


def in_hbm(arrays):
    return [pltpu.with_memory_space_constraint(v, pltpu.HBM) for v in arrays]


def cost(us):
    return pl.CostEstimate(flops=0, transcendentals=0, bytes_accessed=int(us * 3e6))


def dot(left, right):
    return jnp.dot(left, right, preferred_element_type=f32)


def dot_t(left, right):
    return lax.dot_general(left, right, (((1,), (1,)), ((), ())), preferred_element_type=f32)


def tdot(left, right):
    return lax.dot_general(left, right, (((0,), (0,)), ((), ())), preferred_element_type=f32)


def swap_ctx(v):
    return lax.ppermute(v, "ctx", [(0, 1), (1, 0)])


def swap_x(v):
    return lax.ppermute(v, "tp", [(0, 1), (1, 0), (2, 3), (3, 2)])


def swap_y(v):
    return lax.ppermute(v, "tp", [(0, 2), (2, 0), (1, 3), (3, 1)])


def swap_xy(v):
    return lax.ppermute(v, "tp", [(0, 3), (3, 0), (1, 2), (2, 1)])


def ring(v):
    count = lax.axis_size("img")
    if count > 8:
        whole = lax.all_gather(v, "img", axis=0)
        here = lax.axis_index("img")
        return [lax.dynamic_index_in_dim(whole, (here - k) % count, 0, False) for k in range(count)]
    held = [v]
    for _ in range(count - 1):
        held.append(lax.ppermute(held[-1], "img", [(i, (i + 1) % count) for i in range(count)]))
    return held


class Group:
    def __init__(self, own):
        self.arrays, self.plan, self.places = [own], [(0, None)], [(0, 0, None)]

    def add(self, array, subs, keys):
        for core, held in ((0, array), (1, swap_ctx(array))):
            for sub, (k, j) in zip(subs, keys):
                self.plan.append((len(self.arrays), sub))
                self.places.append((k, j, core))
            self.arrays.append(held)

    def table(self):
        z, c, t = (lax.axis_index(name) for name in ("img", "ctx", "tp"))
        count = lax.axis_size("img")
        rows = C // count
        out = []
        for k, j, core in self.places:
            first = ((z - k) % count) * rows
            if core is not None:
                first = first + (c ^ core) * (rows // 2)
            out += [first, t ^ j]
        return jnp.stack([jnp.asarray(v, jnp.int32) for v in out])


def spread_first(own, half):
    group = Group(own)
    held = ring(half)
    by_x = [swap_x(a) for a in held]
    by_y = [swap_y(a) for a in held]
    cut = len(held) // 2
    by_xy = [swap_y(a) for a in by_x[:cut]] + [swap_x(a) for a in by_y[cut:]]
    for k in range(len(held)):
        for j, array in enumerate((held[k], by_x[k], by_y[k], by_xy[k])):
            if k or j:
                group.add(array, [None], [(k, j)])
    return group


def spread_last(own, half, first, second, one, two):
    group = Group(own)
    near = first(half)
    group.add(near, [None], [(0, one)])
    held = ring(jnp.stack([half, near]))
    for k, pair in enumerate(held):
        if k:
            group.add(pair, [0, 1], [(k, 0), (k, one)])
        group.add(second(pair), [0, 1], [(k, two), (k, one + two)])
    return group


def spread_far(own):
    whole = lax.all_gather(own, "img", axis=0, tiled=True)
    group = Group(whole)
    by_x = swap_x(whole)
    group.arrays += [by_x, swap_y(whole), swap_y(by_x)]
    group.plan += [(1, None), (2, None), (3, None)]
    group.places += [(0, 1, None), (0, 2, None), (0, 3, None)]

    def table():
        t = lax.axis_index("tp")
        return jnp.stack([v for j in range(4) for v in (jnp.int32(0), t ^ j)])

    group.table = table
    return group


def norm_parts(field):
    average = jnp.mean(field, -1, keepdims=True)
    centred = field - average
    variance = jnp.mean(centred * centred, -1, keepdims=True)
    scale = lax.rsqrt(variance + EPS)
    return centred * scale, scale


def norm_back(grad, gain, unit, scale):
    scaled = grad * gain
    return scale * (
        scaled
        - jnp.mean(scaled, -1, keepdims=True)
        - unit * jnp.mean(scaled * unit, -1, keepdims=True)
    )


def start(group_refs, plan, places, whole, sems):
    for n, (index, sub) in enumerate(plan):
        source = group_refs[index]
        if sub is not None:
            source = source.at[sub]
        rows = source.shape[0]
        first = pl.multiple_of(places[2 * n], 16)
        block = places[2 * n + 1]
        pltpu.make_async_copy(
            source, whole.at[block, pl.ds(first, rows), :], sems.at[block]
        ).start()


def finish(whole, sems, block):
    pltpu.make_async_copy(whole.at[block], whole.at[block], sems.at[block]).wait()


def lane_group(rows):
    lane = lax.broadcasted_iota(jnp.int32, (rows, LANES), 1) // RANK
    row = lax.broadcasted_iota(jnp.int32, (rows, LANES), 0) % 8
    return (lane == row).astype(f32)


def low_of(spread_sum):
    for step in (64, 32, 16):
        spread_sum = spread_sum + pltpu.roll(spread_sum, step, 1)
    return spread_sum[:, :RANK].astype(bf16)


def over_lanes(low):
    lane = lax.broadcasted_iota(jnp.int32, (RANK, LANES), 1) % RANK
    rank = lax.broadcasted_iota(jnp.int32, (RANK, LANES), 0)
    return dot(low, (lane == rank).astype(bf16)).astype(bf16)


def fold(product):
    rows = product.shape[0]
    kept = (product * lane_group(rows)).reshape(rows // 8, 8, LANES)
    return jnp.sum(kept, 1)


def put_ranks(stage, tile, h, grad):
    for k in range(grad.shape[1] // LANES):
        stage[tile + k, pl.ds(h, RANK, stride=2), :] = grad[:, k * LANES : (k + 1) * LANES]


def pack_ranks(stage, tile, grad):
    width = grad.shape[1] // 2
    for h in range(2):
        put_ranks(stage, tile, h, grad[:, h * width : (h + 1) * width])
    return tile + width // LANES


def pack_flat(stage, tile, flat, rows):
    each = rows // OWNERS
    for k in range(each):
        stage[tile + k] = flat[pl.ds(k, OWNERS, stride=each), :]
    return tile + each


def pack_out(pay_out, stage):
    for k in range(stage.shape[0]):
        pay_out[:, k * LANES : (k + 1) * LANES] = stage[k].astype(bf16)


def cut_kernel(where, tokens, cotangent, own, away):
    image, column = where[0], where[1]
    for i, field in enumerate((tokens, cotangent)):
        block = field[image].astype(f32)
        rows = []
        for r in range(WIN):
            at = r * 2 * WIN
            inner = block[at + SHIFT : at + SHIFT + WIN]
            outer = jnp.concatenate([block[at + SHIFT + WIN : at + 2 * WIN], block[at : at + SHIFT]], 0)
            rows.append(jnp.where(column == 0, inner, outer))
        away[i] = jnp.concatenate(rows[:SHIFT], 0).astype(bf16)
        own[i] = jnp.concatenate(rows[SHIFT:], 0).astype(bf16)


def cut_windows(where, tokens, cotangent):
    flat = (tokens.shape[0], -1, C)
    return pl.pallas_call(
        cut_kernel,
        out_shape=[jax.ShapeDtypeStruct((2, TOK // 2, C), bf16)] * 2,
        in_specs=[SM, VM, VM],
        out_specs=[VM, VM],
        compiler_params=params(8),
        name="cut_windows",
    )(where, tokens.reshape(flat), cotangent.reshape(flat))


def place_kernel(where, *refs):
    pieces, out, held = refs[:4], refs[4], refs[5]
    for j, piece in enumerate(pieces):
        held[where[0] ^ j] = piece[...].astype(f32)
    for i in range(2):
        left, right = held[2 * i], held[2 * i + 1]
        for r in range(WIN):
            rows = slice(r * WIN, (r + 1) * WIN)
            inner, outer = left[rows], right[rows]
            line = jnp.concatenate([outer[SHIFT:], inner, outer[:SHIFT]], 0)
            out[i, r * 2 * WIN : (r + 1) * 2 * WIN] = line.astype(out.dtype)


def place(where, pieces, dtype):
    return pl.pallas_call(
        place_kernel,
        out_shape=jax.ShapeDtypeStruct((2, 2 * TOK, C), dtype),
        in_specs=[SM] + [VM] * 4,
        out_specs=VM,
        scratch_shapes=[pltpu.VMEM((4, TOK, C), f32)],
        compiler_params=params(12),
        cost_estimate=cost(2),
        name="place",
    )(where, *pieces)


TILES = 12 * RANK


def choose_kernel(wanted, main, fc2, qkv, fc1, out, chosen, table, stage):
    col = 0
    for field in (main[0], main[1], main[2], fc2[...], qkv[...], fc1[...], out[0], out[1]):
        table[:, col : col + field.shape[1]] = field.astype(f32)
        col += field.shape[1]
    for k in range(chosen.shape[0]):
        for tile in range(TILES):
            field = table[:, tile * LANES : (tile + 1) * LANES]
            here = lax.broadcasted_iota(jnp.int32, field.shape, 0) == wanted[k]
            stage[tile : tile + 1, :] = jnp.sum(jnp.where(here, field, 0.0), 0, keepdims=True)
        chosen[k] = stage[...].astype(bf16)


def choose(wanted, *tables):
    count = wanted.shape[0]
    return pl.pallas_call(
        choose_kernel,
        out_shape=jax.ShapeDtypeStruct((count, TILES, LANES), bf16),
        in_specs=[SM] + [VM] * 5,
        out_specs=VM,
        scratch_shapes=[pltpu.VMEM((ADAPT, TILES * LANES), f32), pltpu.VMEM((TILES, LANES), f32)],
        compiler_params=params(6),
        cost_estimate=cost(2),
        name="choose",
    )(wanted, *tables)


def adapters_kernel(shards, mine, theirs, qkv_down, proj_down, fc1_down, fc2_down, qkv_up, fc1_up, proj_up, fc2_up, ranks):
    for n in range(SHARDS):
        held = (mine, theirs)[n % 2]
        shard = shards[n]
        row = 0
        for out in (qkv_down, proj_down, fc1_down, fc2_down):
            rows = out.shape[1]
            part = held[n // 2, row : row + rows // 8, :].astype(f32)
            spread = jnp.broadcast_to(part[:, None, :], (rows // 8, 8, LANES)).reshape(rows, LANES)
            out[shard] = (spread * lane_group(rows)).astype(bf16)
            row += rows // 8
        tile = 0
        for width in (3 * C, FF, C, C):
            part = held[n // 2, row : row + 2 * width // LANES, :].astype(f32)
            for e in range(2):
                for k in range(width // LANES):
                    at = e * width // LANES + k
                    ranks[tile + k, pl.ds(2 * shard + e, 1), :] = part[at : at + 1]
            row += 2 * width // LANES
            tile += width // LANES
    wide = C // 4
    tile = 3 * C // LANES
    table = jnp.concatenate([ranks[k] for k in range(tile)], 1)
    for b in range(4):
        parts = [table[:, i * C + b * wide : i * C + (b + 1) * wide] for i in range(3)]
        qkv_up[b] = jnp.concatenate(parts, 1).astype(bf16)
    for out in (fc1_up, proj_up, fc2_up):
        for k in range(out.shape[1] // LANES):
            out[:, k * LANES : (k + 1) * LANES] = ranks[tile + k].astype(bf16)
        tile += out.shape[1] // LANES


def prepare_adapters(shards, mine, theirs):
    downs = [(SHARDS, C // SHARDS, LANES)] * 3 + [(SHARDS, FF // SHARDS, LANES)]
    ups = [(4, RANK, 3 * C // 4), (RANK, FF), (RANK, C), (RANK, C)]
    tiles = (3 * C + FF + 2 * C) // LANES
    made = pl.pallas_call(
        adapters_kernel,
        out_shape=[jax.ShapeDtypeStruct(v, bf16) for v in downs + ups],
        in_specs=[SM, VM, VM],
        out_specs=[VM] * 8,
        scratch_shapes=[pltpu.VMEM((tiles, RANK, LANES), f32)],
        compiler_params=params(8),
        cost_estimate=cost(2),
        name="adapters",
    )(shards, mine, theirs)
    return [v.reshape(-1, LANES) for v in made[:4]] + list(made[4:])


SPAN = 2 * WIN - 1
STRIP = 3 * LANES


def bias_kernel(where, regions, *refs):
    smalls, (additive, bias_qkv, bias_fc1, strips) = refs[:4], refs[4:]
    column = where[1]
    wide = C // 4
    heads = wide // HD
    tables = []
    for j, small in enumerate(smalls):
        field = small[...].astype(f32)
        block = where[0] ^ j
        bias_qkv[block] = jnp.concatenate([field[i : i + 1, :wide] for i in range(3)], 1)
        bias_fc1[block] = field[3:4]
        tables.append(small[8:, :])
    table = jnp.concatenate(tables, 0)
    lane = lax.broadcasted_iota(jnp.int32, (C, STRIP), 1)
    entry = lax.broadcasted_iota(jnp.int32, (C, STRIP), 0) - (lane // WIN) * SPAN - lane % WIN - WIN + 1
    for key in range(WIN):
        strip = dot(table, (entry == -key).astype(bf16))
        for j in range(4):
            for h in range(heads):
                strips[j * heads + h, key : key + 1, :] = strip[8 * j + h : 8 * j + h + 1]
    row = lax.broadcasted_iota(jnp.int32, (TOK, WIN), 0) // WIN
    at_row = (row == lax.broadcasted_iota(jnp.int32, (TOK, WIN), 1)).astype(bf16)
    lines = dot(at_row, regions[...].astype(f32).astype(bf16))
    cell = lax.broadcasted_iota(jnp.int32, lines.shape, 0) % WIN + column * WIN
    lines = jnp.where(cell == lax.broadcasted_iota(jnp.int32, lines.shape, 1), lines, 0.0)
    by_key = jnp.sum(lines, 1, keepdims=True)
    by_query = dot_t(jnp.ones((8, lines.shape[1]), bf16), lines.astype(bf16))[:1]
    mask = jnp.where(by_key == by_query, 0.0, -100.0)
    for j in range(4):
        block = where[0] ^ j
        for h in range(heads):
            strip = strips[j * heads + h]
            rows = [strip[:WIN, (WIN - 1 - r) * WIN :][:, :TOK] for r in range(WIN)]
            additive[block * heads + h] = jnp.concatenate(rows, 0) + mask


def biases(where, regions, smalls):
    heads = C // HD
    return pl.pallas_call(
        bias_kernel,
        out_shape=[
            jax.ShapeDtypeStruct((heads, TOK, TOK), f32),
            jax.ShapeDtypeStruct((4, 1, 3 * C // 4), f32),
            jax.ShapeDtypeStruct((4, 1, FF // 4), f32),
        ],
        in_specs=[SM] + [VM] * 5,
        out_specs=[VM] * 3,
        scratch_shapes=[pltpu.VMEM((heads, 16, STRIP), f32)],
        compiler_params=params(14),
        cost_estimate=cost(6),
        name="biases",
    )(where, regions, *smalls)


def head_mask(head):
    lane = lax.broadcasted_iota(jnp.int32, (TOK, C // 4), 1) // HD
    return lane == head


def only(head, field):
    return jnp.where(head_mask(head), field, jnp.zeros_like(field))


def stacked(field):
    return jnp.concatenate([only(h, field) for h in range(C // 4 // HD)], 0)


def gathered(product):
    total = jnp.zeros((TOK, C // 4), f32)
    for h in range(C // 4 // HD):
        total = jnp.where(head_mask(h), product[h * TOK : (h + 1) * TOK], total)
    return total


def by_heads(field, probs):
    parts = [dot(field[h * HD : (h + 1) * HD], probs[h]) for h in range(C // 4 // HD)]
    return jnp.concatenate(parts, 0)


def attend_kernel(plan, places, valid, own, upper, additive, bias_qkv, bias_proj, gains, offsets, qkv_down, qkv_up, proj_down, proj_up, fc1_down, *rest):
    count = len(rest) - 8 - 2
    pieces, outs, (whole, sems) = rest[:count], rest[count:-2], rest[-2:]
    mixed_out, probs_out, attended_out, low_qkv_out, low_proj_out, low_fc1_out, residual_out, normed_out = outs
    start(pieces, plan, places, whole, sems)
    wide = C // 4
    heads = wide // HD
    inputs = jnp.concatenate([own[0], upper[0]], 0).astype(f32)
    unit, _ = norm_parts(inputs)
    field = (unit * gains[0:1] + offsets[0:1]).astype(bf16)
    low_qkv = low_of(dot(field, qkv_down[...]))
    low_qkv_out[...] = low_qkv
    total = jnp.zeros((TOK, C), f32)
    low_total = jnp.zeros((TOK, LANES), f32)
    for b in range(4):
        finish(whole, sems, b)
        mixed = dot(field, whole[b, :, : 3 * wide]) + bias_qkv[b] + dot(low_qkv, qkv_up[b])
        mixed = mixed.astype(bf16)
        mixed_out[b] = mixed
        queries, keys, values = (mixed[:, i * wide : (i + 1) * wide] for i in range(3))
        scores = SCALE * dot_t(stacked(keys), queries).reshape(heads, TOK, TOK) + additive[b * heads : (b + 1) * heads]
        weight = jnp.exp(scores - jnp.max(scores, 1, keepdims=True))
        probs = weight / jnp.sum(weight, 1, keepdims=True)
        probs_out[b] = probs
        attended = by_heads(values.T, probs.astype(bf16)).astype(bf16).T
        attended_out[b] = attended
        total = total + dot_t(attended, whole[b, :, 3 * wide :])
        low_total = low_total + dot(attended, proj_down[b * wide : (b + 1) * wide, :])
    low_proj = low_of(low_total)
    low_proj_out[...] = low_proj
    residual = inputs + valid[0] * (total + bias_proj[...] + dot(low_proj, proj_up[...]))
    residual_out[...] = residual
    unit, _ = norm_parts(residual)
    normed = (unit * gains[1:2] + offsets[1:2]).astype(bf16)
    normed_out[...] = normed
    low_fc1_out[...] = low_of(dot(normed, fc1_down[...]))


def attend(group, places, valid, *args):
    heads = C // HD
    shapes = [
        ((4, TOK, 3 * C // 4), bf16),
        ((4, heads // 4, TOK, TOK), f32),
        ((4, TOK, C // 4), bf16),
        ((TOK, RANK), bf16),
        ((TOK, RANK), bf16),
        ((TOK, RANK), bf16),
        ((TOK, C), f32),
        ((TOK, C), bf16),
    ]
    return pl.pallas_call(
        lambda *refs: attend_kernel(group.plan, *refs),
        out_shape=[jax.ShapeDtypeStruct(*s) for s in shapes],
        in_specs=[SM, SM] + [VM] * len(args) + [HBM] * len(group.arrays),
        out_specs=[VM] * len(shapes),
        scratch_shapes=[pltpu.VMEM((4, C, C), bf16), pltpu.SemaphoreType.DMA((4,))],
        compiler_params=params(24),
        cost_estimate=cost(15),
        name="attend",
    )(places, valid, *args, *in_hbm(group.arrays))


def expand_kernel(plan, places, normed, low_fc1, fc1_up, bias_fc1, fc2_down, *rest):
    count = len(rest) - 3 - 2
    pieces, (hidden_out, slope_out, low_out), (whole, sems) = rest[:count], rest[count:-2], rest[-2:]
    start(pieces, plan, places, whole, sems)
    field, low_fc1 = normed[...], low_fc1[...]
    low_total = jnp.zeros((TOK, LANES), f32)
    for b in range(4):
        cols = slice(b * C, (b + 1) * C)
        finish(whole, sems, b)
        preact = dot(field, whole[b]) + bias_fc1[b] + dot(low_fc1, fc1_up[:, cols])
        cdf = 0.5 * (1.0 + lax.erf(preact * (0.5**0.5)))
        hidden = (preact * cdf).astype(bf16)
        hidden_out[b] = hidden
        slope_out[b] = cdf + preact * jnp.exp(-0.5 * preact * preact) * (0.5 / jnp.pi) ** 0.5
        low_total = low_total + dot(hidden, fc2_down[cols, :])
    low_out[...] = low_of(low_total)


def expand(group, places, *args):
    shapes = [((4, TOK, C), bf16), ((4, TOK, C), f32), ((TOK, RANK), bf16)]
    return pl.pallas_call(
        lambda *refs: expand_kernel(group.plan, *refs),
        out_shape=[jax.ShapeDtypeStruct(*s) for s in shapes],
        in_specs=[SM] + [VM] * len(args) + [HBM] * len(group.arrays),
        out_specs=[VM] * len(shapes),
        scratch_shapes=[pltpu.VMEM((4, C, C), bf16), pltpu.SemaphoreType.DMA((4,))],
        compiler_params=params(18),
        cost_estimate=cost(10),
        name="expand",
    )(places, *args, *in_hbm(group.arrays))


def contract_kernel(plan_b, plan_c, count_b, places_b, places_c, valid, own, upper, residual, hidden, slope, low_fc2, normed, low_fc1, fc2_down, fc2_up, fc1_down, fc1_up, bias_fc2, gain, *rest):
    pieces, (output_out, grad_out, pay_out), (whole_b, whole_c, sems_b, sems_c, stage, flat) = rest[:-9], rest[-9:-6], rest[-6:]
    start(pieces[count_b:], plan_c, places_c, whole_c, sems_c)
    start(pieces[:count_b], plan_b, places_b, whole_b, sems_b)
    dz = jnp.concatenate([own[1], upper[1]], 0).astype(f32)
    branch = (valid[0] * dz).astype(bf16)
    low_fc2, low_fc1, normed = low_fc2[...], low_fc1[...], normed[...]
    grad_low_fc2 = dot_t(branch, fc2_up[...]).astype(bf16)
    spread_fc2 = over_lanes(grad_low_fc2)
    grad_low_fc1 = jnp.zeros((TOK, RANK), f32)
    grad_normed = jnp.zeros((TOK, C), f32)
    total = jnp.zeros((TOK, C), f32)
    for b in range(4):
        cols = slice(b * C, (b + 1) * C)
        finish(whole_c, sems_c, b)
        total = total + dot_t(hidden[b], whole_c[b])
        grad_hidden = dot(branch, whole_c[b]) + dot_t(spread_fc2, fc2_down[cols, :])
        grad_preact = (grad_hidden * slope[b]).astype(bf16)
        flat[b * C // 8 : (b + 1) * C // 8, :] = fold(tdot(hidden[b], spread_fc2))
        grad_up = tdot(low_fc1, grad_preact)
        width = FF // 2
        at = b * C % width
        put_ranks(stage, (FF // 2 + at) // LANES, b * C // width, grad_up)
        grad_low_fc1 = grad_low_fc1 + dot_t(grad_preact, fc1_up[:, cols])
        finish(whole_b, sems_b, b)
        grad_normed = grad_normed + dot_t(grad_preact, whole_b[b])
    pack_flat(stage, 0, flat, FF // 8)
    tile = FF // LANES
    residual = residual[...]
    output_out[...] = (
        residual + valid[0] * (total + bias_fc2[...] + dot(low_fc2, fc2_up[...]))
    ).astype(bf16)
    tile = pack_ranks(stage, tile, tdot(low_fc2, branch))
    grad_low_fc1 = grad_low_fc1.astype(bf16)
    spread_fc1 = over_lanes(grad_low_fc1)
    grad_normed = grad_normed + dot_t(spread_fc1, fc1_down[...])
    unit, scale = norm_parts(residual)
    grad_out[...] = dz + norm_back(grad_normed, gain[...], unit, scale)
    flat[: C // 8, :] = fold(tdot(normed, spread_fc1))
    pack_flat(stage, tile, flat, C // 8)
    pack_out(pay_out, stage)


def contract(group_b, group_c, places_b, places_c, valid, *args):
    width = FF + C
    shapes = [((TOK, C), bf16), ((TOK, C), f32), ((OWNERS, width), bf16)]
    return pl.pallas_call(
        lambda *refs: contract_kernel(group_b.plan, group_c.plan, len(group_b.arrays), *refs),
        out_shape=[jax.ShapeDtypeStruct(*s) for s in shapes],
        in_specs=[SM] * 3 + [VM] * len(args) + [HBM] * (len(group_b.arrays) + len(group_c.arrays)),
        out_specs=[VM] * len(shapes),
        scratch_shapes=[
            pltpu.VMEM((4, C, C), bf16),
            pltpu.VMEM((4, C, C), bf16),
            pltpu.SemaphoreType.DMA((4,)),
            pltpu.SemaphoreType.DMA((4,)),
            pltpu.VMEM((width // LANES, OWNERS, LANES), f32),
            pltpu.VMEM((FF // 8, LANES), f32),
        ],
        compiler_params=params(32),
        cost_estimate=cost(14),
        name="contract",
    )(places_b, places_c, valid, *args, *in_hbm(group_b.arrays + group_c.arrays))


def back_kernel(plan, places, valid, grad_residual, mixed, probs, attended, low_proj, proj_down, proj_up, *rest):
    pieces, (grad_out, pay_out), (whole, sems, stage, flat) = rest[:-6], rest[-6:-4], rest[-4:]
    start(pieces, plan, places, whole, sems)
    wide = C // 4
    heads = wide // HD
    grad_attn = (valid[0] * grad_residual[...]).astype(bf16)
    grad_low_proj = dot_t(grad_attn, proj_up[...]).astype(bf16)
    spread_proj = over_lanes(grad_low_proj)
    for b in range(4):
        rows = slice(b * wide, (b + 1) * wide)
        finish(whole, sems, b)
        flat[b * wide // 8 : (b + 1) * wide // 8, :] = fold(tdot(attended[b], spread_proj))
        grad_heads = dot(grad_attn, whole[b, :, 3 * wide :]) + dot_t(spread_proj, proj_down[rows, :])
        grad_heads = grad_heads.astype(bf16)
        queries, keys, values = (mixed[b, :, i * wide : (i + 1) * wide] for i in range(3))
        here = probs[b]
        grad_probs = dot_t(stacked(values), grad_heads).reshape(heads, TOK, TOK)
        centre = jnp.sum(grad_probs * here, 1, keepdims=True)
        grad_scores = (here * (grad_probs - centre)).astype(bf16)
        flat_scores = grad_scores.reshape(heads * TOK, TOK)
        grad_queries = by_heads(keys.T, grad_scores).T
        grad_keys = gathered(dot(flat_scores, queries))
        grad_values = gathered(dot(here.astype(bf16).reshape(heads * TOK, TOK), grad_heads))
        grad_out[b] = jnp.concatenate([SCALE * grad_queries, SCALE * grad_keys, grad_values], 1).astype(bf16)
    tile = pack_flat(stage, 0, flat, C // 8)
    pack_ranks(stage, tile, tdot(low_proj[...], grad_attn))
    pack_out(pay_out, stage)


def back(group, places, valid, *args):
    width = 2 * C * RANK // OWNERS
    shapes = [((4, TOK, 3 * C // 4), bf16), ((OWNERS, width), bf16)]
    return pl.pallas_call(
        lambda *refs: back_kernel(group.plan, *refs),
        out_shape=[jax.ShapeDtypeStruct(*s) for s in shapes],
        in_specs=[SM] * 2 + [VM] * len(args) + [HBM] * len(group.arrays),
        out_specs=[VM] * len(shapes),
        scratch_shapes=[
            pltpu.VMEM((4, C, C), bf16),
            pltpu.SemaphoreType.DMA((4,)),
            pltpu.VMEM((width // LANES, OWNERS, LANES), f32),
            pltpu.VMEM((C // 8, LANES), f32),
        ],
        compiler_params=params(24),
        cost_estimate=cost(14),
        name="back",
    )(places, valid, *args, *in_hbm(group.arrays))


def last_kernel(plan, places, grad_residual, own, upper, gain, offset, grad_mixed, low_qkv, qkv_down, qkv_up, *rest):
    pieces, (grad_out, pay_out), (whole, sems, stage, flat, ranks) = rest[:-7], rest[-7:-5], rest[-5:]
    start(pieces, plan, places, whole, sems)
    wide = C // 4
    unit, scale = norm_parts(jnp.concatenate([own[0], upper[0]], 0).astype(f32))
    shifted = (unit * gain[...] + offset[...]).astype(bf16)
    low_qkv = low_qkv[...]
    grad_shifted = jnp.zeros((TOK, C), f32)
    grad_low_qkv = jnp.zeros((TOK, RANK), f32)
    for b in range(4):
        grad = grad_mixed[b]
        grad_up = tdot(low_qkv, grad)
        for i in range(3):
            ranks[:, i * C + b * wide : i * C + (b + 1) * wide] = grad_up[:, i * wide : (i + 1) * wide]
        grad_low_qkv = grad_low_qkv + dot_t(grad, qkv_up[b])
    for b in range(4):
        finish(whole, sems, b)
        grad_shifted = grad_shifted + dot_t(grad_mixed[b], whole[b, :, : 3 * wide])
    spread_qkv = over_lanes(grad_low_qkv.astype(bf16))
    grad_shifted = grad_shifted + dot_t(spread_qkv, qkv_down[...])
    grad_out[...] = (
        grad_residual[...] + norm_back(grad_shifted, gain[...], unit, scale)
    ).astype(bf16)
    tile = pack_ranks(stage, 0, ranks[...])
    flat[...] = fold(tdot(shifted, spread_qkv))
    pack_flat(stage, tile, flat, C // 8)
    pack_out(pay_out, stage)


def last(group, places, *args):
    width = 4 * C * RANK // OWNERS
    shapes = [((TOK, C), bf16), ((OWNERS, width), bf16)]
    return pl.pallas_call(
        lambda *refs: last_kernel(group.plan, *refs),
        out_shape=[jax.ShapeDtypeStruct(*s) for s in shapes],
        in_specs=[SM] + [VM] * len(args) + [HBM] * len(group.arrays),
        out_specs=[VM] * len(shapes),
        scratch_shapes=[
            pltpu.VMEM((4, C, C), bf16),
            pltpu.SemaphoreType.DMA((4,)),
            pltpu.VMEM((width // LANES, OWNERS, LANES), f32),
            pltpu.VMEM((C // 8, LANES), f32),
            pltpu.VMEM((RANK, 3 * C), f32),
        ],
        compiler_params=params(20),
        cost_estimate=cost(8),
        name="last",
    )(places, *args, *in_hbm(group.arrays))


def per_device(
    tokens,
    cotangent,
    adapter_id,
    valid_flag,
    regions,
    w_qkv,
    b_qkv,
    rel_table,
    w_proj,
    b_proj,
    w_fc1,
    b_fc1,
    w_fc2,
    b_fc2,
    norm_gains,
    norm_shifts,
    down_main,
    down_fc2,
    up_qkv,
    up_fc1,
    up_out,
):
    z, c, t = (lax.axis_index(name) for name in ("img", "ctx", "tp"))
    z_count, t_count = lax.axis_size("img"), lax.axis_size("tp")
    images, height, breadth = tokens.shape[:3]
    across = breadth // WIN
    image, column = t // across, t % across
    heads_here = rel_table.shape[1]
    heads = heads_here * t_count
    wide = heads_here * HD
    ff_here = w_fc1.shape[1]

    where = jnp.stack([image, column]).astype(jnp.int32)
    place_at = jnp.stack([t, column]).astype(jnp.int32)

    own, away = cut_windows(where, tokens, cotangent)
    upper = swap_ctx(away)

    def half(v):
        rows = v.shape[0] // 2
        return lax.dynamic_slice_in_dim(v, c * rows, rows, 0)

    own_a = jnp.concatenate([w_qkv.reshape(-1, 3 * wide), w_proj.T], 1)
    own_b = w_fc1
    own_c = w_fc2.T
    if z_count <= 8:
        group_a = spread_first(own_a, half(own_a))
        group_b = spread_last(own_b, half(own_b), swap_x, swap_y, 1, 2)
        group_c = spread_last(own_c, half(own_c), swap_y, swap_x, 2, 1)
    else:
        group_a, group_b, group_c = (spread_far(v) for v in (own_a, own_b, own_c))
    places_a, places_b, places_c = (group.table() for group in (group_a, group_b, group_c))

    if z_count <= 8:
        held = [adapter_id]
        for k in range(1, z_count):
            held.append(lax.ppermute(adapter_id, "img", [(i, (i - k) % z_count) for i in range(z_count)]))
        ahead = jnp.stack(held)
        wanted = lax.dynamic_index_in_dim(ahead, image, 1, False)
        chosen = choose(
            wanted, down_main.transpose(1, 0, 2), down_fc2, up_qkv, up_fc1, up_out.transpose(1, 0, 2)
        )
        held = [chosen[0]]
        for k in range(1, z_count):
            held.append(lax.ppermute(chosen[k], "img", [(i, (i + k) % z_count) for i in range(z_count)]))
        mine = jnp.stack(held)
        theirs = swap_ctx(mine)
        shards = jnp.stack([((z - k) % z_count) * 2 + (c ^ o) for k in range(z_count) for o in (0, 1)])
        ids = jnp.roll(ahead, z, 0)
    else:
        ids = lax.all_gather(adapter_id, "img")
        parts = [down_main[:, i] for i in range(3)] + [down_fc2, up_qkv, up_fc1] + [up_out[:, i] for i in range(2)]
        tables = jnp.concatenate(parts, 1)
        wanted = lax.dynamic_index_in_dim(ids, image, 1, False)
        pick = (wanted[:, None] == jnp.arange(ADAPT)[None, :]).astype(bf16)
        mine = lax.all_to_all(dot(pick, tables).astype(bf16), "img", 0, 0, tiled=True)
        theirs = swap_ctx(mine)
        mine, theirs = jnp.where(c == 0, mine, theirs), jnp.where(c == 0, theirs, mine)
        owned = jnp.stack([mine, theirs], 1).reshape(2 * z_count, -1)
        sizes = [v.shape[1] for v in parts]
        cuts = [sum(sizes[:i]) for i in range(9)]
        owned = jnp.concatenate([owned[:, a:b].reshape(SHARDS, -1) for a, b in zip(cuts, cuts[1:])], 1)
        owned = owned.reshape(SHARDS // 2, 2, TILES, LANES)
        mine, theirs = owned[:, 0], owned[:, 1]
        shards = jnp.arange(SHARDS)
    qkv_down, proj_down, fc1_down, fc2_down, qkv_up, fc1_up, proj_up, fc2_up = prepare_adapters(
        shards.astype(jnp.int32), mine, theirs
    )

    def rows_of(field, rows):
        return jnp.pad(field, ((0, rows - field.shape[0]), (0, C - field.shape[1])))

    small = jnp.concatenate([rows_of(b_qkv, 3), b_fc1[None], jnp.zeros((4, C), bf16), rows_of(rel_table.T, 8)], 0)
    by_x = swap_x(small)
    additive, bias_qkv, bias_fc1 = biases(place_at, regions, [small, by_x, swap_y(small), swap_y(by_x)])
    valid = lax.dynamic_index_in_dim(valid_flag, image, 0, False).astype(f32).reshape(1)
    gains = norm_gains.astype(f32)
    shifts = norm_shifts.astype(f32)

    mixed, probs, attended, low_qkv, low_proj, low_fc1, residual, normed2 = attend(
        group_a, places_a, valid, own, upper, additive, bias_qkv, b_proj.astype(f32)[None],
        gains, shifts, qkv_down, qkv_up, proj_down, proj_up, fc1_down,
    )
    hidden, slope, low_fc2 = expand(group_b, places_b, normed2, low_fc1, fc1_up, bias_fc1, fc2_down)
    output, grad_residual, pay_one = contract(
        group_b, group_c, places_b, places_c, valid, own, upper, residual, hidden, slope,
        low_fc2, normed2, low_fc1, fc2_down, fc2_up, fc1_down, fc1_up, b_fc2.astype(f32)[None], gains[1:],
    )
    grad_mixed, pay_two = back(
        group_a, places_a, valid, grad_residual, mixed, probs, attended, low_proj, proj_down, proj_up
    )

    def placed(field, dtype):
        half = jnp.concatenate([swap_ctx(field[TOK // 2 :]), field[: TOK // 2]], 0)
        pieces = [half, swap_x(half), swap_y(half), swap_xy(half)]
        return place(place_at, pieces, dtype).reshape(images, height, breadth, C)

    output = placed(output, bf16)

    count = 2 * z_count * t_count
    source = jnp.broadcast_to(ids[:, None, :, None], (z_count, 2, images, across)).reshape(-1)
    pick = (jnp.arange(ADAPT)[:, None] == source[None, :]).astype(bf16)

    def summed(pay, widths):
        cuts = [sum(widths[:i]) for i in range(len(widths) + 1)]
        if count != OWNERS:
            pay = jnp.concatenate(
                [pay[:, a:b].reshape(count, -1) for a, b in zip(cuts, cuts[1:])], 1
            )
            cuts = [v * OWNERS // count for v in cuts]
        sums = dot(pick, lax.all_to_all(pay, ("img", "ctx", "tp"), 0, 0, tiled=True))
        return [sums[:, a:b] for a, b in zip(cuts, cuts[1:])]

    one = C * RANK // OWNERS
    grad_fc2, grad_fc1, grad_fc2_up, grad_fc1_down = summed(pay_one, [4 * one, 4 * one, one, one])
    grad_mixed, output, grad_fc2, grad_fc1, grad_fc2_up, grad_fc1_down = lax.optimization_barrier(
        (grad_mixed, output, grad_fc2, grad_fc1, grad_fc2_up, grad_fc1_down)
    )
    grad_tokens, pay_three = last(
        group_a, places_a, grad_residual, own, upper, gains[:1], shifts[:1], grad_mixed, low_qkv, qkv_down, qkv_up
    )
    grad_proj_down, grad_proj_up = summed(pay_two, [one, one])
    grad_qkv, grad_qkv_down = summed(pay_three, [3 * one, one])
    grad_tokens = placed(grad_tokens, f32)
    return (
        output,
        grad_tokens,
        jnp.stack([grad_qkv_down, grad_proj_down, grad_fc1_down], 1),
        grad_fc2,
        grad_qkv,
        grad_fc1,
        jnp.stack([grad_proj_up, grad_fc2_up], 1),
    )


def solution(mesh):
    in_specs = (
        P("img", "ctx", None, None),
        P("img", "ctx", None, None),
        P("img"),
        P("img"),
        P("ctx", None),
        P("img", None, "tp"),
        P(None, "tp"),
        P(None, "tp"),
        P("tp", "img"),
        P(),
        P("img", "tp"),
        P("tp"),
        P("tp", "img"),
        P(),
        P(),
        P(),
        P(None, None, ("img", "ctx")),
        P(None, ("img", "ctx")),
        P(None, ("img", "ctx")),
        P(None, ("img", "ctx")),
        P(None, None, ("img", "ctx")),
    )
    out_specs = (
        P("img", "ctx", None, None),
        P("img", "ctx", None, None),
        P(None, None, ("img", "ctx", "tp")),
        P(None, ("img", "ctx", "tp")),
        P(None, ("img", "ctx", "tp")),
        P(None, ("img", "ctx", "tp")),
        P(None, None, ("img", "ctx", "tp")),
    )
    return jax.shard_map(
        per_device, mesh=mesh, in_specs=in_specs, out_specs=out_specs, check_vma=False
    )
```

```python
import jax
import jax.numpy as jnp
from jax import lax
from jax.experimental import pallas as pl
from jax.experimental.pallas import tpu as pltpu
from jax.sharding import PartitionSpec as P

C = 768
HD = 32
FF = 3072
WIN = 12
SHIFT = 6
RANK = 16
ADAPT = 8
RELS = 529
TOK = WIN * WIN
SCALE = HD ** (-0.5)
EPS = 1e-05
LANES = 128
SHARDS = 8
OWNERS = 32

bf16 = jnp.bfloat16
f32 = jnp.float32

VM = pl.BlockSpec(memory_space=pltpu.VMEM)
SM = pl.BlockSpec(memory_space=pltpu.SMEM)
HBM = pl.BlockSpec(memory_space=pltpu.HBM)


def params(mib):
    return pltpu.CompilerParams(vmem_limit_bytes=mib << 20)


def in_hbm(arrays):
    return [pltpu.with_memory_space_constraint(v, pltpu.HBM) for v in arrays]


def in_hbm_out(shape, dtype):
    return pltpu.HBM(shape, dtype)


def here():
    z, c, t = (lax.axis_index(name) for name in ("img", "ctx", "tp"))
    return z, c, t, lax.div(t, 2), lax.rem(t, 2)


def cost(us):
    return pl.CostEstimate(flops=0, transcendentals=0, bytes_accessed=int(us * 3e6))


def dot(left, right):
    return jnp.dot(left, right, preferred_element_type=f32)


def dot_t(left, right):
    return lax.dot_general(left, right, (((1,), (1,)), ((), ())), preferred_element_type=f32)


def tdot(left, right):
    return lax.dot_general(left, right, (((0,), (0,)), ((), ())), preferred_element_type=f32)


def swap_ctx(v):
    return lax.ppermute(v, "ctx", [(0, 1), (1, 0)])


def swap_x(v):
    return lax.ppermute(v, "tp", [(0, 1), (1, 0), (2, 3), (3, 2)])


def swap_y(v):
    return lax.ppermute(v, "tp", [(0, 2), (2, 0), (1, 3), (3, 1)])


def swap_xy(v):
    return lax.ppermute(v, "tp", [(0, 3), (3, 0), (1, 2), (2, 1)])


def after(v, *others):
    return lax.optimization_barrier((v,) + others)[0]


def shift_img(v, k):
    count = lax.axis_size("img")
    return lax.ppermute(v, "img", [(i, (i + k) % count) for i in range(count)])


class Group:
    def __init__(self, own):
        self.arrays, self.plan, self.places = [own], [(0, 0, own.shape[0])], [(0, 0, None, 0)]

    def add(self, array, parts, other=None):
        for core, held in ((0, array), (1, swap_ctx(array) if other is None else other)):
            for at, rows, k, j, first in parts:
                self.plan.append((len(self.arrays), at, rows))
                self.places.append((k, j, core, first))
            self.arrays.append(held)


HALF = 96


def pair(k, one, two, at=0):
    return [(at, HALF, k, one, 0), (at + HALF, HALF, k, two, 0)]


def spread_far(own):
    whole = lax.all_gather(own, "img", axis=0, tiled=True)
    group = Group(whole)
    by_x = swap_x(whole)
    group.arrays += [by_x, swap_y(whole), swap_y(by_x)]
    group.plan += [(n, 0, C) for n in (1, 2, 3)]
    group.places = [(None, j, None, 0) for j in range(4)]
    return group


def norm_parts(field):
    average = jnp.mean(field, -1, keepdims=True)
    centred = field - average
    variance = jnp.mean(centred * centred, -1, keepdims=True)
    scale = lax.rsqrt(variance + EPS)
    return centred * scale, scale


def norm_back(grad, gain, unit, scale):
    scaled = grad * gain
    return scale * (
        scaled
        - jnp.mean(scaled, -1, keepdims=True)
        - unit * jnp.mean(scaled * unit, -1, keepdims=True)
    )


def start(group_refs, group, whole, sems):
    z, c, t, _, _ = here()
    count = lax.axis_size("img")
    rows_each = C // count
    for (index, at, rows), (k, j, core, first) in zip(group.plan, group.places):
        source = group_refs[index].at[pl.ds(at, rows), :]
        top = 0 if k is None else lax.rem(z + (count - k), count) * rows_each + first
        if core is not None:
            top = top + (c ^ core) * (rows_each // 2)
        block = t ^ j
        target = whole.at[block, pl.ds(pl.multiple_of(top, 16), rows), :]
        pltpu.make_async_copy(source, target, sems.at[block]).start()


def finish(whole, sems, block):
    pltpu.make_async_copy(whole.at[block], whole.at[block], sems.at[block]).wait()


def lane_group(rows):
    lane = lax.broadcasted_iota(jnp.int32, (rows, LANES), 1) // RANK
    row = lax.broadcasted_iota(jnp.int32, (rows, LANES), 0) % 8
    return (lane == row).astype(f32)


def low_of(spread_sum):
    for step in (64, 32, 16):
        spread_sum = spread_sum + pltpu.roll(spread_sum, step, 1)
    return spread_sum[:, :RANK].astype(bf16)


def over_lanes(low):
    lane = lax.broadcasted_iota(jnp.int32, (RANK, LANES), 1) % RANK
    rank = lax.broadcasted_iota(jnp.int32, (RANK, LANES), 0)
    return dot(low, (lane == rank).astype(bf16)).astype(bf16)


def fold(product):
    rows = product.shape[0]
    kept = (product * lane_group(rows)).reshape(rows // 8, 8, LANES)
    return jnp.sum(kept, 1)


def put_ranks(stage, tile, h, grad):
    for k in range(grad.shape[1] // LANES):
        stage[tile + k, pl.ds(h, RANK, stride=2), :] = grad[:, k * LANES : (k + 1) * LANES]


def pack_ranks(stage, tile, grad):
    width = grad.shape[1] // 2
    for h in range(2):
        put_ranks(stage, tile, h, grad[:, h * width : (h + 1) * width])
    return tile + width // LANES


def pack_flat(stage, tile, flat, rows):
    each = rows // OWNERS
    for k in range(each):
        stage[tile + k] = flat[pl.ds(k, OWNERS, stride=each), :]
    return tile + each


def begin_kernel(ids, tokens, cotangent, w_qkv, w_proj, w_fc1, w_fc2, b_qkv, b_fc1, rel, own_a, piece_a, pack_x, pack_y, own, away, ids_here, image, held_qkv, held_proj, held_fc1, held_fc2, held_bq, held_b1, held_rel, small, sems):
    _, c, _, at, column = here()
    half = pl.ds(pl.multiple_of(c * HALF, 16), HALF)
    moves = (
        (w_qkv, held_qkv),
        (w_proj, held_proj),
        (b_qkv, held_bq),
        (b_fc1, held_b1),
        (rel, held_rel),
        (ids, ids_here),
        (w_fc1.at[half, :], held_fc1),
        (w_fc2.at[half, :], held_fc2),
        (tokens.at[at], image.at[0]),
        (cotangent.at[at], image.at[1]),
    )
    copies = [pltpu.make_async_copy(*move, sems.at[i]) for i, move in enumerate(moves)]
    for copy in copies:
        copy.start()
    for copy in copies[:8]:
        copy.wait()
    own_a[...] = jnp.concatenate([held_qkv[0], held_qkv[1], held_qkv[2], held_proj[...].T], 1)
    mine = own_a[half, :]
    lane = lax.broadcasted_iota(jnp.int32, (1, C), 1)
    small[...] = jnp.zeros_like(small)
    small[:3, : b_qkv.shape[1]] = held_bq[...].astype(f32)
    small[3:4, :] = held_b1[...].astype(f32).reshape(1, C)
    first, second = ids_here[0].astype(f32), ids_here[1].astype(f32)
    small[4:5, :] = jnp.where(lane == 0, first, jnp.where(lane == 1, second, 0.0))
    small[8 : 8 + rel.shape[0], : rel.shape[1]] = held_rel[...].astype(f32)
    for target in (piece_a, pack_x, pack_y):
        target[:HALF] = mine
        target[HALF : HALF + 16] = small[...].astype(bf16)
    pack_x[HALF + 16 :] = held_fc1[...]
    pack_y[HALF + 16 :] = held_fc2[...]
    for i, copy in enumerate(copies[8:]):
        copy.wait()
        block = image[i].astype(f32)
        rows = []
        for r in range(WIN):
            at = r * 2 * WIN
            inner = block[at + SHIFT : at + SHIFT + WIN]
            outer = jnp.concatenate([block[at + SHIFT + WIN : at + 2 * WIN], block[at : at + SHIFT]], 0)
            rows.append(jnp.where(column == 0, inner, outer))
        away[i] = jnp.concatenate(rows[:SHIFT], 0).astype(bf16)
        own[i] = jnp.concatenate(rows[SHIFT:], 0).astype(bf16)


def begin(ids, tokens, cotangent, *args):
    flat = (tokens.shape[0], -1, C)
    windows = (2, TOK // 2, C)
    pack = (2 * HALF + 16, C)
    shapes = [(2 * HALF, C), (HALF + 16, C), pack, pack, windows, windows]
    makers = [in_hbm_out, jax.ShapeDtypeStruct, jax.ShapeDtypeStruct, jax.ShapeDtypeStruct, in_hbm_out, jax.ShapeDtypeStruct]
    w_qkv, w_proj, w_fc1, w_fc2, b_qkv, b_fc1, rel = (v.shape for v in args)
    held = [w_qkv, w_proj, (HALF, C), (HALF, C), b_qkv, b_fc1, rel]
    return pl.pallas_call(
        begin_kernel,
        out_shape=[make(v, bf16) for make, v in zip(makers, shapes)],
        in_specs=[HBM] * (3 + len(args)),
        out_specs=[VM] * len(shapes),
        scratch_shapes=[pltpu.SMEM((2,), jnp.int32), pltpu.VMEM((2, 2 * TOK, C), bf16)]
        + [pltpu.VMEM(v, bf16) for v in held]
        + [pltpu.VMEM((16, C), f32), pltpu.SemaphoreType.DMA((10,))],
        compiler_params=params(10),
        cost_estimate=cost(2),
        name="begin",
    )(*in_hbm([ids, tokens.reshape(flat), cotangent.reshape(flat), *args]))


def place_kernel(*refs):
    pieces, out, held = refs[:4], refs[4], refs[5]
    t = here()[2]
    for j, piece in enumerate(pieces):
        held[t ^ j] = piece[...].astype(f32)
    for i in range(2):
        left, right = held[2 * i], held[2 * i + 1]
        for r in range(WIN):
            rows = slice(r * WIN, (r + 1) * WIN)
            inner, outer = left[rows], right[rows]
            line = jnp.concatenate([outer[SHIFT:], inner, outer[:SHIFT]], 0)
            out[i, r * 2 * WIN : (r + 1) * 2 * WIN] = line.astype(out.dtype)


def place(pieces, dtype):
    return pl.pallas_call(
        place_kernel,
        out_shape=jax.ShapeDtypeStruct((2, 2 * TOK, C), dtype),
        in_specs=[VM] * 4,
        out_specs=VM,
        scratch_shapes=[pltpu.VMEM((4, TOK, C), f32)],
        compiler_params=params(8),
        cost_estimate=cost(2),
        name="place",
    )(*pieces)


TILES = 12 * RANK


def choose_kernel(*refs):
    held, tables, (chosen_out, pick), (table, rows, stage, sems) = refs[:4], refs[4:9], refs[9:11], refs[11:]
    z, _, _, image, _ = here()
    copies = [
        pltpu.make_async_copy(v.at[pl.ds(HALF, 16), :], rows.at[n], sems.at[n]) for n, v in enumerate(held)
    ]
    col = 0
    for field in tables:
        for i in range(1 if len(field.shape) == 2 else field.shape[0]):
            source = field if len(field.shape) == 2 else field.at[i]
            width = source.shape[1]
            copies.append(pltpu.make_async_copy(source, table.at[:, pl.ds(col, width)], sems.at[len(copies)]))
            col += width
    for copy in copies:
        copy.start()
    for copy in copies[:4]:
        copy.wait()
    source = lax.broadcasted_iota(jnp.int32, pick.shape, 1)
    owner = jnp.zeros(pick.shape, f32)
    wanted = []
    for k in range(4):
        known = rows[-k % 4].astype(f32)[4:5]
        lane = lax.broadcasted_iota(jnp.int32, known.shape, 1)
        ids = [jnp.sum(jnp.where(lane == i, known, 0.0), 1, keepdims=True) for i in range(2)]
        at = lax.rem(z + k, 4)
        owner = jnp.where(source // 8 == at, jnp.where(source % 4 < 2, ids[0], ids[1]), owner)
        wanted.append(jnp.where(image == 0, ids[0], ids[1]))
    pick[...] = (lax.broadcasted_iota(jnp.int32, pick.shape, 0).astype(f32) == owner).astype(bf16)
    for copy in copies[4:]:
        copy.wait()
    for tile in range(TILES):
        field = table[:, tile * LANES : (tile + 1) * LANES].astype(f32)
        row = lax.broadcasted_iota(jnp.int32, field.shape, 0).astype(f32)
        for k in range(4):
            chosen = jnp.sum(jnp.where(row == wanted[k], field, 0.0), 0, keepdims=True)
            stage[k, tile : tile + 1, :] = chosen
    for k in range(4):
        at = lax.rem(z + k, 4)
        for i in range(C // LANES):
            chosen_out[at, :, i * LANES : (i + 1) * LANES] = stage[k, i * 32 : (i + 1) * 32, :].astype(bf16)


def choose(held, *tables):
    return pl.pallas_call(
        choose_kernel,
        out_shape=[jax.ShapeDtypeStruct((4, 32, C), bf16), in_hbm_out((ADAPT, OWNERS), bf16)],
        in_specs=[HBM] * 9,
        out_specs=[VM] * 2,
        scratch_shapes=[
            pltpu.VMEM((ADAPT, TILES * LANES), bf16),
            pltpu.VMEM((4, 16, C), bf16),
            pltpu.VMEM((4, TILES, LANES), f32),
            pltpu.SemaphoreType.DMA((12,)),
        ],
        compiler_params=params(4),
        cost_estimate=cost(3),
        name="choose",
    )(*in_hbm([*held, *tables]))


def adapters_kernel(mine, theirs, qkv_down, proj_down, fc1_down, fc2_down, qkv_up, fc1_up, proj_up, fc2_up, ranks):
    c = here()[1]
    for n in range(SHARDS):
        shard = n // 2 * 2 + (c ^ (n % 2))
        rows = (mine, theirs)[n % 2][n // 2].astype(f32)
        tiles = jnp.concatenate([rows[:, i * LANES : (i + 1) * LANES] for i in range(C // LANES)], 0)
        row = 0
        for out in (qkv_down, proj_down, fc1_down, fc2_down):
            rows = out.shape[1]
            part = tiles[row : row + rows // 8]
            spread = jnp.broadcast_to(part[:, None, :], (rows // 8, 8, LANES)).reshape(rows, LANES)
            out[shard] = (spread * lane_group(rows)).astype(bf16)
            row += rows // 8
        tile = 0
        for width in (3 * C, FF, C, C):
            for e in range(2):
                for k in range(width // LANES):
                    ranks[tile + k, pl.ds(2 * shard + e, 1), :] = tiles[row : row + 1]
                    row += 1
            tile += width // LANES
    wide = C // 4
    tile = 3 * C // LANES
    table = jnp.concatenate([ranks[k] for k in range(tile)], 1)
    for b in range(4):
        parts = [table[:, i * C + b * wide : i * C + (b + 1) * wide] for i in range(3)]
        qkv_up[b] = jnp.concatenate(parts, 1).astype(bf16)
    for out in (fc1_up, proj_up, fc2_up):
        for k in range(out.shape[1] // LANES):
            out[:, k * LANES : (k + 1) * LANES] = ranks[tile + k].astype(bf16)
        tile += out.shape[1] // LANES


def prepare_adapters(mine, theirs):
    downs = [(SHARDS, C // SHARDS, LANES)] * 3 + [(SHARDS, FF // SHARDS, LANES)]
    ups = [(4, RANK, 3 * C // 4), (RANK, FF), (RANK, C), (RANK, C)]
    tiles = (3 * C + FF + 2 * C) // LANES
    made = pl.pallas_call(
        adapters_kernel,
        out_shape=[in_hbm_out(v, bf16) for v in downs + ups],
        in_specs=[VM, VM],
        out_specs=[VM] * 8,
        scratch_shapes=[pltpu.VMEM((tiles, RANK, LANES), f32)],
        compiler_params=params(6),
        cost_estimate=cost(2),
        name="adapters",
    )(mine, theirs)
    return [v.reshape(-1, LANES) for v in made[:4]] + list(made[4:])


SPAN = 2 * WIN - 1
STRIP = 3 * LANES


def bias_kernel(regions, *refs):
    smalls, (additive, bias_qkv, bias_fc1, strips, held, sems) = refs[:4], refs[4:]
    _, _, t, _, column = here()
    copies = [
        pltpu.make_async_copy(v.at[pl.ds(v.shape[0] - 16 if v.shape[0] < 2 * HALF else HALF, 16), :], held.at[n], sems.at[n])
        for n, v in enumerate(smalls)
    ]
    for copy in copies:
        copy.start()
    wide = C // 4
    heads = wide // HD
    lane = lax.broadcasted_iota(jnp.int32, (C, STRIP), 1)
    entry = lax.broadcasted_iota(jnp.int32, (C, STRIP), 0) - (lane // WIN) * SPAN - lane % WIN - WIN + 1
    for copy in copies:
        copy.wait()
    tables = []
    for j in range(4):
        field = held[j].astype(f32)
        block = t ^ j
        bias_qkv[block] = jnp.concatenate([field[i : i + 1, :wide] for i in range(3)], 1)
        bias_fc1[block] = field[3:4]
        tables.append(field[8:].astype(bf16))
    table = jnp.concatenate(tables, 0)
    for key in range(WIN):
        strip = dot(table, (entry == -key).astype(bf16))
        for j in range(4):
            for h in range(heads):
                strips[j * heads + h, key : key + 1, :] = strip[8 * j + h : 8 * j + h + 1]
    row = lax.broadcasted_iota(jnp.int32, (TOK, WIN), 0) // WIN
    at_row = (row == lax.broadcasted_iota(jnp.int32, (TOK, WIN), 1)).astype(bf16)
    lines = dot(at_row, regions[...].astype(f32).astype(bf16))
    cell = lax.broadcasted_iota(jnp.int32, lines.shape, 0) % WIN + column * WIN
    lines = jnp.where(cell == lax.broadcasted_iota(jnp.int32, lines.shape, 1), lines, 0.0)
    by_key = jnp.sum(lines, 1, keepdims=True)
    by_query = dot_t(jnp.ones((8, lines.shape[1]), bf16), lines.astype(bf16))[:1]
    mask = jnp.where(by_key == by_query, 0.0, -100.0)
    for j in range(4):
        block = t ^ j
        for h in range(heads):
            strip = strips[j * heads + h]
            rows = [strip[:WIN, (WIN - 1 - r) * WIN :][:, :TOK] for r in range(WIN)]
            additive[block * heads + h] = jnp.concatenate(rows, 0) + mask


def biases(regions, smalls):
    heads = C // HD
    return pl.pallas_call(
        bias_kernel,
        out_shape=[
            jax.ShapeDtypeStruct((heads, TOK, TOK), f32),
            jax.ShapeDtypeStruct((4, 1, 3 * C // 4), f32),
            in_hbm_out((4, 1, FF // 4), f32),
        ],
        in_specs=[VM] + [HBM] * 4,
        out_specs=[VM] * 3,
        scratch_shapes=[
            pltpu.VMEM((heads, 16, STRIP), f32),
            pltpu.VMEM((4, 16, C), bf16),
            pltpu.SemaphoreType.DMA((4,)),
        ],
        compiler_params=params(8),
        cost_estimate=cost(6),
        name="biases",
    )(*in_hbm([regions, *smalls]))


def head_mask(head):
    lane = lax.broadcasted_iota(jnp.int32, (TOK, C // 4), 1) // HD
    return lane == head


def only(head, field):
    return jnp.where(head_mask(head), field, jnp.zeros_like(field))


def stacked(field):
    return jnp.concatenate([only(h, field) for h in range(C // 4 // HD)], 0)


def gathered(product):
    total = jnp.zeros((TOK, C // 4), f32)
    for h in range(C // 4 // HD):
        total = jnp.where(head_mask(h), product[h * TOK : (h + 1) * TOK], total)
    return total


def by_heads(field, probs):
    parts = [dot(field[h * HD : (h + 1) * HD], probs[h]) for h in range(C // 4 // HD)]
    return jnp.concatenate(parts, 0)


def row_of(ref, held, sem):
    copy = pltpu.make_async_copy(ref, held, sem)
    copy.start()
    return copy


def attend_kernel(group, valid, bias_proj, own, upper, gains, offsets, additive, bias_qkv, qkv_down, qkv_up, proj_down, proj_up, fc1_down, *rest):
    pieces, rest = rest[: len(group.arrays)], rest[len(group.arrays) :]
    mixed_out, probs_out, attended_out, low_qkv_out, low_proj_out, low_fc1_out, residual_out, normed_out = rest[:8]
    whole, sems, valid_here, bias_here, mixed_held, probs_held, attended_held, more = rest[8:]
    firsts = [row_of(valid, valid_here, more.at[0]), row_of(bias_proj, bias_here, more.at[1])]
    start(pieces, group, whole, sems)
    image = here()[3]
    wide = C // 4
    heads = wide // HD
    inputs = jnp.concatenate([own[0], upper[0]], 0).astype(f32)
    unit, _ = norm_parts(inputs)
    field = (unit * gains[0:1].astype(f32) + offsets[0:1].astype(f32)).astype(bf16)
    low_qkv = low_of(dot(field, qkv_down[...]))
    low_qkv_out[...] = low_qkv
    total = jnp.zeros((TOK, C), f32)
    low_total = jnp.zeros((TOK, LANES), f32)
    kept = []
    for b in range(4):
        finish(whole, sems, b)
        mixed = dot(field, whole[b, :, : 3 * wide]) + bias_qkv[b] + dot(low_qkv, qkv_up[b])
        mixed = mixed.astype(bf16)
        mixed_held[b] = mixed
        queries, keys, values = (mixed[:, i * wide : (i + 1) * wide] for i in range(3))
        scores = SCALE * dot_t(stacked(keys), queries).reshape(heads, TOK, TOK) + additive[b * heads : (b + 1) * heads]
        weight = jnp.exp(scores - jnp.max(scores, 1, keepdims=True))
        probs = weight / jnp.sum(weight, 1, keepdims=True)
        probs_held[b] = probs
        attended = by_heads(values.T, probs.astype(bf16)).astype(bf16).T
        attended_held[b] = attended
        for i, (source, target) in enumerate(
            ((mixed_held, mixed_out), (probs_held, probs_out), (attended_held, attended_out))
        ):
            kept.append(row_of(source.at[b], target.at[b], more.at[2 + 3 * b + i]))
        total = total + dot_t(attended, whole[b, :, 3 * wide :])
        low_total = low_total + dot(attended, proj_down[b * wide : (b + 1) * wide, :])
    low_proj = low_of(low_total)
    low_proj_out[...] = low_proj
    for copy in firsts:
        copy.wait()
    branch = total + bias_here[...].astype(f32).reshape(1, C) + dot(low_proj, proj_up[...])
    residual = inputs + valid_here[image].astype(f32) * branch
    residual_out[...] = residual
    unit, _ = norm_parts(residual)
    normed = (unit * gains[1:2].astype(f32) + offsets[1:2].astype(f32)).astype(bf16)
    normed_out[...] = normed
    low_fc1_out[...] = low_of(dot(normed, fc1_down[...]))
    for copy in kept:
        copy.wait()


def attend(group, valid, bias_proj, own, upper, gains, offsets, additive, bias_qkv, *adapters):
    wide = C // 4
    heads = wide // HD
    mixed, probs, attended = (4, TOK, 3 * wide), (4, heads, TOK, TOK), (4, TOK, wide)
    return pl.pallas_call(
        lambda *refs: attend_kernel(group, *refs),
        out_shape=[
            in_hbm_out(mixed, bf16),
            in_hbm_out(probs, f32),
            in_hbm_out(attended, bf16),
            in_hbm_out((TOK, RANK), bf16),
            in_hbm_out((TOK, RANK), bf16),
            jax.ShapeDtypeStruct((TOK, RANK), bf16),
            jax.ShapeDtypeStruct((TOK, C), f32),
            jax.ShapeDtypeStruct((TOK, C), bf16),
        ],
        in_specs=[HBM] * 2 + [VM] * (6 + len(adapters)) + [HBM] * len(group.arrays),
        out_specs=[HBM] * 3 + [VM] * 5,
        scratch_shapes=[
            pltpu.VMEM((4, C, C), bf16),
            pltpu.SemaphoreType.DMA((4,)),
            pltpu.SMEM((2,), jnp.int32),
            pltpu.VMEM((C,), bf16),
            pltpu.VMEM(mixed, bf16),
            pltpu.VMEM(probs, f32),
            pltpu.VMEM(attended, bf16),
            pltpu.SemaphoreType.DMA((14,)),
        ],
        compiler_params=params(24),
        cost_estimate=cost(10),
        name="attend",
    )(*in_hbm([valid, bias_proj, own, upper, gains, offsets]), additive, bias_qkv, *in_hbm(adapters), *in_hbm(group.arrays))


def expand_kernel(group, normed, low_fc1, fc1_up, bias_fc1, fc2_down, *rest):
    count = len(group.arrays)
    pieces, (hidden_out, slope_out, low_out), (whole, sems) = rest[:count], rest[count:-2], rest[-2:]
    start(pieces, group, whole, sems)
    field, low_fc1 = normed[...], low_fc1[...]
    low_total = jnp.zeros((TOK, LANES), f32)
    for b in range(4):
        cols = slice(b * C, (b + 1) * C)
        finish(whole, sems, b)
        preact = dot(field, whole[b]) + bias_fc1[b] + dot(low_fc1, fc1_up[:, cols])
        cdf = 0.5 * (1.0 + lax.erf(preact * (0.5**0.5)))
        hidden = (preact * cdf).astype(bf16)
        hidden_out[b] = hidden
        slope_out[b] = cdf + preact * jnp.exp(-0.5 * preact * preact) * (0.5 / jnp.pi) ** 0.5
        low_total = low_total + dot(hidden, fc2_down[cols, :])
    low_out[...] = low_of(low_total)


def expand(group, normed, low_fc1, *adapters):
    shapes = [((4, TOK, C), bf16), ((4, TOK, C), f32), ((TOK, RANK), bf16)]
    return pl.pallas_call(
        lambda *refs: expand_kernel(group, *refs),
        out_shape=[jax.ShapeDtypeStruct(*s) for s in shapes],
        in_specs=[VM] * (2 + len(adapters)) + [HBM] * len(group.arrays),
        out_specs=[VM] * len(shapes),
        scratch_shapes=[pltpu.VMEM((4, C, C), bf16), pltpu.SemaphoreType.DMA((4,))],
        compiler_params=params(16),
        cost_estimate=cost(6),
        name="expand",
    )(normed, low_fc1, *in_hbm(adapters), *in_hbm(group.arrays))


def contract_kernel(group_b, group_c, valid, bias_fc2, own, upper, gains, fc2_down, fc2_up, fc1_down, fc1_up, residual, hidden, slope, low_fc2, normed, low_fc1, *rest):
    count_b, count = len(group_b.arrays), len(group_b.arrays) + len(group_c.arrays)
    pieces, (keep_out, away_out, grad_out, pay_out) = rest[:count], rest[count : count + 4]
    whole_b, whole_c, sems_b, sems_c, stage, flat, valid_here, bias_here, more = rest[count + 4 :]
    firsts = [row_of(valid, valid_here, more.at[0]), row_of(bias_fc2, bias_here, more.at[1])]
    start(pieces[count_b:], group_c, whole_c, sems_c)
    start(pieces[:count_b], group_b, whole_b, sems_b)
    for copy in firsts:
        copy.wait()
    flag = valid_here[here()[3]].astype(f32)
    dz = jnp.concatenate([own[1], upper[1]], 0).astype(f32)
    branch = (flag * dz).astype(bf16)
    low_fc2, low_fc1, normed = low_fc2[...], low_fc1[...], normed[...]
    grad_low_fc2 = dot_t(branch, fc2_up[...]).astype(bf16)
    spread_fc2 = over_lanes(grad_low_fc2)
    grad_low_fc1 = jnp.zeros((TOK, RANK), f32)
    grad_normed = jnp.zeros((TOK, C), f32)
    total = jnp.zeros((TOK, C), f32)
    for b in range(4):
        cols = slice(b * C, (b + 1) * C)
        finish(whole_c, sems_c, b)
        total = total + dot_t(hidden[b], whole_c[b])
        grad_hidden = dot(branch, whole_c[b]) + dot_t(spread_fc2, fc2_down[cols, :])
        grad_preact = (grad_hidden * slope[b]).astype(bf16)
        flat[b * C // 8 : (b + 1) * C // 8, :] = fold(tdot(hidden[b], spread_fc2))
        grad_up = tdot(low_fc1, grad_preact)
        width = FF // 2
        at = b * C % width
        put_ranks(stage, (FF // 2 + at) // LANES, b * C // width, grad_up)
        grad_low_fc1 = grad_low_fc1 + dot_t(grad_preact, fc1_up[:, cols])
        finish(whole_b, sems_b, b)
        grad_normed = grad_normed + dot_t(grad_preact, whole_b[b])
    residual = residual[...]
    output = residual + flag * (total + bias_here[...].astype(f32).reshape(1, C) + dot(low_fc2, fc2_up[...]))
    keep_out[...] = output[: TOK // 2].astype(bf16)
    away_out[...] = output[TOK // 2 :].astype(bf16)
    pack_flat(stage, 0, flat, FF // 8)
    tile = pack_ranks(stage, FF // LANES, tdot(low_fc2, branch))
    grad_low_fc1 = grad_low_fc1.astype(bf16)
    spread_fc1 = over_lanes(grad_low_fc1)
    grad_normed = grad_normed + dot_t(spread_fc1, fc1_down[...])
    unit, scale = norm_parts(residual)
    grad_out[...] = dz + norm_back(grad_normed, gains[1:2].astype(f32), unit, scale)
    flat[: C // 8, :] = fold(tdot(normed, spread_fc1))
    pack_flat(stage, tile, flat, C // 8)
    pay_out[...] = stage[...].astype(bf16)


def contract(group_b, group_c, valid, bias_fc2, own, upper, gains, adapters, *near):
    pay = ((FF + C) // LANES, OWNERS, LANES)
    half = jax.ShapeDtypeStruct((TOK // 2, C), bf16)
    arrays = group_b.arrays + group_c.arrays
    return pl.pallas_call(
        lambda *refs: contract_kernel(group_b, group_c, *refs),
        out_shape=[half, half, jax.ShapeDtypeStruct((TOK, C), f32), in_hbm_out(pay, bf16)],
        in_specs=[HBM] * 2 + [VM] * (3 + len(adapters) + len(near)) + [HBM] * len(arrays),
        out_specs=[VM] * 4,
        scratch_shapes=[
            pltpu.VMEM((4, C, C), bf16),
            pltpu.VMEM((4, C, C), bf16),
            pltpu.SemaphoreType.DMA((4,)),
            pltpu.SemaphoreType.DMA((4,)),
            pltpu.VMEM(pay, f32),
            pltpu.VMEM((FF // 8, LANES), f32),
            pltpu.SMEM((2,), jnp.int32),
            pltpu.VMEM((C,), bf16),
            pltpu.SemaphoreType.DMA((2,)),
        ],
        compiler_params=params(28),
        cost_estimate=cost(10),
        name="contract",
    )(*in_hbm([valid, bias_fc2, own, upper, gains, *adapters]), *near, *in_hbm(arrays))


def back_kernel(group, valid, mixed, probs, attended, low_proj, proj_down, proj_up, grad_residual, *rest):
    count = len(group.arrays)
    pieces, (grad_out, pay_out) = rest[:count], rest[count : count + 2]
    whole, sems, stage, flat, valid_here, mixed_held, probs_held, attended_held, more = rest[count + 2 :]
    first = row_of(valid, valid_here, more.at[0])
    start(pieces, group, whole, sems)
    held = [
        [
            row_of(source.at[b], target.at[b], more.at[1 + 3 * b + i])
            for i, (source, target) in enumerate(
                ((mixed, mixed_held), (probs, probs_held), (attended, attended_held))
            )
        ]
        for b in range(4)
    ]
    wide = C // 4
    heads = wide // HD
    first.wait()
    grad_attn = (valid_here[here()[3]].astype(f32) * grad_residual[...]).astype(bf16)
    grad_low_proj = dot_t(grad_attn, proj_up[...]).astype(bf16)
    spread_proj = over_lanes(grad_low_proj)
    for b in range(4):
        rows = slice(b * wide, (b + 1) * wide)
        finish(whole, sems, b)
        for copy in held[b]:
            copy.wait()
        flat[b * wide // 8 : (b + 1) * wide // 8, :] = fold(tdot(attended_held[b], spread_proj))
        grad_heads = dot(grad_attn, whole[b, :, 3 * wide :]) + dot_t(spread_proj, proj_down[rows, :])
        grad_heads = grad_heads.astype(bf16)
        queries, keys, values = (mixed_held[b, :, i * wide : (i + 1) * wide] for i in range(3))
        probs_here = probs_held[b]
        grad_probs = dot_t(stacked(values), grad_heads).reshape(heads, TOK, TOK)
        centre = jnp.sum(grad_probs * probs_here, 1, keepdims=True)
        grad_scores = (probs_here * (grad_probs - centre)).astype(bf16)
        flat_scores = grad_scores.reshape(heads * TOK, TOK)
        grad_queries = by_heads(keys.T, grad_scores).T
        grad_keys = gathered(dot(flat_scores, queries))
        grad_values = gathered(dot(probs_here.astype(bf16).reshape(heads * TOK, TOK), grad_heads))
        grad_out[b] = jnp.concatenate([SCALE * grad_queries, SCALE * grad_keys, grad_values], 1).astype(bf16)
    tile = pack_flat(stage, 0, flat, C // 8)
    pack_ranks(stage, tile, tdot(low_proj[...], grad_attn))
    pay_out[...] = stage[...].astype(bf16)


def back(group, valid, mixed, probs, attended, low_proj, proj_down, proj_up, grad_residual):
    pay = (2 * C * RANK // OWNERS // LANES, OWNERS, LANES)
    far = in_hbm([valid, mixed, probs, attended, low_proj, proj_down, proj_up])
    return pl.pallas_call(
        lambda *refs: back_kernel(group, *refs),
        out_shape=[jax.ShapeDtypeStruct(mixed.shape, bf16), jax.ShapeDtypeStruct(pay, bf16)],
        in_specs=[HBM] * 4 + [VM] * 4 + [HBM] * len(group.arrays),
        out_specs=[VM] * 2,
        scratch_shapes=[
            pltpu.VMEM((4, C, C), bf16),
            pltpu.SemaphoreType.DMA((4,)),
            pltpu.VMEM(pay, f32),
            pltpu.VMEM((C // 8, LANES), f32),
            pltpu.SMEM((2,), jnp.int32),
            pltpu.VMEM(mixed.shape, bf16),
            pltpu.VMEM(probs.shape, f32),
            pltpu.VMEM(attended.shape, bf16),
            pltpu.SemaphoreType.DMA((13,)),
        ],
        compiler_params=params(24),
        cost_estimate=cost(8),
        name="back",
    )(*far, grad_residual, *in_hbm(group.arrays))


def last_kernel(group, own, upper, gains, offsets, low_qkv, qkv_down, qkv_up, pay_one, grad_residual, grad_mixed, pay_two, *rest):
    count = len(group.arrays)
    pieces, (keep_out, away_out, pay_out), (whole, sems, stage, flat, ranks) = rest[:count], rest[count:-5], rest[-5:]
    start(pieces, group, whole, sems)
    wide = C // 4
    gain = gains[0:1].astype(f32)
    unit, scale = norm_parts(jnp.concatenate([own[0], upper[0]], 0).astype(f32))
    shifted = (unit * gain + offsets[0:1].astype(f32)).astype(bf16)
    low_qkv = low_qkv[...]
    grad_shifted = jnp.zeros((TOK, C), f32)
    grad_low_qkv = jnp.zeros((TOK, RANK), f32)
    for b in range(4):
        grad = grad_mixed[b]
        grad_up = tdot(low_qkv, grad)
        for i in range(3):
            ranks[:, i * C + b * wide : i * C + (b + 1) * wide] = grad_up[:, i * wide : (i + 1) * wide]
        grad_low_qkv = grad_low_qkv + dot_t(grad, qkv_up[b])
    for b in range(4):
        finish(whole, sems, b)
        grad_shifted = grad_shifted + dot_t(grad_mixed[b], whole[b, :, : 3 * wide])
    spread_qkv = over_lanes(grad_low_qkv.astype(bf16))
    grad_shifted = grad_shifted + dot_t(spread_qkv, qkv_down[...])
    grad = (grad_residual[...] + norm_back(grad_shifted, gain, unit, scale)).astype(bf16)
    keep_out[...] = grad[: TOK // 2]
    away_out[...] = grad[TOK // 2 :]
    tile = pay_one.shape[0]
    stage[:tile] = pay_one[...].astype(f32)
    stage[tile : tile + pay_two.shape[0]] = pay_two[...].astype(f32)
    tile = pack_ranks(stage, tile + pay_two.shape[0], ranks[...])
    flat[...] = fold(tdot(shifted, spread_qkv))
    pack_flat(stage, tile, flat, C // 8)
    pay_out[...] = jnp.swapaxes(stage[...], 0, 1).astype(bf16)


PAY = 16 * C * RANK // OWNERS // LANES


def last(group, own, upper, gains, offsets, low_qkv, qkv_down, qkv_up, pay_one, *near):
    half = jax.ShapeDtypeStruct((TOK // 2, C), bf16)
    far = in_hbm([own, upper, gains, offsets, low_qkv, qkv_down, qkv_up, pay_one])
    return pl.pallas_call(
        lambda *refs: last_kernel(group, *refs),
        out_shape=[half, half, jax.ShapeDtypeStruct((OWNERS, PAY, LANES), bf16)],
        in_specs=[VM] * (len(far) + len(near)) + [HBM] * len(group.arrays),
        out_specs=[VM] * 3,
        scratch_shapes=[
            pltpu.VMEM((4, C, C), bf16),
            pltpu.SemaphoreType.DMA((4,)),
            pltpu.VMEM((PAY, OWNERS, LANES), f32),
            pltpu.VMEM((C // 8, LANES), f32),
            pltpu.VMEM((RANK, 3 * C), f32),
        ],
        compiler_params=params(16),
        cost_estimate=cost(6),
        name="last",
    )(*far, *near, *in_hbm(group.arrays))


WIDTHS = (12, 12, 3, 3, 3, 3, 9, 3)


def sums_kernel(terms, pick, grad_main, grad_fc2, grad_qkv, grad_fc1, grad_out):
    by_tile = jnp.swapaxes(terms[...].astype(f32), 0, 1).astype(bf16)
    targets = (grad_fc2, grad_fc1, grad_out.at[1], grad_main.at[2], grad_main.at[1], grad_out.at[0], grad_qkv, grad_main.at[0])
    tile = 0
    for target, width in zip(targets, WIDTHS):
        for k in range(width):
            target[:, k * LANES : (k + 1) * LANES] = dot(pick[...], by_tile[tile])
            tile += 1


def sums(terms, pick):
    shapes = [(3, ADAPT, 3 * LANES), (ADAPT, 12 * LANES), (ADAPT, 9 * LANES), (ADAPT, 12 * LANES), (2, ADAPT, 3 * LANES)]
    main, fc2, qkv, fc1, out = pl.pallas_call(
        sums_kernel,
        out_shape=[jax.ShapeDtypeStruct(v, f32) for v in shapes],
        in_specs=[VM] * 2,
        out_specs=[VM] * 5,
        compiler_params=params(8),
        cost_estimate=cost(3),
        name="sums",
    )(terms, *in_hbm([pick]))
    return main.transpose(1, 0, 2), fc2, qkv, fc1, out.transpose(1, 0, 2)


def per_device(
    tokens,
    cotangent,
    adapter_id,
    valid_flag,
    regions,
    w_qkv,
    b_qkv,
    rel_table,
    w_proj,
    b_proj,
    w_fc1,
    b_fc1,
    w_fc2,
    b_fc2,
    norm_gains,
    norm_shifts,
    down_main,
    down_fc2,
    up_qkv,
    up_fc1,
    up_out,
):
    z_count, t_count = lax.axis_size("img"), lax.axis_size("tp")
    images, height, breadth = tokens.shape[:3]
    across = breadth // WIN
    wide = rel_table.shape[1] * HD
    count = 2 * z_count * t_count

    if z_count == 4:
        own_a, piece_a, pack_x, pack_y, own, away = begin(
            adapter_id, tokens, cotangent, w_qkv.transpose(1, 0, 2), w_proj, w_fc1, w_fc2.T, b_qkv, b_fc1,
            rel_table.T,
        )
        along = [shift_img(piece_a, k) for k in (1, 2, 3)]
        by_x, by_y = swap_x(pack_x), swap_y(pack_y)
        upper = swap_ctx(away)
        at = HALF + 16
        pair_b = [jnp.concatenate([pack_x[at:], by_x[at:]], 0)]
        pair_c = [jnp.concatenate([pack_y[at:], by_y[at:]], 0)]
        pair_b.append(shift_img(pair_b[0], 1))
        pair_c.append(shift_img(pair_c[0], 1))
        chosen, pick = choose(
            [piece_a] + along, down_main.transpose(1, 0, 2), down_fc2, up_qkv, up_fc1, up_out.transpose(1, 0, 2)
        )
        many = jnp.concatenate([v[:HALF] for v in along], 0)
        many_x, many_y = swap_x(many), swap_y(many)
        far = swap_xy(after(piece_a, *along))
        mine = lax.all_to_all(chosen, "img", 0, 0, tiled=True)
        gate = (many_x, many_y, far, mine, pair_b[1], pair_c[1], upper)
        cut = many.shape[0] // 2
        relay_y, relay_x = swap_y(after(many_x, *gate)[:cut]), swap_x(after(many_y, *gate)[cut:])
        pair_b.append(shift_img(after(pair_b[1], *gate), 1))
        pair_c.append(shift_img(after(pair_c[1], *gate), 1))
        theirs = swap_ctx(after(mine, *gate))
        adapters = prepare_adapters(mine, theirs)
        additive, bias_qkv, bias_fc1 = biases(after(regions, *gate), [piece_a, by_x, by_y, far])
        gate = (relay_x, relay_y, pair_b[2], pair_c[2], adapters[0], additive)
        first_b = swap_y(after(jnp.concatenate(pair_b[:2], 0), *gate))
        first_c = swap_x(after(jnp.concatenate(pair_c[:2], 0), *gate))
        pair_b.append(shift_img(after(pair_b[2], *gate), 1))
        pair_c.append(shift_img(after(pair_c[2], *gate), 1))
        other_x, other_y = swap_ctx(by_x), swap_ctx(by_y)
        group_a, group_b, group_c = Group(own_a), Group(w_fc1), Group(w_fc2.T)
        group_a.add(by_x, [(0, HALF, 0, 1, 0)], other_x)
        group_a.add(by_y, [(0, HALF, 0, 2, 0)], other_y)
        group_a.add(far, [(0, HALF, 0, 3, 0)])
        for j, array in enumerate((many, many_x, many_y)):
            group_a.add(array, [(HALF * i, HALF, i + 1, j, 0) for i in range(3)])
        group_a.add(relay_y, [(0, HALF, 1, 3, 0), (HALF, HALF // 2, 2, 3, 0)])
        group_a.add(relay_x, [(0, HALF // 2, 2, 3, HALF // 2), (HALF // 2, HALF, 3, 3, 0)])
        group_b.add(by_x, [(at, HALF, 0, 1, 0)], other_x)
        group_c.add(by_y, [(at, HALF, 0, 2, 0)], other_y)
        for k in (1, 2, 3):
            group_b.add(pair_b[k], pair(k, 0, 1))
            group_c.add(pair_c[k], pair(k, 0, 2))
        group_b.add(first_b, pair(0, 2, 3) + pair(1, 2, 3, 2 * HALF))
        group_c.add(first_c, pair(0, 1, 3) + pair(1, 1, 3, 2 * HALF))
    else:
        c, t = lax.axis_index("ctx"), lax.axis_index("tp")
        image, column = t // across, t % across
        both = jnp.stack([lax.dynamic_index_in_dim(a, image, 0, False) for a in (tokens, cotangent)])
        both = lax.dynamic_slice_in_dim(jnp.roll(both, -SHIFT, 2), column * WIN, WIN, 2)
        own = both[:, SHIFT:].reshape(2, TOK // 2, C)
        upper = swap_ctx(both[:, :SHIFT].reshape(2, TOK // 2, C))
        own_a = jnp.concatenate([w_qkv.reshape(-1, 3 * wide), w_proj.T], 1)
        group_a, group_b, group_c = (spread_far(v) for v in (own_a, w_fc1, w_fc2.T))
        ids = lax.all_gather(adapter_id, "img")
        parts = [down_main[:, i] for i in range(3)] + [down_fc2, up_qkv, up_fc1] + [up_out[:, i] for i in range(2)]
        tables = jnp.concatenate(parts, 1)
        wanted = lax.dynamic_index_in_dim(ids, image, 1, False)
        pick = (wanted[:, None] == jnp.arange(ADAPT)[None, :]).astype(bf16)
        mine = lax.all_to_all(dot(pick, tables).astype(bf16), "img", 0, 0, tiled=True)
        theirs = swap_ctx(mine)
        mine, theirs = jnp.where(c == 0, mine, theirs), jnp.where(c == 0, theirs, mine)
        owned = jnp.stack([mine, theirs], 1).reshape(2 * z_count, -1)
        sizes = [v.shape[1] for v in parts]
        cuts = [sum(sizes[:i]) for i in range(9)]
        owned = jnp.concatenate([owned[:, a:b].reshape(SHARDS, -1) for a, b in zip(cuts, cuts[1:])], 1)
        owned = owned.reshape(SHARDS, C // LANES, 32, LANES).transpose(0, 2, 1, 3).reshape(SHARDS // 2, 2, 32, C)
        mine, theirs = jnp.where(c == 0, owned[:, 0], owned[:, 1]), jnp.where(c == 0, owned[:, 1], owned[:, 0])
        adapters = prepare_adapters(mine, theirs)
        source = jnp.broadcast_to(ids[:, None, :, None], (z_count, 2, images, across)).reshape(-1)
        pick = (jnp.arange(ADAPT)[:, None] == source[None, :]).astype(bf16)

        def rows_of(field, rows):
            return jnp.pad(field, ((0, rows - field.shape[0]), (0, C - field.shape[1])))

        small = jnp.concatenate([rows_of(b_qkv, 3), b_fc1[None], jnp.zeros((4, C), bf16), rows_of(rel_table.T, 8)], 0)
        smalls = [small, swap_x(small), swap_y(small), swap_xy(small)]
        additive, bias_qkv, bias_fc1 = biases(regions, smalls)
    qkv_down, proj_down, fc1_down, fc2_down, qkv_up, fc1_up, proj_up, fc2_up = adapters

    mixed, probs, attended, low_qkv, low_proj, low_fc1, residual, normed2 = attend(
        group_a, valid_flag, b_proj, own, upper, norm_gains, norm_shifts, additive, bias_qkv,
        qkv_down, qkv_up, proj_down, proj_up, fc1_down,
    )
    if z_count == 4:
        gate = (first_b, first_c, pair_b[3], pair_c[3], normed2)
        last_b = swap_y(after(jnp.concatenate(pair_b[2:], 0), *gate))
        last_c = swap_x(after(jnp.concatenate(pair_c[2:], 0), *gate))
        group_b.add(last_b, pair(2, 2, 3) + pair(3, 2, 3, 2 * HALF))
        group_c.add(last_c, pair(2, 1, 3) + pair(3, 1, 3, 2 * HALF))
    hidden, slope, low_fc2 = expand(group_b, normed2, low_fc1, fc1_up, bias_fc1, fc2_down)
    keep, away, grad_residual, pay_one = contract(
        group_b, group_c, valid_flag, b_fc2, own, upper, norm_gains, (fc2_down, fc2_up, fc1_down, fc1_up),
        residual, hidden, slope, low_fc2, normed2, low_fc1,
    )
    grad_mixed, pay_two = back(
        group_a, valid_flag, mixed, probs, attended, low_proj, proj_down, proj_up, grad_residual
    )

    def placed(keep, away, dtype):
        half = jnp.concatenate([swap_ctx(away), keep], 0)
        pieces = [half, swap_x(half), swap_y(half), swap_xy(half)]
        return place(pieces, dtype).reshape(images, height, breadth, C), half

    output, _ = placed(keep, away, bf16)
    grad_mixed, output = lax.optimization_barrier((grad_mixed, output))
    keep, away, pay = last(
        group_a, own, upper, norm_gains, norm_shifts, low_qkv, qkv_down, qkv_up, pay_one, grad_residual,
        grad_mixed, pay_two,
    )
    grad_tokens, half = placed(keep, away, f32)

    if count == OWNERS:
        grads = sums(lax.all_to_all(after(pay, half), ("img", "ctx", "tp"), 0, 0, tiled=True), pick)
    else:
        cuts = [LANES * sum(WIDTHS[:i]) for i in range(9)]
        pay = pay.reshape(OWNERS, PAY * LANES)
        pay = jnp.concatenate([pay[:, a:b].reshape(count, -1) for a, b in zip(cuts, cuts[1:])], 1)
        cuts = [v * OWNERS // count for v in cuts]
        added = dot(pick, lax.all_to_all(pay, ("img", "ctx", "tp"), 0, 0, tiled=True))
        fc2, fc1, out1, main2, main1, out0, qkv, main0 = (added[:, a:b] for a, b in zip(cuts, cuts[1:]))
        grads = jnp.stack([main0, main1, main2], 1), fc2, qkv, fc1, jnp.stack([out0, out1], 1)
    return (output, grad_tokens, *grads)


def solution(mesh):
    in_specs = (
        P("img", "ctx", None, None),
        P("img", "ctx", None, None),
        P("img"),
        P("img"),
        P("ctx", None),
        P("img", None, "tp"),
        P(None, "tp"),
        P(None, "tp"),
        P("tp", "img"),
        P(),
        P("img", "tp"),
        P("tp"),
        P("tp", "img"),
        P(),
        P(),
        P(),
        P(None, None, ("img", "ctx")),
        P(None, ("img", "ctx")),
        P(None, ("img", "ctx")),
        P(None, ("img", "ctx")),
        P(None, None, ("img", "ctx")),
    )
    out_specs = (
        P("img", "ctx", None, None),
        P("img", "ctx", None, None),
        P(None, None, ("img", "ctx", "tp")),
        P(None, ("img", "ctx", "tp")),
        P(None, ("img", "ctx", "tp")),
        P(None, ("img", "ctx", "tp")),
        P(None, None, ("img", "ctx", "tp")),
    )
    return jax.shard_map(
        per_device, mesh=mesh, in_specs=in_specs, out_specs=out_specs, check_vma=False
    )
```

```python
import jax
import jax.numpy as jnp
from jax import lax
from jax.experimental import pallas as pl
from jax.experimental.pallas import tpu as pltpu
from jax.sharding import PartitionSpec as P

C = 768
HD = 32
FF = 3072
WIN = 12
SHIFT = 6
RANK = 16
ADAPT = 8
RELS = 529
TOK = WIN * WIN
SCALE = HD ** (-0.5)
EPS = 1e-05
LANES = 128
SHARDS = 8
OWNERS = 32

bf16 = jnp.bfloat16
f32 = jnp.float32

VM = pl.BlockSpec(memory_space=pltpu.VMEM)
SM = pl.BlockSpec(memory_space=pltpu.SMEM)
HBM = pl.BlockSpec(memory_space=pltpu.HBM)


def params(mib):
    return pltpu.CompilerParams(vmem_limit_bytes=mib << 20)


def in_hbm(arrays):
    return [pltpu.with_memory_space_constraint(v, pltpu.HBM) for v in arrays]


def in_hbm_out(shape, dtype):
    return pltpu.HBM(shape, dtype)


def here():
    z, c, t = (lax.axis_index(name) for name in ("img", "ctx", "tp"))
    return z, c, t, lax.div(t, 2), lax.rem(t, 2)


def cost(us):
    return pl.CostEstimate(flops=0, transcendentals=0, bytes_accessed=int(us * 3e6))


def dot(left, right):
    return jnp.dot(left, right, preferred_element_type=f32)


def dot_t(left, right):
    return lax.dot_general(left, right, (((1,), (1,)), ((), ())), preferred_element_type=f32)


def tdot(left, right):
    return lax.dot_general(left, right, (((0,), (0,)), ((), ())), preferred_element_type=f32)


def swap_ctx(v):
    return lax.ppermute(v, "ctx", [(0, 1), (1, 0)])


def swap_x(v):
    return lax.ppermute(v, "tp", [(0, 1), (1, 0), (2, 3), (3, 2)])


def swap_y(v):
    return lax.ppermute(v, "tp", [(0, 2), (2, 0), (1, 3), (3, 1)])


def swap_xy(v):
    return lax.ppermute(v, "tp", [(0, 3), (3, 0), (1, 2), (2, 1)])


def after(v, *others):
    return lax.optimization_barrier((v,) + others)[0]


def shift_img(v, k):
    count = lax.axis_size("img")
    return lax.ppermute(v, "img", [(i, (i + k) % count) for i in range(count)])


HALF = 96
PIECE = 3 * HALF
SMALL = 16


class Group:
    def __init__(self):
        self.plan, self.places = [], []

    def add(self, index, at, rows, k, j, core, first):
        self.plan.append((index, at, rows))
        self.places.append((k, j, core, first))


def spread(groups, arrays, held, parts):
    for core, array in enumerate((held, swap_ctx(held))):
        for at, rows, top, k, j in parts:
            for n, group in enumerate(groups):
                first, last = max(top, n * HALF), min(top + rows, (n + 1) * HALF)
                if first < last:
                    group.add(len(arrays), at + first - top, last - first, k, j, core, first - n * HALF)
        arrays.append(array)


def spread_far(own):
    whole = lax.all_gather(own, "img", axis=0, tiled=True)
    by_x = swap_x(whole)
    return [whole, by_x, swap_y(whole), swap_y(by_x)]


def norm_parts(field):
    average = jnp.mean(field, -1, keepdims=True)
    centred = field - average
    variance = jnp.mean(centred * centred, -1, keepdims=True)
    scale = lax.rsqrt(variance + EPS)
    return centred * scale, scale


def norm_back(grad, gain, unit, scale):
    scaled = grad * gain
    return scale * (
        scaled
        - jnp.mean(scaled, -1, keepdims=True)
        - unit * jnp.mean(scaled * unit, -1, keepdims=True)
    )


def start(group_refs, group, whole, sems, only=None):
    z, c, t, _, _ = here()
    count = lax.axis_size("img")
    rows_each = C // count
    for (index, at, rows), (k, j, core, first) in zip(group.plan, group.places):
        if only not in (None, j):
            continue
        source = group_refs[index].at[pl.ds(at, rows), :]
        top = 0 if k is None else lax.rem(z + (count - k), count) * rows_each + first
        if core is not None:
            top = top + (c ^ core) * (rows_each // 2)
        block = t ^ j
        target = whole.at[block, pl.ds(pl.multiple_of(top, 16), rows), :]
        pltpu.make_async_copy(source, target, sems.at[block]).start()


def finish(whole, sems, block):
    pltpu.make_async_copy(whole.at[block], whole.at[block], sems.at[block]).wait()


def lane_group(rows):
    lane = lax.broadcasted_iota(jnp.int32, (rows, LANES), 1) // RANK
    row = lax.broadcasted_iota(jnp.int32, (rows, LANES), 0) % 8
    return (lane == row).astype(f32)


def low_of(spread_sum):
    for step in (64, 32, 16):
        spread_sum = spread_sum + pltpu.roll(spread_sum, step, 1)
    return spread_sum[:, :RANK].astype(bf16)


def over_lanes(low):
    lane = lax.broadcasted_iota(jnp.int32, (RANK, LANES), 1) % RANK
    rank = lax.broadcasted_iota(jnp.int32, (RANK, LANES), 0)
    return dot(low, (lane == rank).astype(bf16)).astype(bf16)


def fold(product):
    rows = product.shape[0]
    kept = (product * lane_group(rows)).reshape(rows // 8, 8, LANES)
    return jnp.sum(kept, 1)


def put_ranks(stage, tile, h, grad):
    for k in range(grad.shape[1] // LANES):
        stage[tile + k, pl.ds(h, RANK, stride=2), :] = grad[:, k * LANES : (k + 1) * LANES]


def pack_ranks(stage, tile, grad):
    width = grad.shape[1] // 2
    for h in range(2):
        put_ranks(stage, tile, h, grad[:, h * width : (h + 1) * width])
    return tile + width // LANES


def pack_flat(stage, tile, flat, rows):
    each = rows // OWNERS
    for k in range(each):
        stage[tile + k] = flat[pl.ds(k, OWNERS, stride=each), :]
    return tile + each


def begin_kernel(ids, w_qkv, w_proj, w_fc1, w_fc2, b_qkv, b_fc1, rel, piece, ids_here, held_qkv, held_proj, held_bq, held_b1, held_rel, small, sems):
    c = here()[1]
    half = pl.ds(pl.multiple_of(c * HALF, 16), HALF)
    moves = (
        (w_qkv.at[:, half, :], held_qkv),
        (w_proj, held_proj),
        (b_qkv, held_bq),
        (b_fc1, held_b1),
        (rel, held_rel),
        (ids, ids_here),
        (w_fc1.at[half, :], piece.at[pl.ds(HALF, HALF), :]),
        (w_fc2.at[half, :], piece.at[pl.ds(2 * HALF, HALF), :]),
    )
    copies = [pltpu.make_async_copy(*move, sems.at[i]) for i, move in enumerate(moves)]
    for copy in copies:
        copy.start()
    lane = lax.broadcasted_iota(jnp.int32, (1, C), 1)
    small[...] = jnp.zeros_like(small)
    for copy in copies[:6]:
        copy.wait()
    proj = held_proj[...].T
    proj = jnp.where(c == 0, proj[:HALF], proj[HALF:])
    piece[:HALF] = jnp.concatenate([held_qkv[0], held_qkv[1], held_qkv[2], proj], 1)
    small[:3, : b_qkv.shape[1]] = held_bq[...].astype(f32)
    small[3:4, :] = held_b1[...].astype(f32).reshape(1, C)
    first, second = ids_here[0].astype(f32), ids_here[1].astype(f32)
    small[4:5, :] = jnp.where(lane == 0, first, jnp.where(lane == 1, second, 0.0))
    small[8 : 8 + rel.shape[0], : rel.shape[1]] = held_rel[...].astype(f32)
    piece[PIECE:] = small[...].astype(bf16)
    for copy in copies[6:]:
        copy.wait()


def begin(ids, *args):
    w_qkv, w_proj, _, _, b_qkv, b_fc1, rel = (v.shape for v in args)
    held = [(3, HALF, w_qkv[2]), w_proj, b_qkv, b_fc1, rel]
    return pl.pallas_call(
        begin_kernel,
        out_shape=jax.ShapeDtypeStruct((PIECE + SMALL, C), bf16),
        in_specs=[HBM] * (1 + len(args)),
        out_specs=VM,
        scratch_shapes=[pltpu.SMEM((2,), jnp.int32)]
        + [pltpu.VMEM(v, bf16) for v in held]
        + [pltpu.VMEM((SMALL, C), f32), pltpu.SemaphoreType.DMA((8,))],
        compiler_params=params(6),
        name="begin",
    )(*in_hbm([ids, *args]))


def cut_kernel(tokens, cotangent, w_qkv, w_proj, own_a, own, away, image, held_qkv, held_proj, sems):
    at, column = here()[3:]
    moves = (
        (w_qkv, held_qkv),
        (w_proj, held_proj),
        (tokens.at[at], image.at[0]),
        (cotangent.at[at], image.at[1]),
    )
    copies = [pltpu.make_async_copy(*move, sems.at[i]) for i, move in enumerate(moves)]
    for copy in copies:
        copy.start()
    for copy in copies[:2]:
        copy.wait()
    own_a[...] = jnp.concatenate([held_qkv[0], held_qkv[1], held_qkv[2], held_proj[...].T], 1)
    for i, copy in enumerate(copies[2:]):
        copy.wait()
        block = image[i].astype(f32)
        rows = []
        for r in range(WIN):
            at = r * 2 * WIN
            inner = block[at + SHIFT : at + SHIFT + WIN]
            outer = jnp.concatenate([block[at + SHIFT + WIN : at + 2 * WIN], block[at : at + SHIFT]], 0)
            rows.append(jnp.where(column == 0, inner, outer))
        away[i] = jnp.concatenate(rows[:SHIFT], 0).astype(bf16)
        own[i] = jnp.concatenate(rows[SHIFT:], 0).astype(bf16)


def cut_windows(tokens, cotangent, w_qkv, w_proj):
    flat = (tokens.shape[0], -1, C)
    windows = (2, TOK // 2, C)
    return pl.pallas_call(
        cut_kernel,
        out_shape=[in_hbm_out((2 * HALF, C), bf16), in_hbm_out(windows, bf16), jax.ShapeDtypeStruct(windows, bf16)],
        in_specs=[HBM] * 4,
        out_specs=[VM] * 3,
        scratch_shapes=[
            pltpu.VMEM((2, 2 * TOK, C), bf16),
            pltpu.VMEM(w_qkv.shape, bf16),
            pltpu.VMEM(w_proj.shape, bf16),
            pltpu.SemaphoreType.DMA((4,)),
        ],
        compiler_params=params(10),
        name="cut_windows",
    )(*in_hbm([tokens.reshape(flat), cotangent.reshape(flat), w_qkv, w_proj]))


def place_kernel(*refs):
    pieces, out, held = refs[:4], refs[4], refs[5]
    t = here()[2]
    for j, piece in enumerate(pieces):
        held[t ^ j] = piece[...].astype(f32)
    for i in range(2):
        left, right = held[2 * i], held[2 * i + 1]
        for r in range(WIN):
            rows = slice(r * WIN, (r + 1) * WIN)
            inner, outer = left[rows], right[rows]
            line = jnp.concatenate([outer[SHIFT:], inner, outer[:SHIFT]], 0)
            out[i, r * 2 * WIN : (r + 1) * 2 * WIN] = line.astype(out.dtype)


def place(pieces, dtype):
    return pl.pallas_call(
        place_kernel,
        out_shape=jax.ShapeDtypeStruct((2, 2 * TOK, C), dtype),
        in_specs=[VM] * 4,
        out_specs=VM,
        scratch_shapes=[pltpu.VMEM((4, TOK, C), f32)],
        compiler_params=params(8),
        cost_estimate=cost(2),
        name="place",
    )(*pieces)


TILES = 12 * RANK


def choose_kernel(*refs):
    held, tables, (chosen_out, pick), (table, stage, sems) = refs[0], refs[1:6], refs[6:8], refs[8:]
    z, _, _, image, _ = here()
    copies = []
    col = 0
    for field in tables:
        for i in range(1 if len(field.shape) == 2 else field.shape[0]):
            source = field if len(field.shape) == 2 else field.at[i]
            width = source.shape[1]
            copies.append(pltpu.make_async_copy(source, table.at[:, pl.ds(col, width)], sems.at[len(copies)]))
            col += width
    for copy in copies:
        copy.start()
    source = lax.broadcasted_iota(jnp.int32, pick.shape, 1)
    owner = jnp.zeros(pick.shape, f32)
    wanted = []
    for k in range(4):
        known = held[-k % 4 * 16 : -k % 4 * 16 + 16, :].astype(f32)[4:5]
        lane = lax.broadcasted_iota(jnp.int32, known.shape, 1)
        ids = [jnp.sum(jnp.where(lane == i, known, 0.0), 1, keepdims=True) for i in range(2)]
        at = lax.rem(z + k, 4)
        owner = jnp.where(source // 8 == at, jnp.where(source % 4 < 2, ids[0], ids[1]), owner)
        wanted.append(jnp.where(image == 0, ids[0], ids[1]))
    pick[...] = (lax.broadcasted_iota(jnp.int32, pick.shape, 0).astype(f32) == owner).astype(bf16)
    for copy in copies:
        copy.wait()
    for tile in range(TILES):
        field = table[:, tile * LANES : (tile + 1) * LANES].astype(f32)
        row = lax.broadcasted_iota(jnp.int32, field.shape, 0).astype(f32)
        for k in range(4):
            chosen = jnp.sum(jnp.where(row == wanted[k], field, 0.0), 0, keepdims=True)
            stage[k, tile : tile + 1, :] = chosen
    for k in range(4):
        at = lax.rem(z + k, 4)
        for i in range(C // LANES):
            chosen_out[at, :, i * LANES : (i + 1) * LANES] = stage[k, i * 32 : (i + 1) * 32, :].astype(bf16)


def choose(held, *tables):
    return pl.pallas_call(
        choose_kernel,
        out_shape=[jax.ShapeDtypeStruct((4, 32, C), bf16), in_hbm_out((ADAPT, OWNERS), bf16)],
        in_specs=[VM] + [HBM] * 5,
        out_specs=[VM] * 2,
        scratch_shapes=[
            pltpu.VMEM((ADAPT, TILES * LANES), bf16),
            pltpu.VMEM((4, TILES, LANES), f32),
            pltpu.SemaphoreType.DMA((8,)),
        ],
        compiler_params=params(4),
        cost_estimate=cost(0.1),
        name="choose",
    )(held, *in_hbm(tables))


def expand_adapters(joined, qkv_down, proj_down, fc1_down, fc2_down, qkv_up, fc1_up, proj_up, fc2_up, ranks):
    for shard in range(SHARDS):
        rows = joined[shard].astype(f32)
        tiles = jnp.concatenate([rows[:, i * LANES : (i + 1) * LANES] for i in range(C // LANES)], 0)
        row = 0
        for out in (qkv_down, proj_down, fc1_down, fc2_down):
            rows = out.shape[1]
            part = tiles[row : row + rows // 8]
            spread = jnp.broadcast_to(part[:, None, :], (rows // 8, 8, LANES)).reshape(rows, LANES)
            out[shard] = (spread * lane_group(rows)).astype(bf16)
            row += rows // 8
        tile = 0
        for width in (3 * C, FF, C, C):
            for e in range(2):
                for k in range(width // LANES):
                    ranks[tile + k, 2 * shard + e : 2 * shard + e + 1, :] = tiles[row : row + 1]
                    row += 1
            tile += width // LANES
    wide = C // 4
    tile = 3 * C // LANES
    table = jnp.concatenate([ranks[k] for k in range(tile)], 1)
    for b in range(4):
        parts = [table[:, i * C + b * wide : i * C + (b + 1) * wide] for i in range(3)]
        qkv_up[b] = jnp.concatenate(parts, 1).astype(bf16)
    for out in (fc1_up, proj_up, fc2_up):
        for k in range(out.shape[1] // LANES):
            out[:, k * LANES : (k + 1) * LANES] = ranks[tile + k].astype(bf16)
        tile += out.shape[1] // LANES


def join_kernel(mine, theirs, out):
    c = here()[1]
    for n in range(SHARDS // 2):
        out[2 * n + c] = mine[n]
        out[2 * n + (c ^ 1)] = theirs[n]


def join(mine, theirs):
    return pl.pallas_call(
        join_kernel,
        out_shape=in_hbm_out((SHARDS, 32, C), bf16),
        in_specs=[VM, VM],
        out_specs=VM,
        compiler_params=params(4),
        name="join",
    )(mine, theirs)


SPAN = 2 * WIN - 1
STRIP = 3 * LANES


ENTRIES = 5 * LANES


def bias_kernel(regions, held, strips, mask_out, bias_qkv, bias_fc1):
    _, _, t, _, column = here()
    wide = C // 4
    heads = wide // HD
    lane = lax.broadcasted_iota(jnp.int32, (ENTRIES, STRIP), 1)
    entry = lax.broadcasted_iota(jnp.int32, (ENTRIES, STRIP), 0)
    chosen = (entry == (lane // WIN) * SPAN + lane % WIN + WIN - 1).astype(bf16)
    tables = []
    for j in range(4):
        field = held[16 * j : 16 * (j + 1), :].astype(f32)
        block = t ^ j
        bias_qkv[block] = jnp.concatenate([field[i : i + 1, :wide] for i in range(3)], 1)
        bias_fc1[block] = field[3:4]
        tables.append(field[8:, :ENTRIES])
    table = jnp.concatenate(tables, 0)
    rolled = [pltpu.roll(table, key, 1) if key else table for key in range(WIN)]
    all_strips = dot(jnp.concatenate(rolled, 0).astype(bf16), chosen)
    for key in range(WIN):
        strip = all_strips[key * table.shape[0] : (key + 1) * table.shape[0]]
        for j in range(4):
            for h in range(heads):
                strips[t ^ j, h, key : key + 1, :] = strip[8 * j + h : 8 * j + h + 1]
    row = lax.broadcasted_iota(jnp.int32, (TOK, WIN), 0) // WIN
    at_row = (row == lax.broadcasted_iota(jnp.int32, (TOK, WIN), 1)).astype(bf16)
    lines = dot(at_row, regions[...].astype(f32).astype(bf16))
    cell = lax.broadcasted_iota(jnp.int32, lines.shape, 0) % WIN + column * WIN
    lines = jnp.where(cell == lax.broadcasted_iota(jnp.int32, lines.shape, 1), lines, 0.0)
    by_key = jnp.sum(lines, 1, keepdims=True)
    by_query = dot_t(jnp.ones((8, lines.shape[1]), bf16), lines.astype(bf16))[:1]
    mask_out[...] = jnp.where(by_key == by_query, 0.0, -100.0)


def placed_biases(strips):
    strip = strips[:WIN]
    return jnp.concatenate([strip[:, (WIN - 1 - r) * WIN : (WIN - 1 - r) * WIN + TOK] for r in range(WIN)], 0)


def biases(regions, smalls):
    heads = C // HD
    return pl.pallas_call(
        bias_kernel,
        out_shape=[
            in_hbm_out((4, heads // 4, 16, STRIP), f32),
            in_hbm_out((TOK, TOK), f32),
            in_hbm_out((4, 1, 3 * C // 4), f32),
            in_hbm_out((4, 1, FF // 4), f32),
        ],
        in_specs=[VM] * 2,
        out_specs=[VM] * 4,
        compiler_params=params(12),
        cost_estimate=cost(0.1),
        name="biases",
    )(*in_hbm([regions]), smalls)


def head_mask(head):
    lane = lax.broadcasted_iota(jnp.int32, (TOK, C // 4), 1) // HD
    return lane == head


def only(head, field):
    return jnp.where(head_mask(head), field, jnp.zeros_like(field))


def stacked(field):
    return jnp.concatenate([only(h, field) for h in range(C // 4 // HD)], 0)


def gathered(product):
    total = jnp.zeros((TOK, C // 4), f32)
    for h in range(C // 4 // HD):
        total = jnp.where(head_mask(h), product[h * TOK : (h + 1) * TOK], total)
    return total


def by_heads(field, probs):
    parts = [dot(field[h * HD : (h + 1) * HD], probs[h]) for h in range(C // 4 // HD)]
    return jnp.concatenate(parts, 0)


def row_of(ref, held, sem):
    copy = pltpu.make_async_copy(ref, held, sem)
    copy.start()
    return copy


FAR = (
    "joined", "valid", "own", "upper", "gains", "offsets", "bias_qkv", "mask", "strips", "bias_proj",
    "bias_fc1", "bias_fc2",
)
FAR_BACK = ("valid", "own", "upper", "gains", "offsets", "pay")


def loading(names, far, held, sems):
    loads = {name: pltpu.make_async_copy(far[name], held[name], sems.at[n]) for n, name in enumerate(names)}

    def take(*wanted):
        for name in wanted:
            loads[name].wait()

    return loads, take


def forward_kernel(group_a, group_b, group_c, count, *refs):
    far, refs = dict(zip(FAR, refs)), refs[len(FAR) :]
    pieces, refs = refs[:count], refs[count:]
    keep_out, away_out, pay_out, residual_out, low_qkv_out, low_proj_out, all_mixed, all_probs, all_attended = refs[:9]
    whole_a, qkv_down, proj_down, qkv_up, proj_up = refs[9:14]
    held, refs = dict(zip(FAR, refs[14:])), refs[14 + len(FAR) :]
    whole_b, whole_c, sems_a, sems_b, sems_c, hidden, slope, stage, flat, more, fc1_down, fc2_down, fc1_up, fc2_up, ranks = refs
    loads, take = loading(FAR, far, held, more)
    for name in FAR[:9]:
        loads[name].start()
    t = here()[2]
    blocks = [t ^ j for j in range(4)]
    for j in range(4):
        start(pieces, group_a, whole_a, sems_a, j)
    for name in FAR[9:]:
        loads[name].start()
    wide = C // 4
    heads = wide // HD

    take("joined")
    expand_adapters(
        held["joined"], qkv_down, proj_down, fc1_down, fc2_down, qkv_up, fc1_up, proj_up, fc2_up, ranks
    )
    take("valid", "own", "upper", "gains", "offsets")
    flag = held["valid"][here()[3]].astype(f32)
    gains, offsets = held["gains"][...].astype(f32), held["offsets"][...].astype(f32)
    inputs = jnp.concatenate([held["own"][0], held["upper"][0]], 0).astype(f32)
    unit, _ = norm_parts(inputs)
    shifted = (unit * gains[0:1] + offsets[0:1]).astype(bf16)
    take("bias_qkv")
    low_qkv = low_of(dot(shifted, qkv_down[...].reshape(C, LANES)))
    low_qkv_out[...] = low_qkv
    total = jnp.zeros((TOK, C), f32)
    low_total = jnp.zeros((TOK, LANES), f32)
    for j, b in enumerate(blocks):
        finish(whole_a, sems_a, b)
        mixed = dot(shifted, whole_a[b, :, : 3 * wide]) + held["bias_qkv"][b] + dot(low_qkv, qkv_up[b])
        mixed = mixed.astype(bf16)
        all_mixed[b] = mixed
        queries, keys, values = (mixed[:, i * wide : (i + 1) * wide] for i in range(3))
        if j == 0:
            take("mask", "strips")
            start(pieces, group_b, whole_b, sems_b)
        biases_here = [placed_biases(held["strips"][b, h]) + held["mask"][...] for h in range(heads)]
        scores = SCALE * dot_t(stacked(keys), queries).reshape(heads, TOK, TOK) + jnp.stack(biases_here)
        weight = jnp.exp(scores - jnp.max(scores, 1, keepdims=True))
        probs = weight / jnp.sum(weight, 1, keepdims=True)
        all_probs[b] = probs
        attended = by_heads(values.T, probs.astype(bf16)).astype(bf16).T
        all_attended[b] = attended
        total = total + dot_t(attended, whole_a[b, :, 3 * wide :])
        low_total = low_total + dot(attended, proj_down[pl.ds(2 * b, 2)].reshape(wide, LANES))
    low_proj = low_of(low_total)
    low_proj_out[...] = low_proj
    take("bias_proj")
    branch = total + held["bias_proj"][...].astype(f32).reshape(1, C) + dot(low_proj, proj_up[...])
    residual = inputs + flag * branch
    unit, _ = norm_parts(residual)
    field = (unit * gains[1:2] + offsets[1:2]).astype(bf16)
    low_fc1 = low_of(dot(field, fc1_down[...].reshape(C, LANES)))

    take("bias_fc1")
    low_total = jnp.zeros((TOK, LANES), f32)
    for b in range(4):
        cols = slice(b * C, (b + 1) * C)
        finish(whole_b, sems_b, b)
        if b == 0:
            start(pieces, group_c, whole_c, sems_c)
        preact = dot(field, whole_b[b]) + held["bias_fc1"][b] + dot(low_fc1, fc1_up[:, cols])
        cdf = 0.5 * (1.0 + lax.erf(preact * (0.5**0.5)))
        active = (preact * cdf).astype(bf16)
        hidden[b] = active
        slope[b] = cdf + preact * jnp.exp(-0.5 * preact * preact) * (0.5 / jnp.pi) ** 0.5
        low_total = low_total + dot(active, fc2_down[2 * b : 2 * b + 2].reshape(C, LANES))
    low_fc2 = low_of(low_total)

    take("bias_fc2")
    dz = jnp.concatenate([held["own"][1], held["upper"][1]], 0).astype(f32)
    branch = (flag * dz).astype(bf16)
    grad_low_fc2 = dot_t(branch, fc2_up[...]).astype(bf16)
    spread_fc2 = over_lanes(grad_low_fc2)
    grad_low_fc1 = jnp.zeros((TOK, RANK), f32)
    grad_normed = jnp.zeros((TOK, C), f32)
    total = jnp.zeros((TOK, C), f32)
    for b in range(4):
        cols = slice(b * C, (b + 1) * C)
        finish(whole_c, sems_c, b)
        total = total + dot_t(hidden[b], whole_c[b])
        grad_hidden = dot(branch, whole_c[b]) + dot_t(spread_fc2, fc2_down[2 * b : 2 * b + 2].reshape(C, LANES))
        grad_preact = (grad_hidden * slope[b]).astype(bf16)
        flat[b * C // 8 : (b + 1) * C // 8, :] = fold(tdot(hidden[b], spread_fc2))
        grad_up = tdot(low_fc1, grad_preact)
        width = FF // 2
        at = b * C % width
        put_ranks(stage, (FF // 2 + at) // LANES, b * C // width, grad_up)
        grad_low_fc1 = grad_low_fc1 + dot_t(grad_preact, fc1_up[:, cols])
        grad_normed = grad_normed + dot_t(grad_preact, whole_b[b])
    pack_flat(stage, 0, flat, FF // 8)
    tile = pack_ranks(stage, FF // LANES, tdot(low_fc2, branch))
    grad_low_fc1 = grad_low_fc1.astype(bf16)
    spread_fc1 = over_lanes(grad_low_fc1)
    grad_normed = grad_normed + dot_t(spread_fc1, fc1_down[...].reshape(C, LANES))
    bias = held["bias_fc2"][...].astype(f32).reshape(1, C)
    output = residual + flag * (total + bias + dot(low_fc2, fc2_up[...]))
    keep_out[...] = output[: TOK // 2].astype(bf16)
    away_out[...] = output[TOK // 2 :].astype(bf16)
    unit, scale = norm_parts(residual)
    residual_out[...] = dz + norm_back(grad_normed, held["gains"][1:2].astype(f32), unit, scale)
    flat[: C // 8, :] = fold(tdot(field, spread_fc1))
    pack_flat(stage, tile, flat, C // 8)
    pay_out[...] = stage[...].astype(bf16)


def scratch_of(far):
    return [(pltpu.SMEM if v.dtype == jnp.int32 else pltpu.VMEM)(v.shape, v.dtype) for v in far]


def forward(groups, arrays, **far):
    pay = ((FF + C) // LANES, OWNERS, LANES)
    half = jax.ShapeDtypeStruct((TOK // 2, C), bf16)
    wide = C // 4
    mixed, probs, attended = (4, TOK, 3 * wide), (4, wide // HD, TOK, TOK), (4, TOK, wide)
    far = [far[name] for name in FAR]
    return pl.pallas_call(
        lambda *refs: forward_kernel(*groups, len(arrays), *refs),
        out_shape=[
            half,
            half,
            in_hbm_out(pay, bf16),
            jax.ShapeDtypeStruct((TOK, C), f32),
            jax.ShapeDtypeStruct((TOK, RANK), bf16),
            jax.ShapeDtypeStruct((TOK, RANK), bf16),
            jax.ShapeDtypeStruct(mixed, bf16),
            jax.ShapeDtypeStruct(probs, f32),
            jax.ShapeDtypeStruct(attended, bf16),
            jax.ShapeDtypeStruct((4, C, C), bf16),
            jax.ShapeDtypeStruct((SHARDS, HALF, LANES), bf16),
            jax.ShapeDtypeStruct((SHARDS, HALF, LANES), bf16),
            jax.ShapeDtypeStruct((4, RANK, 3 * wide), bf16),
            jax.ShapeDtypeStruct((RANK, C), bf16),
        ],
        in_specs=[HBM] * (len(far) + len(arrays)),
        out_specs=[VM] * 14,
        scratch_shapes=scratch_of(far)
        + [pltpu.VMEM((4, C, C), bf16)] * 2
        + [pltpu.SemaphoreType.DMA((4,))] * 3
        + [
            pltpu.VMEM((4, TOK, C), bf16),
            pltpu.VMEM((4, TOK, C), f32),
            pltpu.VMEM(pay, f32),
            pltpu.VMEM((FF // 8, LANES), f32),
            pltpu.SemaphoreType.DMA((len(FAR),)),
            pltpu.VMEM((SHARDS, HALF, LANES), bf16),
            pltpu.VMEM((SHARDS, FF // SHARDS, LANES), bf16),
            pltpu.VMEM((RANK, FF), bf16),
            pltpu.VMEM((RANK, C), bf16),
            pltpu.VMEM(((3 * C + FF + 2 * C) // LANES, RANK, LANES), f32),
        ],
        compiler_params=params(36),
        cost_estimate=cost(17),
        name="forward",
    )(*in_hbm(far), *in_hbm(arrays))


def backward_kernel(*refs):
    far, refs = dict(zip(FAR_BACK, refs)), refs[len(FAR_BACK) :]
    residual_in, low_qkv_in, low_proj_in, all_mixed, all_probs, all_attended, whole_a = refs[:7]
    qkv_down, proj_down, qkv_up, proj_up, keep_out, away_out, pay_out = refs[7:14]
    held, refs = dict(zip(FAR_BACK, refs[14:])), refs[14 + len(FAR_BACK) :]
    stage, flat, ranks, more = refs
    loads, take = loading(FAR_BACK, far, held, more)
    for name in FAR_BACK:
        loads[name].start()
    wide = C // 4
    heads = wide // HD
    take("valid", "own", "upper", "gains", "offsets")
    flag = held["valid"][here()[3]].astype(f32)
    gain = held["gains"][0:1].astype(f32)
    inputs = jnp.concatenate([held["own"][0], held["upper"][0]], 0).astype(f32)
    unit, scale = norm_parts(inputs)
    shifted = (unit * gain + held["offsets"][0:1].astype(f32)).astype(bf16)
    low_qkv = low_qkv_in[...]
    grad_residual = residual_in[...]
    grad_attn = (flag * grad_residual).astype(bf16)
    grad_low_proj = dot_t(grad_attn, proj_up[...]).astype(bf16)
    spread_proj = over_lanes(grad_low_proj)
    grad_low_qkv = jnp.zeros((TOK, RANK), f32)
    grad_shifted = jnp.zeros((TOK, C), f32)
    for b in range(4):
        rows = slice(b * wide, (b + 1) * wide)
        flat[b * wide // 8 : (b + 1) * wide // 8, :] = fold(tdot(all_attended[b], spread_proj))
        grad_heads = dot(grad_attn, whole_a[b, :, 3 * wide :]) + dot_t(spread_proj, proj_down[2 * b : 2 * b + 2].reshape(wide, LANES))
        grad_heads = grad_heads.astype(bf16)
        queries, keys, values = (all_mixed[b, :, i * wide : (i + 1) * wide] for i in range(3))
        probs = all_probs[b]
        grad_probs = dot_t(stacked(values), grad_heads).reshape(heads, TOK, TOK)
        centre = jnp.sum(grad_probs * probs, 1, keepdims=True)
        grad_scores = (probs * (grad_probs - centre)).astype(bf16)
        flat_scores = grad_scores.reshape(heads * TOK, TOK)
        grad_queries = by_heads(keys.T, grad_scores).T
        grad_keys = gathered(dot(flat_scores, queries))
        grad_values = gathered(dot(probs.astype(bf16).reshape(heads * TOK, TOK), grad_heads))
        grad = jnp.concatenate([SCALE * grad_queries, SCALE * grad_keys, grad_values], 1).astype(bf16)
        grad_up = tdot(low_qkv, grad)
        for i in range(3):
            ranks[:, i * C + b * wide : i * C + (b + 1) * wide] = grad_up[:, i * wide : (i + 1) * wide]
        grad_low_qkv = grad_low_qkv + dot_t(grad, qkv_up[b])
        grad_shifted = grad_shifted + dot_t(grad, whole_a[b, :, : 3 * wide])
    spread_qkv = over_lanes(grad_low_qkv.astype(bf16))
    grad_shifted = grad_shifted + dot_t(spread_qkv, qkv_down[...].reshape(C, LANES))
    grad = grad_residual + norm_back(grad_shifted, gain, unit, scale)
    keep_out[...] = grad[: TOK // 2].astype(bf16)
    away_out[...] = grad[TOK // 2 :].astype(bf16)
    take("pay")
    tile = held["pay"].shape[0]
    stage[:tile] = held["pay"][...].astype(f32)
    tile = pack_flat(stage, tile, flat, C // 8)
    tile = pack_ranks(stage, tile, tdot(low_proj_in[...], grad_attn))
    tile = pack_ranks(stage, tile, ranks[...])
    flat[...] = fold(tdot(shifted, spread_qkv))
    pack_flat(stage, tile, flat, C // 8)
    pay_out[...] = jnp.swapaxes(stage[...], 0, 1).astype(bf16)


PAY = 16 * C * RANK // OWNERS // LANES


def backward(near, **far):
    half = jax.ShapeDtypeStruct((TOK // 2, C), bf16)
    far = [far[name] for name in FAR_BACK]
    return pl.pallas_call(
        backward_kernel,
        out_shape=[half, half, jax.ShapeDtypeStruct((OWNERS, PAY, LANES), bf16)],
        in_specs=[HBM] * len(far) + [VM] * len(near),
        out_specs=[VM] * 3,
        scratch_shapes=scratch_of(far)
        + [
            pltpu.VMEM((PAY, OWNERS, LANES), f32),
            pltpu.VMEM((C // 8, LANES), f32),
            pltpu.VMEM((RANK, 3 * C), f32),
            pltpu.SemaphoreType.DMA((len(FAR_BACK),)),
        ],
        compiler_params=params(16),
        cost_estimate=cost(14),
        name="backward",
    )(*in_hbm(far), *near)


WIDTHS = (12, 12, 3, 3, 3, 3, 9, 3)


def sums_kernel(terms, pick, grad_main, grad_fc2, grad_qkv, grad_fc1, grad_out):
    by_tile = jnp.swapaxes(terms[...].astype(f32), 0, 1).astype(bf16)
    targets = (grad_fc2, grad_fc1, grad_out.at[1], grad_main.at[2], grad_main.at[1], grad_out.at[0], grad_qkv, grad_main.at[0])
    tile = 0
    for target, width in zip(targets, WIDTHS):
        for k in range(width):
            target[:, k * LANES : (k + 1) * LANES] = dot(pick[...], by_tile[tile])
            tile += 1


def sums(terms, pick):
    shapes = [(3, ADAPT, 3 * LANES), (ADAPT, 12 * LANES), (ADAPT, 9 * LANES), (ADAPT, 12 * LANES), (2, ADAPT, 3 * LANES)]
    main, fc2, qkv, fc1, out = pl.pallas_call(
        sums_kernel,
        out_shape=[jax.ShapeDtypeStruct(v, f32) for v in shapes],
        in_specs=[VM] * 2,
        out_specs=[VM] * 5,
        compiler_params=params(8),
        cost_estimate=cost(3),
        name="sums",
    )(terms, *in_hbm([pick]))
    return main.transpose(1, 0, 2), fc2, qkv, fc1, out.transpose(1, 0, 2)


def per_device(
    tokens,
    cotangent,
    adapter_id,
    valid_flag,
    regions,
    w_qkv,
    b_qkv,
    rel_table,
    w_proj,
    b_proj,
    w_fc1,
    b_fc1,
    w_fc2,
    b_fc2,
    norm_gains,
    norm_shifts,
    down_main,
    down_fc2,
    up_qkv,
    up_fc1,
    up_out,
):
    z_count, t_count = lax.axis_size("img"), lax.axis_size("tp")
    images, height, breadth = tokens.shape[:3]
    across = breadth // WIN
    wide = rel_table.shape[1] * HD
    count = 2 * z_count * t_count

    groups = [Group() for _ in range(3)]
    if z_count == 4:
        w_planes = w_qkv.transpose(1, 0, 2)
        piece = begin(adapter_id, w_planes, w_proj, w_fc1, w_fc2.T, b_qkv, b_fc1, rel_table.T)
        own_a, own, away = cut_windows(tokens, cotangent, w_planes, w_proj)
        arrays = [own_a, w_fc1, w_fc2.T]
        for n, group in enumerate(groups):
            group.add(n, 0, 2 * HALF, 0, 0, None, 0)
        cut = PIECE // 2
        upper = swap_ctx(away)
        along = [piece, shift_img(piece, 1)]
        by_x, by_y = swap_x(piece), swap_y(piece)
        gate = (along[1], by_x, by_y, upper)
        relayed = ()
        for k in (1, 2, 3):
            held = after(along[k], *gate)
            swapped = len(arrays)
            spread(groups, arrays, held, [(0, PIECE, 0, k, 0)])
            end = PIECE + SMALL if k == 1 else PIECE
            half_x, half_y = after(by_x[:cut], *gate), after(by_y[cut:end], *gate)
            old_x, old_y = by_x, by_y
            by_x = swap_x(jnp.concatenate([held[:PIECE], half_y], 0))
            by_y = swap_y(after(jnp.concatenate([held[:PIECE], half_x], 0), arrays[-1]))
            if k == 2:
                smalls = jnp.concatenate(
                    [piece[PIECE:], first_x[PIECE:], first_y[PIECE:], old_x[-SMALL:]], 0
                )
                additive, mask, bias_qkv, bias_fc1 = biases(regions, after(smalls, arrays[-1]))
                held = after(held, additive)
            if k < 3:
                along.append(shift_img(held, 1))
            if k == 3:
                rows = jnp.concatenate([v[PIECE:] for v in along], 0)
                chosen, pick = choose(
                    after(rows, arrays[-1]), down_main.transpose(1, 0, 2), down_fc2, up_qkv, up_fc1, up_out.transpose(1, 0, 2)
                )
                mine = lax.all_to_all(chosen, "img", 0, 0, tiled=True)
            near = [(0, PIECE, 0, k - 1, 1)], [(0, PIECE, 0, k - 1, 2)]
            if k > 1:
                near[0].append((PIECE, cut, cut, k - 2, 3))
                near[1].append((PIECE, cut, 0, k - 2, 3))
            for array, parts in ((old_x, near[0]), (old_y, near[1])):
                spread(groups, arrays, array, parts)
            if k == 1:
                first_x, first_y = old_x, old_y
            if k == 2:
                corner = jnp.concatenate([old_y[PIECE : PIECE + cut], old_x[PIECE : PIECE + cut]], 0)
            if k == 3:
                last = shift_img(after(corner, *gate), -1)
            gate = (by_x, by_y, *along[k + 1 :], *arrays[swapped:])
        theirs = swap_ctx(mine)
        spread(groups, arrays, by_x, [(0, PIECE, 0, 3, 1), (PIECE, cut, cut, 2, 3)])
        spread(groups, arrays, by_y, [(0, PIECE, 0, 3, 2), (PIECE, cut, 0, 2, 3)])
        spread(groups, arrays, last, [(0, PIECE, 0, 3, 3)])
    else:
        c, t = lax.axis_index("ctx"), lax.axis_index("tp")
        image, column = t // across, t % across
        both = jnp.stack([lax.dynamic_index_in_dim(a, image, 0, False) for a in (tokens, cotangent)])
        both = lax.dynamic_slice_in_dim(jnp.roll(both, -SHIFT, 2), column * WIN, WIN, 2)
        own = both[:, SHIFT:].reshape(2, TOK // 2, C)
        upper = swap_ctx(both[:, :SHIFT].reshape(2, TOK // 2, C))
        own_a = jnp.concatenate([w_qkv.reshape(-1, 3 * wide), w_proj.T], 1)
        arrays = []
        for group, weights in zip(groups, (own_a, w_fc1, w_fc2.T)):
            for j, array in enumerate(spread_far(weights)):
                group.add(len(arrays), 0, C, None, j, None, 0)
                arrays.append(array)
        ids = lax.all_gather(adapter_id, "img")
        parts = [down_main[:, i] for i in range(3)] + [down_fc2, up_qkv, up_fc1] + [up_out[:, i] for i in range(2)]
        tables = jnp.concatenate(parts, 1)
        wanted = lax.dynamic_index_in_dim(ids, image, 1, False)
        pick = (wanted[:, None] == jnp.arange(ADAPT)[None, :]).astype(bf16)
        mine = lax.all_to_all(dot(pick, tables).astype(bf16), "img", 0, 0, tiled=True)
        theirs = swap_ctx(mine)
        mine, theirs = jnp.where(c == 0, mine, theirs), jnp.where(c == 0, theirs, mine)
        owned = jnp.stack([mine, theirs], 1).reshape(2 * z_count, -1)
        sizes = [v.shape[1] for v in parts]
        cuts = [sum(sizes[:i]) for i in range(9)]
        owned = jnp.concatenate([owned[:, a:b].reshape(SHARDS, -1) for a, b in zip(cuts, cuts[1:])], 1)
        owned = owned.reshape(SHARDS, C // LANES, 32, LANES).transpose(0, 2, 1, 3).reshape(SHARDS // 2, 2, 32, C)
        mine, theirs = jnp.where(c == 0, owned[:, 0], owned[:, 1]), jnp.where(c == 0, owned[:, 1], owned[:, 0])
        source = jnp.broadcast_to(ids[:, None, :, None], (z_count, 2, images, across)).reshape(-1)
        pick = (jnp.arange(ADAPT)[:, None] == source[None, :]).astype(bf16)

        def rows_of(field, rows):
            return jnp.pad(field, ((0, rows - field.shape[0]), (0, C - field.shape[1])))

        small = jnp.concatenate([rows_of(b_qkv, 3), b_fc1[None], jnp.zeros((4, C), bf16), rows_of(rel_table.T, 8)], 0)
        smalls = jnp.concatenate([small, swap_x(small), swap_y(small), swap_xy(small)], 0)
        additive, mask, bias_qkv, bias_fc1 = biases(regions, smalls)
    keep, away, pay, *near = forward(
        groups, arrays, strips=additive, joined=join(mine, theirs), valid=valid_flag, own=own, upper=upper,
        gains=norm_gains, offsets=norm_shifts, bias_qkv=bias_qkv, mask=mask, bias_proj=b_proj,
        bias_fc1=bias_fc1, bias_fc2=b_fc2,
    )

    def moved(keep, away):
        half = jnp.concatenate([swap_ctx(away), keep], 0)
        return [half, swap_x(half), swap_y(half), swap_xy(half)]

    def placed(pieces, dtype):
        return place(pieces, dtype).reshape(images, height, breadth, C)

    outputs = moved(keep, away)
    keep, away, pay = backward(
        near, valid=valid_flag, own=own, upper=upper, gains=norm_gains, offsets=norm_shifts, pay=pay
    )
    keep, away, pay, *outputs = lax.optimization_barrier((keep, away, pay, *outputs))
    grads = moved(keep, away)
    output = placed(outputs, bf16)

    if count == OWNERS:
        added = sums(lax.all_to_all(pay, ("img", "ctx", "tp"), 0, 0, tiled=True), pick)
    else:
        cuts = [LANES * sum(WIDTHS[:i]) for i in range(9)]
        pay = pay.reshape(OWNERS, PAY * LANES)
        pay = jnp.concatenate([pay[:, a:b].reshape(count, -1) for a, b in zip(cuts, cuts[1:])], 1)
        cuts = [v * OWNERS // count for v in cuts]
        totals = dot(pick, lax.all_to_all(pay, ("img", "ctx", "tp"), 0, 0, tiled=True))
        fc2, fc1, out1, main2, main1, out0, qkv, main0 = (totals[:, a:b] for a, b in zip(cuts, cuts[1:]))
        added = jnp.stack([main0, main1, main2], 1), fc2, qkv, fc1, jnp.stack([out0, out1], 1)
    grads = [after(grads[0], added[0], output), *grads[1:]]
    return (output, placed(grads, f32), *added)


def solution(mesh):
    in_specs = (
        P("img", "ctx", None, None),
        P("img", "ctx", None, None),
        P("img"),
        P("img"),
        P("ctx", None),
        P("img", None, "tp"),
        P(None, "tp"),
        P(None, "tp"),
        P("tp", "img"),
        P(),
        P("img", "tp"),
        P("tp"),
        P("tp", "img"),
        P(),
        P(),
        P(),
        P(None, None, ("img", "ctx")),
        P(None, ("img", "ctx")),
        P(None, ("img", "ctx")),
        P(None, ("img", "ctx")),
        P(None, None, ("img", "ctx")),
    )
    out_specs = (
        P("img", "ctx", None, None),
        P("img", "ctx", None, None),
        P(None, None, ("img", "ctx", "tp")),
        P(None, ("img", "ctx", "tp")),
        P(None, ("img", "ctx", "tp")),
        P(None, ("img", "ctx", "tp")),
        P(None, None, ("img", "ctx", "tp")),
    )
    return jax.shard_map(
        per_device, mesh=mesh, in_specs=in_specs, out_specs=out_specs, check_vma=False
    )
```

```python
import jax
import jax.numpy as jnp
from jax import lax
from jax.experimental import pallas as pl
from jax.experimental.pallas import tpu as pltpu
from jax.sharding import PartitionSpec as P

C = 768
HD = 32
FF = 3072
WIN = 12
SHIFT = 6
RANK = 16
ADAPT = 8
RELS = 529
TOK = WIN * WIN
SCALE = HD ** (-0.5)
EPS = 1e-05
LANES = 128
SHARDS = 8
OWNERS = 32

bf16 = jnp.bfloat16
f32 = jnp.float32

VM = pl.BlockSpec(memory_space=pltpu.VMEM)
SM = pl.BlockSpec(memory_space=pltpu.SMEM)
HBM = pl.BlockSpec(memory_space=pltpu.HBM)


def params(mib):
    return pltpu.CompilerParams(vmem_limit_bytes=mib << 20)


def in_hbm(arrays):
    return [pltpu.with_memory_space_constraint(v, pltpu.HBM) for v in arrays]


def in_hbm_out(shape, dtype):
    return pltpu.HBM(shape, dtype)


def here():
    z, c, t = (lax.axis_index(name) for name in ("img", "ctx", "tp"))
    return z, c, t, lax.div(t, 2), lax.rem(t, 2)


def cost(us):
    return pl.CostEstimate(flops=0, transcendentals=0, bytes_accessed=int(us * 3e6))


def dot(left, right):
    return jnp.dot(left, right, preferred_element_type=f32)


def dot_t(left, right):
    return lax.dot_general(left, right, (((1,), (1,)), ((), ())), preferred_element_type=f32)


def tdot(left, right):
    return lax.dot_general(left, right, (((0,), (0,)), ((), ())), preferred_element_type=f32)


def swap_ctx(v):
    return lax.ppermute(v, "ctx", [(0, 1), (1, 0)])


def swap_x(v):
    return lax.ppermute(v, "tp", [(0, 1), (1, 0), (2, 3), (3, 2)])


def swap_y(v):
    return lax.ppermute(v, "tp", [(0, 2), (2, 0), (1, 3), (3, 1)])


def swap_xy(v):
    return lax.ppermute(v, "tp", [(0, 3), (3, 0), (1, 2), (2, 1)])


def after(v, *others):
    return lax.optimization_barrier((v,) + others)[0]


def shift_img(v, k):
    count = lax.axis_size("img")
    return lax.ppermute(v, "img", [(i, (i + k) % count) for i in range(count)])


HALF = 96
PIECE = 3 * HALF
SMALL = 16


class Group:
    def __init__(self):
        self.plan, self.places = [], []

    def add(self, index, at, rows, k, j, core, first):
        self.plan.append((index, at, rows))
        self.places.append((k, j, core, first))


def spread(groups, arrays, held, parts):
    for core, array in enumerate((held, swap_ctx(held))):
        for at, rows, top, k, j in parts:
            for n, group in enumerate(groups):
                first, last = max(top, n * HALF), min(top + rows, (n + 1) * HALF)
                if first < last:
                    group.add(len(arrays), at + first - top, last - first, k, j, core, first - n * HALF)
        arrays.append(array)


def spread_far(own):
    whole = lax.all_gather(own, "img", axis=0, tiled=True)
    by_x = swap_x(whole)
    return [whole, by_x, swap_y(whole), swap_y(by_x)]


def norm_parts(field):
    average = jnp.mean(field, -1, keepdims=True)
    centred = field - average
    variance = jnp.mean(centred * centred, -1, keepdims=True)
    scale = lax.rsqrt(variance + EPS)
    return centred * scale, scale


def norm_back(grad, gain, unit, scale):
    scaled = grad * gain
    return scale * (
        scaled
        - jnp.mean(scaled, -1, keepdims=True)
        - unit * jnp.mean(scaled * unit, -1, keepdims=True)
    )


def start(group_refs, group, whole, sems, only=None):
    z, c, t, _, _ = here()
    count = lax.axis_size("img")
    rows_each = C // count
    for (index, at, rows), (k, j, core, first) in zip(group.plan, group.places):
        if only not in (None, j):
            continue
        source = group_refs[index].at[pl.ds(at, rows), :]
        top = 0 if k is None else lax.rem(z + (count - k), count) * rows_each + first
        if core is not None:
            top = top + (c ^ core) * (rows_each // 2)
        block = t ^ j
        target = whole.at[block, pl.ds(pl.multiple_of(top, 16), rows), :]
        pltpu.make_async_copy(source, target, sems.at[block]).start()


def finish(whole, sems, block):
    pltpu.make_async_copy(whole.at[block], whole.at[block], sems.at[block]).wait()


def lane_group(rows):
    lane = lax.broadcasted_iota(jnp.int32, (rows, LANES), 1) // RANK
    row = lax.broadcasted_iota(jnp.int32, (rows, LANES), 0) % 8
    return (lane == row).astype(f32)


def low_of(spread_sum):
    for step in (64, 32, 16):
        spread_sum = spread_sum + pltpu.roll(spread_sum, step, 1)
    return spread_sum[:, :RANK].astype(bf16)


def over_lanes(low):
    lane = lax.broadcasted_iota(jnp.int32, (RANK, LANES), 1) % RANK
    rank = lax.broadcasted_iota(jnp.int32, (RANK, LANES), 0)
    return dot(low, (lane == rank).astype(bf16)).astype(bf16)


def fold(product):
    rows = product.shape[0]
    kept = (product * lane_group(rows)).reshape(rows // 8, 8, LANES)
    return jnp.sum(kept, 1)


def put_ranks(stage, tile, h, grad):
    for k in range(grad.shape[1] // LANES):
        stage[tile + k, pl.ds(h, RANK, stride=2), :] = grad[:, k * LANES : (k + 1) * LANES]


def pack_ranks(stage, tile, grad):
    width = grad.shape[1] // 2
    for h in range(2):
        put_ranks(stage, tile, h, grad[:, h * width : (h + 1) * width])
    return tile + width // LANES


def pack_flat(stage, tile, flat, rows):
    each = rows // OWNERS
    for k in range(each):
        stage[tile + k] = flat[pl.ds(k, OWNERS, stride=each), :]
    return tile + each


def begin_kernel(ids, w_qkv, w_proj, w_fc1, w_fc2, b_qkv, b_fc1, rel, piece, ids_here, held_qkv, held_proj, held_bq, held_b1, held_rel, small, sems):
    c = here()[1]
    half = pl.ds(pl.multiple_of(c * HALF, 16), HALF)
    moves = (
        (w_qkv.at[:, half, :], held_qkv),
        (w_proj, held_proj),
        (b_qkv, held_bq),
        (b_fc1, held_b1),
        (rel, held_rel),
        (ids, ids_here),
        (w_fc1.at[half, :], piece.at[pl.ds(HALF, HALF), :]),
        (w_fc2.at[half, :], piece.at[pl.ds(2 * HALF, HALF), :]),
    )
    copies = [pltpu.make_async_copy(*move, sems.at[i]) for i, move in enumerate(moves)]
    for copy in copies:
        copy.start()
    lane = lax.broadcasted_iota(jnp.int32, (1, C), 1)
    small[...] = jnp.zeros_like(small)
    for copy in copies[:6]:
        copy.wait()
    proj = held_proj[...].T
    proj = jnp.where(c == 0, proj[:HALF], proj[HALF:])
    piece[:HALF] = jnp.concatenate([held_qkv[0], held_qkv[1], held_qkv[2], proj], 1)
    small[:3, : b_qkv.shape[1]] = held_bq[...].astype(f32)
    small[3:4, :] = held_b1[...].astype(f32).reshape(1, C)
    first, second = ids_here[0].astype(f32), ids_here[1].astype(f32)
    small[4:5, :] = jnp.where(lane == 0, first, jnp.where(lane == 1, second, 0.0))
    small[8 : 8 + rel.shape[0], : rel.shape[1]] = held_rel[...].astype(f32)
    piece[PIECE:] = small[...].astype(bf16)
    for copy in copies[6:]:
        copy.wait()


def begin(ids, *args):
    w_qkv, w_proj, _, _, b_qkv, b_fc1, rel = (v.shape for v in args)
    held = [(3, HALF, w_qkv[2]), w_proj, b_qkv, b_fc1, rel]
    return pl.pallas_call(
        begin_kernel,
        out_shape=jax.ShapeDtypeStruct((PIECE + SMALL, C), bf16),
        in_specs=[HBM] * (1 + len(args)),
        out_specs=VM,
        scratch_shapes=[pltpu.SMEM((2,), jnp.int32)]
        + [pltpu.VMEM(v, bf16) for v in held]
        + [pltpu.VMEM((SMALL, C), f32), pltpu.SemaphoreType.DMA((8,))],
        compiler_params=params(6),
        name="begin",
    )(*in_hbm([ids, *args]))


def cut_kernel(tokens, cotangent, w_qkv, w_proj, own_a, own, away, image, held_qkv, held_proj, sems):
    at, column = here()[3:]
    moves = (
        (w_qkv, held_qkv),
        (w_proj, held_proj),
        (tokens.at[at], image.at[0]),
        (cotangent.at[at], image.at[1]),
    )
    copies = [pltpu.make_async_copy(*move, sems.at[i]) for i, move in enumerate(moves)]
    for copy in copies:
        copy.start()
    for copy in copies[:2]:
        copy.wait()
    own_a[...] = jnp.concatenate([held_qkv[0], held_qkv[1], held_qkv[2], held_proj[...].T], 1)
    for i, copy in enumerate(copies[2:]):
        copy.wait()
        block = image[i].astype(f32)
        rows = []
        for r in range(WIN):
            at = r * 2 * WIN
            inner = block[at + SHIFT : at + SHIFT + WIN]
            outer = jnp.concatenate([block[at + SHIFT + WIN : at + 2 * WIN], block[at : at + SHIFT]], 0)
            rows.append(jnp.where(column == 0, inner, outer))
        away[i] = jnp.concatenate(rows[:SHIFT], 0).astype(bf16)
        own[i] = jnp.concatenate(rows[SHIFT:], 0).astype(bf16)


def cut_windows(tokens, cotangent, w_qkv, w_proj):
    flat = (tokens.shape[0], -1, C)
    windows = (2, TOK // 2, C)
    return pl.pallas_call(
        cut_kernel,
        out_shape=[in_hbm_out((2 * HALF, C), bf16), in_hbm_out(windows, bf16), jax.ShapeDtypeStruct(windows, bf16)],
        in_specs=[HBM] * 4,
        out_specs=[VM] * 3,
        scratch_shapes=[
            pltpu.VMEM((2, 2 * TOK, C), bf16),
            pltpu.VMEM(w_qkv.shape, bf16),
            pltpu.VMEM(w_proj.shape, bf16),
            pltpu.SemaphoreType.DMA((4,)),
        ],
        compiler_params=params(10),
        name="cut_windows",
    )(*in_hbm([tokens.reshape(flat), cotangent.reshape(flat), w_qkv, w_proj]))


def place_kernel(*refs):
    pieces, out, held = refs[:4], refs[4], refs[5]
    t = here()[2]
    for j, piece in enumerate(pieces):
        held[t ^ j] = piece[...].astype(f32)
    for i in range(2):
        left, right = held[2 * i], held[2 * i + 1]
        for r in range(WIN):
            rows = slice(r * WIN, (r + 1) * WIN)
            inner, outer = left[rows], right[rows]
            line = jnp.concatenate([outer[SHIFT:], inner, outer[:SHIFT]], 0)
            out[i, r * 2 * WIN : (r + 1) * 2 * WIN] = line.astype(out.dtype)


def place(pieces, dtype):
    return pl.pallas_call(
        place_kernel,
        out_shape=jax.ShapeDtypeStruct((2, 2 * TOK, C), dtype),
        in_specs=[VM] * 4,
        out_specs=VM,
        scratch_shapes=[pltpu.VMEM((4, TOK, C), f32)],
        compiler_params=params(8),
        cost_estimate=cost(2),
        name="place",
    )(*pieces)


TILES = 12 * RANK


def choose_kernel(*refs):
    held, tables, (chosen_out, pick), (table, stage, sems) = refs[0], refs[1:6], refs[6:8], refs[8:]
    z, _, _, image, _ = here()
    copies = []
    col = 0
    for field in tables:
        for i in range(1 if len(field.shape) == 2 else field.shape[0]):
            source = field if len(field.shape) == 2 else field.at[i]
            width = source.shape[1]
            copies.append(pltpu.make_async_copy(source, table.at[:, pl.ds(col, width)], sems.at[len(copies)]))
            col += width
    for copy in copies:
        copy.start()
    source = lax.broadcasted_iota(jnp.int32, pick.shape, 1)
    owner = jnp.zeros(pick.shape, f32)
    wanted = []
    for k in range(4):
        known = held[-k % 4 * 16 : -k % 4 * 16 + 16, :].astype(f32)[4:5]
        lane = lax.broadcasted_iota(jnp.int32, known.shape, 1)
        ids = [jnp.sum(jnp.where(lane == i, known, 0.0), 1, keepdims=True) for i in range(2)]
        at = lax.rem(z + k, 4)
        owner = jnp.where(source // 8 == at, jnp.where(source % 4 < 2, ids[0], ids[1]), owner)
        wanted.append(jnp.where(image == 0, ids[0], ids[1]))
    pick[...] = (lax.broadcasted_iota(jnp.int32, pick.shape, 0).astype(f32) == owner).astype(bf16)
    for copy in copies:
        copy.wait()
    for tile in range(TILES):
        field = table[:, tile * LANES : (tile + 1) * LANES].astype(f32)
        row = lax.broadcasted_iota(jnp.int32, field.shape, 0).astype(f32)
        for k in range(4):
            chosen = jnp.sum(jnp.where(row == wanted[k], field, 0.0), 0, keepdims=True)
            stage[k, tile : tile + 1, :] = chosen
    for k in range(4):
        at = lax.rem(z + k, 4)
        for i in range(C // LANES):
            chosen_out[at, :, i * LANES : (i + 1) * LANES] = stage[k, i * 32 : (i + 1) * 32, :].astype(bf16)


def choose(held, *tables):
    return pl.pallas_call(
        choose_kernel,
        out_shape=[jax.ShapeDtypeStruct((4, 32, C), bf16), in_hbm_out((ADAPT, OWNERS), bf16)],
        in_specs=[VM] + [HBM] * 5,
        out_specs=[VM] * 2,
        scratch_shapes=[
            pltpu.VMEM((ADAPT, TILES * LANES), bf16),
            pltpu.VMEM((4, TILES, LANES), f32),
            pltpu.SemaphoreType.DMA((8,)),
        ],
        compiler_params=params(4),
        cost_estimate=cost(0.1),
        name="choose",
    )(held, *in_hbm(tables))


def expand_adapters(joined, qkv_down, proj_down, fc1_down, fc2_down, qkv_up, fc1_up, proj_up, fc2_up, ranks):
    for shard in range(SHARDS):
        rows = joined[shard].astype(f32)
        tiles = jnp.concatenate([rows[:, i * LANES : (i + 1) * LANES] for i in range(C // LANES)], 0)
        row = 0
        for out in (qkv_down, proj_down, fc1_down, fc2_down):
            rows = out.shape[1]
            part = tiles[row : row + rows // 8]
            spread = jnp.broadcast_to(part[:, None, :], (rows // 8, 8, LANES)).reshape(rows, LANES)
            out[shard] = (spread * lane_group(rows)).astype(bf16)
            row += rows // 8
        tile = 0
        for width in (3 * C, FF, C, C):
            for e in range(2):
                for k in range(width // LANES):
                    ranks[tile + k, 2 * shard + e : 2 * shard + e + 1, :] = tiles[row : row + 1]
                    row += 1
            tile += width // LANES
    wide = C // 4
    tile = 3 * C // LANES
    table = jnp.concatenate([ranks[k] for k in range(tile)], 1)
    for b in range(4):
        parts = [table[:, i * C + b * wide : i * C + (b + 1) * wide] for i in range(3)]
        qkv_up[b] = jnp.concatenate(parts, 1).astype(bf16)
    for out in (fc1_up, proj_up, fc2_up):
        for k in range(out.shape[1] // LANES):
            out[:, k * LANES : (k + 1) * LANES] = ranks[tile + k].astype(bf16)
        tile += out.shape[1] // LANES


def join_kernel(mine, theirs, out):
    c = here()[1]
    for n in range(SHARDS // 2):
        out[2 * n + c] = mine[n]
        out[2 * n + (c ^ 1)] = theirs[n]


def join(mine, theirs):
    return pl.pallas_call(
        join_kernel,
        out_shape=in_hbm_out((SHARDS, 32, C), bf16),
        in_specs=[VM, VM],
        out_specs=VM,
        compiler_params=params(4),
        name="join",
    )(mine, theirs)


SPAN = 2 * WIN - 1
STRIP = 3 * LANES


ENTRIES = 5 * LANES


def bias_kernel(regions, held, strips, mask_out, bias_qkv, bias_fc1):
    _, _, t, _, column = here()
    wide = C // 4
    heads = wide // HD
    lane = lax.broadcasted_iota(jnp.int32, (ENTRIES, STRIP), 1)
    entry = lax.broadcasted_iota(jnp.int32, (ENTRIES, STRIP), 0)
    chosen = (entry == (lane // WIN) * SPAN + lane % WIN + WIN - 1).astype(bf16)
    tables = []
    for j in range(4):
        field = held[16 * j : 16 * (j + 1), :].astype(f32)
        block = t ^ j
        bias_qkv[block] = jnp.concatenate([field[i : i + 1, :wide] for i in range(3)], 1)
        bias_fc1[block] = field[3:4]
        tables.append(field[8:, :ENTRIES])
    table = jnp.concatenate(tables, 0)
    rolled = [pltpu.roll(table, key, 1) if key else table for key in range(WIN)]
    all_strips = dot(jnp.concatenate(rolled, 0).astype(bf16), chosen)
    for key in range(WIN):
        strip = all_strips[key * table.shape[0] : (key + 1) * table.shape[0]]
        for j in range(4):
            for h in range(heads):
                strips[t ^ j, h, key : key + 1, :] = strip[8 * j + h : 8 * j + h + 1]
    row = lax.broadcasted_iota(jnp.int32, (TOK, WIN), 0) // WIN
    at_row = (row == lax.broadcasted_iota(jnp.int32, (TOK, WIN), 1)).astype(bf16)
    lines = dot(at_row, regions[...].astype(f32).astype(bf16))
    cell = lax.broadcasted_iota(jnp.int32, lines.shape, 0) % WIN + column * WIN
    lines = jnp.where(cell == lax.broadcasted_iota(jnp.int32, lines.shape, 1), lines, 0.0)
    by_key = jnp.sum(lines, 1, keepdims=True)
    by_query = dot_t(jnp.ones((8, lines.shape[1]), bf16), lines.astype(bf16))[:1]
    mask_out[...] = jnp.where(by_key == by_query, 0.0, -100.0)


def placed_biases(strips):
    strip = strips[:WIN]
    return jnp.concatenate([strip[:, (WIN - 1 - r) * WIN : (WIN - 1 - r) * WIN + TOK] for r in range(WIN)], 0)


def biases(regions, smalls):
    heads = C // HD
    return pl.pallas_call(
        bias_kernel,
        out_shape=[
            in_hbm_out((4, heads // 4, 16, STRIP), f32),
            in_hbm_out((TOK, TOK), f32),
            in_hbm_out((4, 1, 3 * C // 4), f32),
            in_hbm_out((4, 1, FF // 4), f32),
        ],
        in_specs=[VM] * 2,
        out_specs=[VM] * 4,
        compiler_params=params(12),
        cost_estimate=cost(0.1),
        name="biases",
    )(*in_hbm([regions]), smalls)


def head_mask(head):
    lane = lax.broadcasted_iota(jnp.int32, (TOK, C // 4), 1) // HD
    return lane == head


def only(head, field):
    return jnp.where(head_mask(head), field, jnp.zeros_like(field))


def stacked(field):
    return jnp.concatenate([only(h, field) for h in range(C // 4 // HD)], 0)


def gathered(product):
    total = jnp.zeros((TOK, C // 4), f32)
    for h in range(C // 4 // HD):
        total = jnp.where(head_mask(h), product[h * TOK : (h + 1) * TOK], total)
    return total


def by_heads(field, probs):
    parts = [dot(field[h * HD : (h + 1) * HD], probs[h]) for h in range(C // 4 // HD)]
    return jnp.concatenate(parts, 0)


def row_of(ref, held, sem):
    copy = pltpu.make_async_copy(ref, held, sem)
    copy.start()
    return copy


FAR = (
    "joined", "valid", "own", "upper", "gains", "offsets", "bias_qkv", "mask", "strips", "bias_proj",
    "bias_fc1", "bias_fc2",
)
FAR_BACK = ("valid", "own", "upper", "gains", "offsets", "pay")


def loading(names, far, held, sems):
    loads = {name: pltpu.make_async_copy(far[name], held[name], sems.at[n]) for n, name in enumerate(names)}

    def take(*wanted):
        for name in wanted:
            loads[name].wait()

    return loads, take


def forward_kernel(group_a, group_b, group_c, count, *refs):
    far, refs = dict(zip(FAR, refs)), refs[len(FAR) :]
    pieces, refs = refs[:count], refs[count:]
    keep_out, away_out, pay_out, residual_out, low_qkv_out, low_proj_out, all_mixed, all_probs, all_attended = refs[:9]
    whole_a, qkv_down, proj_down, qkv_up, proj_up = refs[9:14]
    held, refs = dict(zip(FAR, refs[14:])), refs[14 + len(FAR) :]
    whole_b, whole_c, sems_a, sems_b, sems_c, hidden, slope, stage, flat, more, fc1_down, fc2_down, fc1_up, fc2_up, ranks = refs
    loads, take = loading(FAR, far, held, more)
    for name in FAR[:9]:
        loads[name].start()
    t = here()[2]
    blocks = [t ^ j for j in range(4)]
    for j in range(2):
        start(pieces, group_a, whole_a, sems_a, j)
    wide = C // 4
    heads = wide // HD

    take("joined")
    expand_adapters(
        held["joined"], qkv_down, proj_down, fc1_down, fc2_down, qkv_up, fc1_up, proj_up, fc2_up, ranks
    )
    take("valid", "own", "upper", "gains", "offsets")
    flag = held["valid"][here()[3]].astype(f32)
    gains, offsets = held["gains"][...].astype(f32), held["offsets"][...].astype(f32)
    inputs = jnp.concatenate([held["own"][0], held["upper"][0]], 0).astype(f32)
    unit, _ = norm_parts(inputs)
    shifted = (unit * gains[0:1] + offsets[0:1]).astype(bf16)
    take("bias_qkv")
    low_qkv = low_of(dot(shifted, qkv_down[...].reshape(C, LANES)))
    low_qkv_out[...] = low_qkv
    total = jnp.zeros((TOK, C), f32)
    low_total = jnp.zeros((TOK, LANES), f32)
    for j, b in enumerate(blocks):
        finish(whole_a, sems_a, b)
        if j < 2:
            start(pieces, group_a, whole_a, sems_a, j + 2)
        elif j == 2:
            start(pieces, group_b, whole_b, sems_b)
            for name in FAR[9:]:
                loads[name].start()
        mixed = dot(shifted, whole_a[b, :, : 3 * wide]) + held["bias_qkv"][b] + dot(low_qkv, qkv_up[b])
        mixed = mixed.astype(bf16)
        all_mixed[b] = mixed
        queries, keys, values = (mixed[:, i * wide : (i + 1) * wide] for i in range(3))
        if j == 0:
            take("mask", "strips")
        biases_here = [placed_biases(held["strips"][b, h]) + held["mask"][...] for h in range(heads)]
        scores = SCALE * dot_t(stacked(keys), queries).reshape(heads, TOK, TOK) + jnp.stack(biases_here)
        weight = jnp.exp(scores - jnp.max(scores, 1, keepdims=True))
        probs = weight / jnp.sum(weight, 1, keepdims=True)
        all_probs[b] = probs
        attended = by_heads(values.T, probs.astype(bf16)).astype(bf16).T
        all_attended[b] = attended
        total = total + dot_t(attended, whole_a[b, :, 3 * wide :])
        low_total = low_total + dot(attended, proj_down[pl.ds(2 * b, 2)].reshape(wide, LANES))
    low_proj = low_of(low_total)
    low_proj_out[...] = low_proj
    take("bias_proj")
    branch = total + held["bias_proj"][...].astype(f32).reshape(1, C) + dot(low_proj, proj_up[...])
    residual = inputs + flag * branch
    unit, _ = norm_parts(residual)
    field = (unit * gains[1:2] + offsets[1:2]).astype(bf16)
    low_fc1 = low_of(dot(field, fc1_down[...].reshape(C, LANES)))

    take("bias_fc1")
    low_total = jnp.zeros((TOK, LANES), f32)
    for b in range(4):
        cols = slice(b * C, (b + 1) * C)
        finish(whole_b, sems_b, b)
        if b == 0:
            start(pieces, group_c, whole_c, sems_c)
        preact = dot(field, whole_b[b]) + held["bias_fc1"][b] + dot(low_fc1, fc1_up[:, cols])
        cdf = 0.5 * (1.0 + lax.erf(preact * (0.5**0.5)))
        active = (preact * cdf).astype(bf16)
        hidden[b] = active
        slope[b] = cdf + preact * jnp.exp(-0.5 * preact * preact) * (0.5 / jnp.pi) ** 0.5
        low_total = low_total + dot(active, fc2_down[2 * b : 2 * b + 2].reshape(C, LANES))
    low_fc2 = low_of(low_total)

    take("bias_fc2")
    dz = jnp.concatenate([held["own"][1], held["upper"][1]], 0).astype(f32)
    branch = (flag * dz).astype(bf16)
    grad_low_fc2 = dot_t(branch, fc2_up[...]).astype(bf16)
    spread_fc2 = over_lanes(grad_low_fc2)
    grad_low_fc1 = jnp.zeros((TOK, RANK), f32)
    grad_normed = jnp.zeros((TOK, C), f32)
    total = jnp.zeros((TOK, C), f32)
    for b in range(4):
        cols = slice(b * C, (b + 1) * C)
        finish(whole_c, sems_c, b)
        total = total + dot_t(hidden[b], whole_c[b])
        grad_hidden = dot(branch, whole_c[b]) + dot_t(spread_fc2, fc2_down[2 * b : 2 * b + 2].reshape(C, LANES))
        grad_preact = (grad_hidden * slope[b]).astype(bf16)
        flat[b * C // 8 : (b + 1) * C // 8, :] = fold(tdot(hidden[b], spread_fc2))
        grad_up = tdot(low_fc1, grad_preact)
        width = FF // 2
        at = b * C % width
        put_ranks(stage, (FF // 2 + at) // LANES, b * C // width, grad_up)
        grad_low_fc1 = grad_low_fc1 + dot_t(grad_preact, fc1_up[:, cols])
        grad_normed = grad_normed + dot_t(grad_preact, whole_b[b])
    pack_flat(stage, 0, flat, FF // 8)
    tile = pack_ranks(stage, FF // LANES, tdot(low_fc2, branch))
    grad_low_fc1 = grad_low_fc1.astype(bf16)
    spread_fc1 = over_lanes(grad_low_fc1)
    grad_normed = grad_normed + dot_t(spread_fc1, fc1_down[...].reshape(C, LANES))
    bias = held["bias_fc2"][...].astype(f32).reshape(1, C)
    output = residual + flag * (total + bias + dot(low_fc2, fc2_up[...]))
    keep_out[...] = output[: TOK // 2].astype(bf16)
    away_out[...] = output[TOK // 2 :].astype(bf16)
    unit, scale = norm_parts(residual)
    residual_out[...] = dz + norm_back(grad_normed, held["gains"][1:2].astype(f32), unit, scale)
    flat[: C // 8, :] = fold(tdot(field, spread_fc1))
    pack_flat(stage, tile, flat, C // 8)
    pay_out[...] = stage[...].astype(bf16)


def scratch_of(far):
    return [(pltpu.SMEM if v.dtype == jnp.int32 else pltpu.VMEM)(v.shape, v.dtype) for v in far]


def forward(groups, arrays, **far):
    pay = ((FF + C) // LANES, OWNERS, LANES)
    half = jax.ShapeDtypeStruct((TOK // 2, C), bf16)
    wide = C // 4
    mixed, probs, attended = (4, TOK, 3 * wide), (4, wide // HD, TOK, TOK), (4, TOK, wide)
    far = [far[name] for name in FAR]
    return pl.pallas_call(
        lambda *refs: forward_kernel(*groups, len(arrays), *refs),
        out_shape=[
            half,
            half,
            in_hbm_out(pay, bf16),
            jax.ShapeDtypeStruct((TOK, C), f32),
            jax.ShapeDtypeStruct((TOK, RANK), bf16),
            jax.ShapeDtypeStruct((TOK, RANK), bf16),
            jax.ShapeDtypeStruct(mixed, bf16),
            jax.ShapeDtypeStruct(probs, f32),
            jax.ShapeDtypeStruct(attended, bf16),
            jax.ShapeDtypeStruct((4, C, C), bf16),
            jax.ShapeDtypeStruct((SHARDS, HALF, LANES), bf16),
            jax.ShapeDtypeStruct((SHARDS, HALF, LANES), bf16),
            jax.ShapeDtypeStruct((4, RANK, 3 * wide), bf16),
            jax.ShapeDtypeStruct((RANK, C), bf16),
        ],
        in_specs=[HBM] * (len(far) + len(arrays)),
        out_specs=[VM] * 14,
        scratch_shapes=scratch_of(far)
        + [pltpu.VMEM((4, C, C), bf16)] * 2
        + [pltpu.SemaphoreType.DMA((4,))] * 3
        + [
            pltpu.VMEM((4, TOK, C), bf16),
            pltpu.VMEM((4, TOK, C), f32),
            pltpu.VMEM(pay, f32),
            pltpu.VMEM((FF // 8, LANES), f32),
            pltpu.SemaphoreType.DMA((len(FAR),)),
            pltpu.VMEM((SHARDS, HALF, LANES), bf16),
            pltpu.VMEM((SHARDS, FF // SHARDS, LANES), bf16),
            pltpu.VMEM((RANK, FF), bf16),
            pltpu.VMEM((RANK, C), bf16),
            pltpu.VMEM(((3 * C + FF + 2 * C) // LANES, RANK, LANES), f32),
        ],
        compiler_params=params(36),
        cost_estimate=cost(17),
        name="forward",
    )(*in_hbm(far), *in_hbm(arrays))


def backward_kernel(*refs):
    far, refs = dict(zip(FAR_BACK, refs)), refs[len(FAR_BACK) :]
    residual_in, low_qkv_in, low_proj_in, all_mixed, all_probs, all_attended, whole_a = refs[:7]
    qkv_down, proj_down, qkv_up, proj_up, keep_out, away_out, pay_out = refs[7:14]
    held, refs = dict(zip(FAR_BACK, refs[14:])), refs[14 + len(FAR_BACK) :]
    stage, flat, ranks, more = refs
    loads, take = loading(FAR_BACK, far, held, more)
    for name in FAR_BACK:
        loads[name].start()
    wide = C // 4
    heads = wide // HD
    take("valid", "own", "upper", "gains", "offsets")
    flag = held["valid"][here()[3]].astype(f32)
    gain = held["gains"][0:1].astype(f32)
    inputs = jnp.concatenate([held["own"][0], held["upper"][0]], 0).astype(f32)
    unit, scale = norm_parts(inputs)
    shifted = (unit * gain + held["offsets"][0:1].astype(f32)).astype(bf16)
    low_qkv = low_qkv_in[...]
    grad_residual = residual_in[...]
    grad_attn = (flag * grad_residual).astype(bf16)
    grad_low_proj = dot_t(grad_attn, proj_up[...]).astype(bf16)
    spread_proj = over_lanes(grad_low_proj)
    grad_low_qkv = jnp.zeros((TOK, RANK), f32)
    grad_shifted = jnp.zeros((TOK, C), f32)
    for b in range(4):
        rows = slice(b * wide, (b + 1) * wide)
        flat[b * wide // 8 : (b + 1) * wide // 8, :] = fold(tdot(all_attended[b], spread_proj))
        grad_heads = dot(grad_attn, whole_a[b, :, 3 * wide :]) + dot_t(spread_proj, proj_down[2 * b : 2 * b + 2].reshape(wide, LANES))
        grad_heads = grad_heads.astype(bf16)
        queries, keys, values = (all_mixed[b, :, i * wide : (i + 1) * wide] for i in range(3))
        probs = all_probs[b]
        grad_probs = dot_t(stacked(values), grad_heads).reshape(heads, TOK, TOK)
        centre = jnp.sum(grad_probs * probs, 1, keepdims=True)
        grad_scores = (probs * (grad_probs - centre)).astype(bf16)
        flat_scores = grad_scores.reshape(heads * TOK, TOK)
        grad_queries = by_heads(keys.T, grad_scores).T
        grad_keys = gathered(dot(flat_scores, queries))
        grad_values = gathered(dot(probs.astype(bf16).reshape(heads * TOK, TOK), grad_heads))
        grad = jnp.concatenate([SCALE * grad_queries, SCALE * grad_keys, grad_values], 1).astype(bf16)
        grad_up = tdot(low_qkv, grad)
        for i in range(3):
            ranks[:, i * C + b * wide : i * C + (b + 1) * wide] = grad_up[:, i * wide : (i + 1) * wide]
        grad_low_qkv = grad_low_qkv + dot_t(grad, qkv_up[b])
        grad_shifted = grad_shifted + dot_t(grad, whole_a[b, :, : 3 * wide])
    spread_qkv = over_lanes(grad_low_qkv.astype(bf16))
    grad_shifted = grad_shifted + dot_t(spread_qkv, qkv_down[...].reshape(C, LANES))
    grad = grad_residual + norm_back(grad_shifted, gain, unit, scale)
    keep_out[...] = grad[: TOK // 2].astype(bf16)
    away_out[...] = grad[TOK // 2 :].astype(bf16)
    take("pay")
    tile = held["pay"].shape[0]
    stage[:tile] = held["pay"][...].astype(f32)
    tile = pack_flat(stage, tile, flat, C // 8)
    tile = pack_ranks(stage, tile, tdot(low_proj_in[...], grad_attn))
    tile = pack_ranks(stage, tile, ranks[...])
    flat[...] = fold(tdot(shifted, spread_qkv))
    pack_flat(stage, tile, flat, C // 8)
    pay_out[...] = jnp.swapaxes(stage[...], 0, 1).astype(bf16)


PAY = 16 * C * RANK // OWNERS // LANES


def backward(near, **far):
    half = jax.ShapeDtypeStruct((TOK // 2, C), bf16)
    far = [far[name] for name in FAR_BACK]
    return pl.pallas_call(
        backward_kernel,
        out_shape=[half, half, jax.ShapeDtypeStruct((OWNERS, PAY, LANES), bf16)],
        in_specs=[HBM] * len(far) + [VM] * len(near),
        out_specs=[VM] * 3,
        scratch_shapes=scratch_of(far)
        + [
            pltpu.VMEM((PAY, OWNERS, LANES), f32),
            pltpu.VMEM((C // 8, LANES), f32),
            pltpu.VMEM((RANK, 3 * C), f32),
            pltpu.SemaphoreType.DMA((len(FAR_BACK),)),
        ],
        compiler_params=params(16),
        cost_estimate=cost(14),
        name="backward",
    )(*in_hbm(far), *near)


WIDTHS = (12, 12, 3, 3, 3, 3, 9, 3)


def sums_kernel(terms, pick, grad_main, grad_fc2, grad_qkv, grad_fc1, grad_out):
    by_tile = jnp.swapaxes(terms[...].astype(f32), 0, 1).astype(bf16)
    targets = (grad_fc2, grad_fc1, grad_out.at[1], grad_main.at[2], grad_main.at[1], grad_out.at[0], grad_qkv, grad_main.at[0])
    tile = 0
    for target, width in zip(targets, WIDTHS):
        for k in range(width):
            target[:, k * LANES : (k + 1) * LANES] = dot(pick[...], by_tile[tile])
            tile += 1


def sums(terms, pick):
    shapes = [(3, ADAPT, 3 * LANES), (ADAPT, 12 * LANES), (ADAPT, 9 * LANES), (ADAPT, 12 * LANES), (2, ADAPT, 3 * LANES)]
    main, fc2, qkv, fc1, out = pl.pallas_call(
        sums_kernel,
        out_shape=[jax.ShapeDtypeStruct(v, f32) for v in shapes],
        in_specs=[VM] * 2,
        out_specs=[VM] * 5,
        compiler_params=params(8),
        cost_estimate=cost(3),
        name="sums",
    )(terms, *in_hbm([pick]))
    return main.transpose(1, 0, 2), fc2, qkv, fc1, out.transpose(1, 0, 2)


def per_device(
    tokens,
    cotangent,
    adapter_id,
    valid_flag,
    regions,
    w_qkv,
    b_qkv,
    rel_table,
    w_proj,
    b_proj,
    w_fc1,
    b_fc1,
    w_fc2,
    b_fc2,
    norm_gains,
    norm_shifts,
    down_main,
    down_fc2,
    up_qkv,
    up_fc1,
    up_out,
):
    z_count, t_count = lax.axis_size("img"), lax.axis_size("tp")
    images, height, breadth = tokens.shape[:3]
    across = breadth // WIN
    wide = rel_table.shape[1] * HD
    count = 2 * z_count * t_count

    groups = [Group() for _ in range(3)]
    if z_count == 4:
        w_planes = w_qkv.transpose(1, 0, 2)
        piece = begin(adapter_id, w_planes, w_proj, w_fc1, w_fc2.T, b_qkv, b_fc1, rel_table.T)
        own_a, own, away = cut_windows(tokens, cotangent, w_planes, w_proj)
        arrays = [own_a, w_fc1, w_fc2.T]
        for n, group in enumerate(groups):
            group.add(n, 0, 2 * HALF, 0, 0, None, 0)
        cut = PIECE // 2
        upper = swap_ctx(away)
        along = [piece, shift_img(piece, 1)]
        by_x, by_y = swap_x(piece), swap_y(piece)
        gate = (along[1], by_x, by_y, upper)
        relayed = ()
        for k in (1, 2, 3):
            held = after(along[k], *gate)
            swapped = len(arrays)
            spread(groups, arrays, held, [(0, PIECE, 0, k, 0)])
            end = PIECE + SMALL if k == 1 else PIECE
            half_x, half_y = after(by_x[:cut], *gate), after(by_y[cut:end], *gate)
            old_x, old_y = by_x, by_y
            by_x = swap_x(jnp.concatenate([held[:PIECE], half_y], 0))
            by_y = swap_y(after(jnp.concatenate([held[:PIECE], half_x], 0), arrays[-1]))
            if k == 2:
                smalls = jnp.concatenate(
                    [piece[PIECE:], first_x[PIECE:], first_y[PIECE:], old_x[-SMALL:]], 0
                )
                additive, mask, bias_qkv, bias_fc1 = biases(regions, after(smalls, arrays[-1]))
                held = after(held, additive)
            if k < 3:
                along.append(shift_img(held, 1))
            if k == 3:
                rows = jnp.concatenate([v[PIECE:] for v in along], 0)
                chosen, pick = choose(
                    after(rows, arrays[-1]), down_main.transpose(1, 0, 2), down_fc2, up_qkv, up_fc1, up_out.transpose(1, 0, 2)
                )
                mine = lax.all_to_all(chosen, "img", 0, 0, tiled=True)
            near = [(0, PIECE, 0, k - 1, 1)], [(0, PIECE, 0, k - 1, 2)]
            if k > 1:
                near[0].append((PIECE, cut, cut, k - 2, 3))
                near[1].append((PIECE, cut, 0, k - 2, 3))
            for array, parts in ((old_x, near[0]), (old_y, near[1])):
                spread(groups, arrays, array, parts)
            if k == 1:
                first_x, first_y = old_x, old_y
            if k == 2:
                corner = jnp.concatenate([old_y[PIECE : PIECE + cut], old_x[PIECE : PIECE + cut]], 0)
            if k == 3:
                last = shift_img(after(corner, *gate), -1)
            gate = (by_x, by_y, *along[k + 1 :], *arrays[swapped:])
        theirs = swap_ctx(mine)
        spread(groups, arrays, by_x, [(0, PIECE, 0, 3, 1), (PIECE, cut, cut, 2, 3)])
        spread(groups, arrays, by_y, [(0, PIECE, 0, 3, 2), (PIECE, cut, 0, 2, 3)])
        spread(groups, arrays, last, [(0, PIECE, 0, 3, 3)])
    else:
        c, t = lax.axis_index("ctx"), lax.axis_index("tp")
        image, column = t // across, t % across
        both = jnp.stack([lax.dynamic_index_in_dim(a, image, 0, False) for a in (tokens, cotangent)])
        both = lax.dynamic_slice_in_dim(jnp.roll(both, -SHIFT, 2), column * WIN, WIN, 2)
        own = both[:, SHIFT:].reshape(2, TOK // 2, C)
        upper = swap_ctx(both[:, :SHIFT].reshape(2, TOK // 2, C))
        own_a = jnp.concatenate([w_qkv.reshape(-1, 3 * wide), w_proj.T], 1)
        arrays = []
        for group, weights in zip(groups, (own_a, w_fc1, w_fc2.T)):
            for j, array in enumerate(spread_far(weights)):
                group.add(len(arrays), 0, C, None, j, None, 0)
                arrays.append(array)
        ids = lax.all_gather(adapter_id, "img")
        parts = [down_main[:, i] for i in range(3)] + [down_fc2, up_qkv, up_fc1] + [up_out[:, i] for i in range(2)]
        tables = jnp.concatenate(parts, 1)
        wanted = lax.dynamic_index_in_dim(ids, image, 1, False)
        pick = (wanted[:, None] == jnp.arange(ADAPT)[None, :]).astype(bf16)
        mine = lax.all_to_all(dot(pick, tables).astype(bf16), "img", 0, 0, tiled=True)
        theirs = swap_ctx(mine)
        mine, theirs = jnp.where(c == 0, mine, theirs), jnp.where(c == 0, theirs, mine)
        owned = jnp.stack([mine, theirs], 1).reshape(2 * z_count, -1)
        sizes = [v.shape[1] for v in parts]
        cuts = [sum(sizes[:i]) for i in range(9)]
        owned = jnp.concatenate([owned[:, a:b].reshape(SHARDS, -1) for a, b in zip(cuts, cuts[1:])], 1)
        owned = owned.reshape(SHARDS, C // LANES, 32, LANES).transpose(0, 2, 1, 3).reshape(SHARDS // 2, 2, 32, C)
        mine, theirs = jnp.where(c == 0, owned[:, 0], owned[:, 1]), jnp.where(c == 0, owned[:, 1], owned[:, 0])
        source = jnp.broadcast_to(ids[:, None, :, None], (z_count, 2, images, across)).reshape(-1)
        pick = (jnp.arange(ADAPT)[:, None] == source[None, :]).astype(bf16)

        def rows_of(field, rows):
            return jnp.pad(field, ((0, rows - field.shape[0]), (0, C - field.shape[1])))

        small = jnp.concatenate([rows_of(b_qkv, 3), b_fc1[None], jnp.zeros((4, C), bf16), rows_of(rel_table.T, 8)], 0)
        smalls = jnp.concatenate([small, swap_x(small), swap_y(small), swap_xy(small)], 0)
        additive, mask, bias_qkv, bias_fc1 = biases(regions, smalls)
    keep, away, pay, *near = forward(
        groups, arrays, strips=additive, joined=join(mine, theirs), valid=valid_flag, own=own, upper=upper,
        gains=norm_gains, offsets=norm_shifts, bias_qkv=bias_qkv, mask=mask, bias_proj=b_proj,
        bias_fc1=bias_fc1, bias_fc2=b_fc2,
    )

    def moved(keep, away):
        half = jnp.concatenate([swap_ctx(away), keep], 0)
        return [half, swap_x(half), swap_y(half), swap_xy(half)]

    def placed(pieces, dtype):
        return place(pieces, dtype).reshape(images, height, breadth, C)

    outputs = moved(keep, away)
    keep, away, pay = backward(
        near, valid=valid_flag, own=own, upper=upper, gains=norm_gains, offsets=norm_shifts, pay=pay
    )
    keep, away, pay, *outputs = lax.optimization_barrier((keep, away, pay, *outputs))
    grads = moved(keep, away)
    output = placed(outputs, bf16)

    if count == OWNERS:
        added = sums(lax.all_to_all(pay, ("img", "ctx", "tp"), 0, 0, tiled=True), pick)
    else:
        cuts = [LANES * sum(WIDTHS[:i]) for i in range(9)]
        pay = pay.reshape(OWNERS, PAY * LANES)
        pay = jnp.concatenate([pay[:, a:b].reshape(count, -1) for a, b in zip(cuts, cuts[1:])], 1)
        cuts = [v * OWNERS // count for v in cuts]
        totals = dot(pick, lax.all_to_all(pay, ("img", "ctx", "tp"), 0, 0, tiled=True))
        fc2, fc1, out1, main2, main1, out0, qkv, main0 = (totals[:, a:b] for a, b in zip(cuts, cuts[1:]))
        added = jnp.stack([main0, main1, main2], 1), fc2, qkv, fc1, jnp.stack([out0, out1], 1)
    grads = [after(grads[0], added[0], output), *grads[1:]]
    return (output, placed(grads, f32), *added)


def solution(mesh):
    in_specs = (
        P("img", "ctx", None, None),
        P("img", "ctx", None, None),
        P("img"),
        P("img"),
        P("ctx", None),
        P("img", None, "tp"),
        P(None, "tp"),
        P(None, "tp"),
        P("tp", "img"),
        P(),
        P("img", "tp"),
        P("tp"),
        P("tp", "img"),
        P(),
        P(),
        P(),
        P(None, None, ("img", "ctx")),
        P(None, ("img", "ctx")),
        P(None, ("img", "ctx")),
        P(None, ("img", "ctx")),
        P(None, None, ("img", "ctx")),
    )
    out_specs = (
        P("img", "ctx", None, None),
        P("img", "ctx", None, None),
        P(None, None, ("img", "ctx", "tp")),
        P(None, ("img", "ctx", "tp")),
        P(None, ("img", "ctx", "tp")),
        P(None, ("img", "ctx", "tp")),
        P(None, None, ("img", "ctx", "tp")),
    )
    return jax.shard_map(
        per_device, mesh=mesh, in_specs=in_specs, out_specs=out_specs, check_vma=False
    )
```
